32 devices in a mesh: head: 2 (over y), blk: 16 (over z, x, core).
Axes of the slice: x: 2, y: 2, z: 4, core: 2. Of those that a mesh axis runs over, the one named last changes fastest.
Arguments:
- tokens: bfloat16 [16384, 768], P(('blk', 'head')), may hold values from -6 to 6
- cotangent: bfloat16 [16384, 768], P(('blk', 'head')), may hold values from -6 to 6
- doc_lengths: int32 [8], replicated, may hold values from 1 to 15872, 16384 in all
- global_blocks: int32 [2], replicated, may hold values from 0 to 255
- random_blocks: int32 [12, 256, 3], P('head', 'blk'), may hold values from 0 to 255, as said below
- query_weight: bfloat16 [768, 768], P(('head', 'blk')), may hold values from -0.21875 to 0.21875
- query_bias: bfloat16 [768], P(('head', 'blk')), may hold values from -3 to 3
- key_weight: bfloat16 [768, 768], P(('head', 'blk')), may hold values from -0.21875 to 0.21875
- value_weight: bfloat16 [768, 768], P(('head', 'blk')), may hold values from -0.21875 to 0.21875
- value_bias: bfloat16 [768], P(('head', 'blk')), may hold values from -3 to 3
- output_weight: bfloat16 [768, 768], P(('head', 'blk')), may hold values from -6 to 6
- output_bias: bfloat16 [768], P(('head', 'blk')), may hold values from -3 to 3
- first_gain: bfloat16 [768], P(('head', 'blk')), may hold values from 0.5 to 1.5
- first_shift: bfloat16 [768], P(('head', 'blk')), may hold values from -3 to 3
- up_weight: bfloat16 [768, 3072], P(('head', 'blk')), may hold values from -0.21875 to 0.21875
- up_bias: bfloat16 [3072], P(('head', 'blk')), may hold values from -3 to 3
- down_weight: bfloat16 [3072, 768], P(('head', 'blk')), may hold values from -0.109375 to 0.109375
- down_bias: bfloat16 [768], P(('head', 'blk')), may hold values from -3 to 3
- second_gain: bfloat16 [768], P(('head', 'blk')), may hold values from 0.5 to 1.5
- second_shift: bfloat16 [768], P(('head', 'blk')), may hold values from -3 to 3
Outputs:
- out: bfloat16 [16384, 768], P(('blk', 'head'))
- tokens_grad: float32 [16384, 768], P(('blk', 'head'))
- query_weight_grad: float32 [768, 768], P(('head', 'blk'))
- query_bias_grad: float32 [768], P(('head', 'blk'))
- key_weight_grad: float32 [768, 768], P(('head', 'blk'))
- value_weight_grad: float32 [768, 768], P(('head', 'blk'))
- value_bias_grad: float32 [768], P(('head', 'blk'))
- output_weight_grad: float32 [768, 768], P(('head', 'blk'))
- output_bias_grad: float32 [768], P(('head', 'blk'))
- first_gain_grad: float32 [768], P(('head', 'blk'))
- first_shift_grad: float32 [768], P(('head', 'blk'))
- up_weight_grad: float32 [768, 3072], P(('head', 'blk'))
- up_bias_grad: float32 [3072], P(('head', 'blk'))
- down_weight_grad: float32 [3072, 768], P(('head', 'blk'))
- down_bias_grad: float32 [768], P(('head', 'blk'))
- second_gain_grad: float32 [768], P(('head', 'blk'))
- second_shift_grad: float32 [768], P(('head', 'blk'))
The draws below stay inside these ranges and needn't reach their ends.
Inputs may be any that keep to these rules, and one draw needn't show every extreme that they name: `random_blocks`: each id lies within 32 blocks of its query block, counted cyclically over the 256 blocks, and for every head both ends of that reach occur. `doc_lengths`: the lengths sum to 16384.
All inputs are finite; a program needn't handle non-finite values.
Results may differ from the reference program's by a relative error of at most 0.014.
Values may be sent and summed in bfloat16 or wider, within the bound.
No kernel may reach another device: no remote copies, remote signals or barrier semaphores. Data moves between devices by JAX's collectives and lax.ppermute only.
A program may use at most 256 MiB of HBM per device.

```python
import math
import jax
import jax.numpy as jnp
import numpy as np
from jax import lax

D = 768
HEADS = 12
HEAD_DIM = 64
FF = 3072
BLOCK = 64
TOK_DEV = 512
REACH = 2
N_GLOBAL = 2
N_RANDOM = 3
NDOCS = 8
TOKENS = 16384
NB = 256


def draw_random_blocks(key, part):
    key = jax.random.fold_in(key, 11)
    reach = REACH * 2 * TOK_DEV // BLOCK
    offsets = jax.random.randint(key, (HEADS, NB, N_RANDOM), -reach, reach + 1)
    offsets = offsets.at[:, 0, 0].set(reach)
    offsets = offsets.at[:, 0, 1].set(-reach)
    query_blocks = jnp.arange(NB, dtype=jnp.int32)
    return ((query_blocks[None, :, None] + offsets) % NB).astype(jnp.int32)


def block_scale(own_key, dims, split, low, largest):
    factor_of, own = 1.0, jax.random.fold_in(own_key, 6)
    for position, shards_of in split:
        steps = jnp.exp(jax.random.uniform(jax.random.fold_in(own, position), (shards_of,), jnp.float32, low / len(split), largest / len(split)))
        factor_of = factor_of * jnp.repeat(steps, dims[position] // shards_of).reshape([-1 if axis == position else 1 for axis in range(len(dims))])
    return factor_of


def profile(number_of, total, most, lean):
    weights = [(1 << 20) // math.isqrt(standing ** lean) + 1 for standing in range(2, number_of + 1)]
    rest, counts = total - most - (number_of - 1), [1] * (number_of - 1)
    while rest > 0:
        movable = [i for i in range(number_of - 1) if counts[i] < most]
        mass, left = sum([weights[i] for i in movable]), rest
        for i in movable:
            addition = min(most - counts[i], max(1, left * weights[i] // mass), rest)
            counts[i] = counts[i] + addition
            rest = rest - addition
    return np.array([most] + counts)


def ragged_sizes(rng, count, total, limit, lean):
    if count == 2:
        one = jax.random.randint(rng, (), max(1, total - limit), min(limit, total - 1) + 1)
        return jnp.stack([one, total - one])
    sizes = jnp.asarray(profile(count, total, limit, lean), jnp.int32)
    pairs = (count - 1) // 2
    giver, sink = sizes[1:1 + 2 * pairs:2], sizes[2:2 + 2 * pairs:2]
    room = jnp.minimum(giver - 1, limit - sink)
    moved = jax.random.randint(jax.random.fold_in(rng, 1), (pairs,), 0, 1 << 20) % (room + 1)
    sizes = sizes.at[1:1 + 2 * pairs:2].set(giver - moved).at[2:2 + 2 * pairs:2].set(sink + moved)
    return sizes[jax.random.permutation(jax.random.fold_in(rng, 2), count)]


def scatter_about(own_key, dims, deviation, bound, pieces=(), kind=jnp.bfloat16):
    values = jax.random.normal(own_key, dims, jnp.float32) * deviation
    if len(pieces) > 0:
        values = block_scale(own_key, dims, pieces, -0.22, 0.18) * values
    return jnp.clip(values, min=-bound, max=bound).astype(kind)


def setup_inputs(seed: int = 0) -> dict:
    key_of = jax.random.split(jax.random.key(seed), 21)
    tokens = scatter_about(key_of[0], (TOKENS, D), 1.0, 6.0, ((0, 32),))
    cotangent = scatter_about(key_of[1], (TOKENS, D), 1.0, 6.0, ((0, 32),))
    doc_lengths = ragged_sizes(key_of[2], NDOCS, TOKENS, TOKENS - TOK_DEV, 2).astype(jnp.int32)
    global_blocks = jax.random.randint(key_of[3], (N_GLOBAL,), 0, NB).astype(jnp.int32)
    random_blocks = draw_random_blocks(jax.random.fold_in(key_of[20], 71), 0)
    query_weight = scatter_about(key_of[5], (D, D), D ** -0.5, 0.21875, ((0, 32),))
    query_bias = scatter_about(key_of[6], (D,), 0.5, 3.0, ((0, 32),))
    key_weight = scatter_about(key_of[7], (D, D), D ** -0.5, 0.21875, ((0, 32),))
    value_weight = scatter_about(key_of[8], (D, D), D ** -0.5, 0.21875, ((0, 32),))
    value_bias = scatter_about(key_of[9], (D,), 0.5, 3.0, ((0, 32),))
    output_weight = scatter_about(key_of[10], (D, D), (max(1, D // (8 * BLOCK))) ** -0.5, 6.0, ((0, 32),))
    output_bias = scatter_about(key_of[11], (D,), 0.5, 3.0, ((0, 32),))
    first_gain = jnp.clip(1.0 + 0.1 * jax.random.normal(key_of[12], (D,), jnp.float32), 0.5, 1.5).astype(jnp.bfloat16)
    first_shift = scatter_about(key_of[13], (D,), 0.5, 3.0, ((0, 32),))
    up_weight = scatter_about(key_of[14], (D, FF), D ** -0.5, 0.21875, ((0, 32),))
    up_bias = scatter_about(key_of[15], (FF,), 0.5, 3.0, ((0, 32),))
    down_weight = scatter_about(key_of[16], (FF, D), FF ** -0.5, 0.109375, ((0, 32),))
    down_bias = scatter_about(key_of[17], (D,), 0.5, 3.0, ((0, 32),))
    second_gain = jnp.clip(1.0 + 0.1 * jax.random.normal(key_of[18], (D,), jnp.float32), 0.5, 1.5).astype(jnp.bfloat16)
    second_shift = scatter_about(key_of[19], (D,), 0.5, 3.0, ((0, 32),))
    return {"tokens": tokens, "cotangent": cotangent, "doc_lengths": doc_lengths, "global_blocks": global_blocks, "random_blocks": random_blocks, "query_weight": query_weight, "query_bias": query_bias, "key_weight": key_weight, "value_weight": value_weight, "value_bias": value_bias, "output_weight": output_weight, "output_bias": output_bias, "first_gain": first_gain, "first_shift": first_shift, "up_weight": up_weight, "up_bias": up_bias, "down_weight": down_weight, "down_bias": down_bias, "second_gain": second_gain, "second_shift": second_shift}


@jax.custom_vjp
def low(v):
    return lax.optimization_barrier(v.astype(jnp.bfloat16)).astype(jnp.float32)

@jax.custom_vjp
def low_back(v):
    return v

def low_keep(v):
    return (low(v), None)

def low_pass(kept, grad):
    return (grad,)

def back_keep(v):
    return (v, None)

def back_low(kept, grad):
    return (low(grad),)
low.defvjp(low_keep, low_pass)
low_back.defvjp(back_keep, back_low)
NORM_EPS = 1e-06
MASKED = -1e+30
HIGH = lax.Precision.HIGHEST

def slot_table(query_blocks, total, global_blocks, random_blocks):
    offsets = jnp.array([-1, 0, 1], dtype=jnp.int32)
    near = (query_blocks[:, None] + offsets[None, :]) % total
    shape = random_blocks.shape[:2]
    near = jnp.broadcast_to(near[None], shape + (3,))
    chosen = jnp.broadcast_to(global_blocks.astype(jnp.int32)[None, None, :], shape + (global_blocks.shape[0],))
    slot_ids = jnp.concatenate([near, chosen, random_blocks.astype(jnp.int32)], -1)
    count = slot_ids.shape[-1]
    same = slot_ids[..., :, None] == slot_ids[..., None, :]
    order = jnp.arange(count)
    earlier = order[None, :] < order[:, None]
    repeated = jnp.any(same & earlier[None, None], -1)
    return (slot_ids, jnp.logical_not(repeated))

def doc_number(positions, starts):
    return lax.optimization_barrier(jnp.sum((positions[..., None] >= starts).astype(jnp.int32), -1))

def layer_norm(value, gain, shift):
    center = value - lax.optimization_barrier(jnp.mean(value, -1, keepdims=True))
    spread = lax.optimization_barrier(jnp.mean(center * center, -1, keepdims=True))
    return center * lax.rsqrt(spread + NORM_EPS) * gain + shift

def attend(queries, keys, values, slot_ids, slot_valid, block_doc):
    total = TOKENS // BLOCK
    group = 2 * TOK_DEV // BLOCK
    count = total // group

    def heads_first(value):
        return value.reshape(total, BLOCK, HEADS, HEAD_DIM).transpose(2, 0, 1, 3)
    query_heads = heads_first(queries)
    key_heads = heads_first(keys)
    value_heads = heads_first(values)
    query_groups = query_heads.reshape(HEADS, count, group, BLOCK, HEAD_DIM).transpose(1, 0, 2, 3, 4)
    id_groups = slot_ids.reshape(HEADS, count, group, -1).transpose(1, 0, 2, 3)
    valid_groups = slot_valid.reshape(HEADS, count, group, -1).transpose(1, 0, 2, 3)
    doc_groups = block_doc.reshape(count, group, BLOCK)

    def one_group(inputs):
        query_part, id_part, valid_part, doc_part = inputs
        width = id_part.shape[-1] * BLOCK
        picked_keys = jax.vmap(lambda table, index: table[index])(key_heads, id_part)
        picked_values = jax.vmap(lambda table, index: table[index])(value_heads, id_part)
        picked_keys = picked_keys.reshape(HEADS, group, width, HEAD_DIM)
        picked_values = picked_values.reshape(HEADS, group, width, HEAD_DIM)
        key_doc = block_doc[id_part].reshape(HEADS, group, width)
        slot_mask = jnp.repeat(valid_part, BLOCK, -1)
        allowed = slot_mask[:, :, None, :] & (doc_part[None, :, :, None] == key_doc[:, :, None, :])
        scores = jnp.einsum('hqtd,hqsd->hqts', query_part, picked_keys, precision=HIGH) * HEAD_DIM ** (-0.5)
        scores = low_back(scores)
        scores = jnp.where(allowed, scores, MASKED)
        top = lax.optimization_barrier(jnp.max(scores, -1, keepdims=True))
        weights = jnp.exp(scores - top)
        probs = weights / lax.optimization_barrier(jnp.sum(weights, -1, keepdims=True))
        return jnp.einsum('hqts,hqsd->hqtd', low(probs), picked_values, precision=HIGH)
    context = lax.map(jax.checkpoint(one_group), (query_groups, id_groups, valid_groups, doc_groups))
    return context.transpose(0, 2, 3, 1, 4).reshape(TOKENS, HEADS * HEAD_DIM)

def reference(tokens, cotangent, doc_lengths, global_blocks, random_blocks, query_weight, query_bias, key_weight, value_weight, value_bias, output_weight, output_bias, first_gain, first_shift, up_weight, up_bias, down_weight, down_bias, second_gain, second_shift):
    total = TOKENS // BLOCK
    lengths = doc_lengths.astype(jnp.int32)
    starts = jnp.cumsum(lengths) - lengths
    slot_ids, slot_valid = slot_table(jnp.arange(total, dtype=jnp.int32), total, global_blocks, random_blocks)
    block_doc = doc_number(jnp.arange(TOKENS, dtype=jnp.int32).reshape(total, BLOCK), starts)

    def forward(inputs, w_query, b_query, w_key, w_value, b_value, w_output, b_output, gain_one, shift_one, w_up, b_up, w_down, b_down, gain_two, shift_two):
        queries = low(low_back(jnp.dot(inputs, w_query, precision=HIGH) + b_query))
        keys = low(low_back(jnp.dot(inputs, w_key, precision=HIGH)))
        values = low(low_back(jnp.dot(inputs, w_value, precision=HIGH) + b_value))
        context = attend(queries, keys, values, slot_ids, slot_valid, block_doc)
        context = low(low_back(context))
        attended = low_back(jnp.dot(context, w_output, precision=HIGH) + b_output)
        first = layer_norm(inputs + attended, gain_one, shift_one)
        hidden = low_back(jnp.dot(low(first), w_up, precision=HIGH) + b_up)
        active = low(jax.nn.gelu(hidden, approximate=True))
        branch = low_back(jnp.dot(active, w_down, precision=HIGH) + b_down)
        return layer_norm(first + branch, gain_two, shift_two)
    params = (query_weight, query_bias, key_weight, value_weight, value_bias, output_weight, output_bias, first_gain, first_shift, up_weight, up_bias, down_weight, down_bias, second_gain, second_shift)
    params = tuple((item.astype(jnp.float32) for item in params))
    result, pullback = jax.vjp(forward, tokens.astype(jnp.float32), *params)
    grads = pullback(cotangent.astype(jnp.float32))
    return (result.astype(jnp.bfloat16), grads[0], grads[1], grads[2], grads[3], grads[4], grads[5], grads[6], grads[7], grads[8], grads[9], grads[10], grads[11], grads[12], grads[13], grads[14], grads[15])
```

```python
from functools import partial

import jax
import jax.numpy as jnp
from jax import lax
from jax.experimental import pallas as pl
from jax.experimental.pallas import tpu as pltpu
from jax.sharding import PartitionSpec as P

HEAD_DIM = 64
BLOCK = 64
LANES = 128
NORM_EPS = 1e-06
MASKED = -1e30
AXES = ("head", "blk")
BF16 = jnp.bfloat16
F32 = jnp.float32
PAIRS = ((0, 0), (1, 0), (0, 1), (1, 1))
VMEM_LIMIT = 60 * 1024 * 1024


def matmul(left, right):
    return jnp.dot(left, right, preferred_element_type=F32)


def dot_rows(left, right):
    return lax.dot_general(left, right, (((0,), (0,)), ((), ())), preferred_element_type=F32)


def dot_lanes(left, right):
    return lax.dot_general(left, right, (((1,), (1,)), ((), ())), preferred_element_type=F32)


class Place:
    def __init__(self):
        self.size = lax.axis_size("blk")
        self.slabs = self.size // 4
        blk = lax.axis_index("blk")
        self.h = lax.axis_index("head")
        self.n = blk // 4
        self.x = (blk // 2) % 2
        self.c = blk % 2

    def send(self, value, target):
        def index(h, n, x, c):
            return h * self.size + 4 * n + 2 * x + c

        route = [
            (index(h, n, x, c), index(*target(h, n, x, c)))
            for h in range(2)
            for n in range(self.slabs)
            for x in range(2)
            for c in range(2)
        ]
        return lax.ppermute(value, AXES, route)

    def along_slabs(self, value, k):
        return self.send(value, lambda h, n, x, c: (h, n ^ k, x, c))

    def across(self, value, i, j):
        return self.send(value, lambda h, n, x, c: (h ^ i, n, x ^ j, c))

    def sibling(self, value):
        return self.send(value, lambda h, n, x, c: (h, n, x, 1 - c))

    def to_heads(self, value, i, j):
        return self.send(value, lambda h, n, x, c: (h ^ i, n, c ^ j, x))

    def to_tokens(self, value, i, j):
        return self.send(value, lambda h, n, x, c: (h ^ i, n, c, x ^ j))

    def to_next(self, value):
        def target(h, n, x, c):
            return (h, n, x, 1) if c == 0 else (h, (n + 1) % self.slabs, x, 0)

        return self.send(value, target)

    def to_previous(self, value):
        def target(h, n, x, c):
            return (h, n, x, 0) if c == 1 else (h, (n - 1) % self.slabs, x, 1)

        return self.send(value, target)


def pick(value, index, axis=0):
    return lax.dynamic_index_in_dim(value, index, axis, keepdims=False)


def assemble(place, mine, other):
    slabs, rows, columns = mine[0].shape
    pieces = list(mine) + list(other)
    where = jnp.stack([place.h, place.n, place.x, place.c]).astype(jnp.int32)

    def kernel(where_ref, *refs):
        sources, out = refs[:8], refs[8]
        h, x, c = where_ref[0], where_ref[2], where_ref[3]
        for which in range(8):
            i, j = PAIRS[which % 4]
            out[h ^ i, 0, x ^ j, c ^ (which // 4)] = sources[which][0]

    found = pl.pallas_call(
        kernel,
        out_shape=jax.ShapeDtypeStruct((2, slabs, 2, 2, rows, columns), pieces[0].dtype),
        grid_spec=pltpu.PrefetchScalarGridSpec(
            num_scalar_prefetch=1,
            grid=(slabs,),
            in_specs=[pl.BlockSpec((1, rows, columns), lambda k, w: (k, 0, 0))] * 8,
            out_specs=pl.BlockSpec(
                (2, 1, 2, 2, rows, columns), lambda k, w: (0, k ^ w[1], 0, 0, 0, 0)
            ),
        ),
        compiler_params=pltpu.CompilerParams(vmem_limit_bytes=VMEM_LIMIT),
        name="assemble",
    )(where, *pieces)
    return found.reshape(8 * slabs, rows, columns)


def gather_shards(place, value):
    column = jnp.stack([value] + [place.along_slabs(value, k) for k in range(1, place.slabs)])
    mine = [column] + [place.across(column, i, j) for i, j in PAIRS[1:]]
    other = [place.sibling(piece) for piece in mine]
    return assemble(place, mine, other)


def gather_group(place, value):
    column = jnp.stack([value] + [place.along_slabs(value, k) for k in range(1, place.slabs)])

    def part(i, j):
        return pick(column, (place.h ^ i) * 2 + (place.x ^ j), 1)

    mine = [part(0, 0)] + [place.across(part(i, j), i, j) for i, j in PAIRS[1:]]
    other = [place.sibling(piece) for piece in mine]
    return assemble(place, mine, other)


def halve(place, value):
    kept = pick(value, place.c, 3)
    sent = pick(value, 1 - place.c, 3).astype(BF16)
    return kept.astype(F32) + place.sibling(sent).astype(F32)


def scatter_sum(place, value):
    half = halve(place, value).astype(BF16)

    def part(i, j):
        return pick(pick(half, place.h ^ i), place.x ^ j, 1)

    quarter = part(0, 0).astype(F32)
    for i, j in PAIRS[1:]:
        quarter = quarter + place.across(part(i, j), i, j).astype(F32)
    low = quarter.astype(BF16)
    total = pick(quarter, place.n)
    for k in range(1, place.slabs):
        total = total + place.along_slabs(pick(low, place.n ^ k), k).astype(F32)
    return total


def scatter_group(place, value):
    half = halve(place, value).astype(BF16)
    total = pick(half, place.n, 1).astype(F32)
    for k in range(1, place.slabs):
        total = total + place.along_slabs(pick(half, place.n ^ k, 1), k).astype(F32)

    def part(i, j):
        return pick(pick(total, place.h ^ i), place.x ^ j)

    found = [part(0, 0)] + [place.across(part(i, j), i, j) for i, j in PAIRS[1:]]
    found = jnp.stack([found[0], found[2], found[1], found[3]])
    own = place.h * 2 + place.x
    return [pick(found, own ^ group) for group in range(4)]


def doc_count(position, starts_ref, count):
    total = jnp.zeros(position.shape, jnp.int32)
    for which in range(count):
        total = total + (position >= starts_ref[which]).astype(jnp.int32)
    return total


def load_slots(kv, slots_ref, base, head):
    lanes = slice(head * LANES, (head + 1) * LANES)
    return jnp.concatenate([kv[slots_ref[base + s], :, lanes] for s in range(8)], 0)


def copy_in(sources, kv, sems):
    copies = []
    for which, source in enumerate(sources):
        start = 8 * which
        copies.append(
            pltpu.make_async_copy(source, kv.at[pl.ds(start, source.shape[0])], sems.at[which])
        )
    for copy in copies:
        copy.start()
    for copy in copies:
        copy.wait()


STEP = 2


def attend_forward(slots, ids, query_ids, starts, queries, pieces):
    heads = 3
    blocks = queries.shape[0] // BLOCK
    docs = starts.shape[0]
    many = len(pieces)

    def kernel(slots_ref, ids_ref, query_ids_ref, starts_ref, q_ref, *refs):
        sources = refs[:many]
        ctx_ref, p_ref, kv, sems = refs[many:]
        step = pl.program_id(0)

        @pl.when(step == 0)
        def _():
            copy_in(sources, kv, sems)

        lane = lax.broadcasted_iota(jnp.int32, (1, LANES), 1)
        row = lax.broadcasted_iota(jnp.int32, (BLOCK, LANES), 0)
        for u in range(STEP):
            block = step * STEP + u
            query_doc = doc_count(query_ids_ref[block] * BLOCK + row, starts_ref, docs)
            contexts = []
            for head in range(heads):
                base = (head * blocks + block) * 8
                slot = load_slots(kv, slots_ref, base, head)
                q = q_ref[u * BLOCK : (u + 1) * BLOCK, head * LANES : (head + 1) * LANES]
                scores = dot_lanes(q, slot)
                tiles = []
                for tile in range(4):
                    first = ids_ref[base + 2 * tile] * BLOCK
                    second = ids_ref[base + 2 * tile + 1] * BLOCK - BLOCK
                    key_doc = doc_count(
                        jnp.where(lane < BLOCK, first + lane, second + lane), starts_ref, docs
                    )
                    tiles.append(
                        jnp.where(
                            query_doc == key_doc,
                            scores[:, tile * LANES : (tile + 1) * LANES],
                            MASKED,
                        )
                    )
                top = jnp.maximum(
                    jnp.maximum(tiles[0], tiles[1]), jnp.maximum(tiles[2], tiles[3])
                )
                top = jnp.max(top, -1, keepdims=True)
                tiles = [jnp.exp(tile - top) for tile in tiles]
                total = (tiles[0] + tiles[1]) + (tiles[2] + tiles[3])
                inverse = 1.0 / jnp.sum(total, -1, keepdims=True)
                low = jnp.concatenate([(tile * inverse).astype(BF16) for tile in tiles], 1)
                p_ref[u, head] = low
                contexts.append(matmul(low, slot))
            rows = slice(u * BLOCK, (u + 1) * BLOCK)
            ctx_ref[rows, :LANES] = jnp.where(lane < BLOCK, contexts[0], contexts[1]).astype(BF16)
            ctx_ref[rows, LANES:] = jnp.where(lane < BLOCK, contexts[2], 0.0).astype(BF16)

    return pl.pallas_call(
        kernel,
        out_shape=(
            jax.ShapeDtypeStruct((blocks * BLOCK, 2 * LANES), BF16),
            jax.ShapeDtypeStruct((blocks, heads, BLOCK, 8 * BLOCK), BF16),
        ),
        grid_spec=pltpu.PrefetchScalarGridSpec(
            num_scalar_prefetch=4,
            grid=(blocks // STEP,),
            in_specs=[pl.BlockSpec((STEP * BLOCK, heads * LANES), lambda i, *_: (i, 0))]
            + [pl.BlockSpec(memory_space=pl.ANY)] * many,
            out_specs=[
                pl.BlockSpec((STEP * BLOCK, 2 * LANES), lambda i, *_: (i, 0)),
                pl.BlockSpec((STEP, heads, BLOCK, 8 * BLOCK), lambda i, *_: (i, 0, 0, 0)),
            ],
            scratch_shapes=[
                pltpu.VMEM((3 * blocks + 2, BLOCK, heads * LANES), BF16),
                pltpu.SemaphoreType.DMA((many,)),
            ],
        ),
        compiler_params=pltpu.CompilerParams(vmem_limit_bytes=VMEM_LIMIT),
        cost_estimate=pl.CostEstimate(
            flops=20_000_000_000, bytes_accessed=20_000_000, transcendentals=3_000_000
        ),
        name="attend_forward",
    )(slots, ids, query_ids, starts, queries, *pieces)


def attend_backward(slots, queries, probs, context_grad, pieces):
    heads = 3
    blocks = queries.shape[0] // BLOCK
    many = len(pieces)

    def kernel(slots_ref, q_ref, p_ref, grad_ref, *refs):
        sources = refs[:many]
        dq_ref, own_ref, next_ref, prev_ref, glob_ref, kv, acc, sems = refs[many:]
        step = pl.program_id(0)

        @pl.when(step == 0)
        def _():
            def clear(i, _):
                acc[i] = jnp.zeros(acc.shape[1:], F32)
                return _

            lax.fori_loop(0, acc.shape[0], clear, 0)
            copy_in(sources, kv, sems)

        lane = lax.broadcasted_iota(jnp.int32, (1, LANES), 1)
        left = lane < BLOCK
        for u in range(STEP):
            block = step * STEP + u
            rows = slice(u * BLOCK, (u + 1) * BLOCK)
            for head in range(heads):
                base = (head * blocks + block) * 8
                lanes = slice(head * LANES, (head + 1) * LANES)
                slot = load_slots(kv, slots_ref, base, head)
                q = q_ref[rows, lanes]
                value_side = left if head % 2 == 0 else jnp.logical_not(left)
                tile = head // 2
                grad = grad_ref[rows, tile * LANES : (tile + 1) * LANES].astype(F32)
                grad = jnp.where(value_side, grad, 0.0).astype(BF16)
                low = p_ref[u, head]
                probs_f = low.astype(F32)
                prob_grad = dot_lanes(grad, slot)
                both = probs_f * prob_grad
                inner = jnp.sum(both, -1, keepdims=True)
                score_grad = (both - probs_f * inner).astype(BF16)
                dq = matmul(score_grad, slot)
                dq_ref[rows, lanes] = jnp.where(value_side, 0.0, dq).astype(BF16)
                slot_grad = dot_rows(
                    jnp.concatenate([score_grad, low], 0), jnp.concatenate([q, grad], 0)
                )
                for s in range(8):
                    where = slots_ref[base + s]
                    acc[where, :, lanes] += slot_grad[s * BLOCK : (s + 1) * BLOCK]

        @pl.when(step == blocks // STEP - 1)
        def _():
            def finish(i, _):
                own_ref[i] = acc[i]
                next_ref[i] = acc[blocks + i].astype(BF16)
                prev_ref[i] = acc[2 * blocks + i].astype(BF16)
                return _

            lax.fori_loop(0, blocks, finish, 0)
            glob_ref[...] = acc[3 * blocks :]

    shape = (blocks, BLOCK, heads * LANES)
    return pl.pallas_call(
        kernel,
        out_shape=(
            jax.ShapeDtypeStruct((blocks * BLOCK, heads * LANES), BF16),
            jax.ShapeDtypeStruct(shape, F32),
            jax.ShapeDtypeStruct(shape, BF16),
            jax.ShapeDtypeStruct(shape, BF16),
            jax.ShapeDtypeStruct((2,) + shape[1:], F32),
        ),
        grid_spec=pltpu.PrefetchScalarGridSpec(
            num_scalar_prefetch=1,
            grid=(blocks // STEP,),
            in_specs=[
                pl.BlockSpec((STEP * BLOCK, heads * LANES), lambda i, *_: (i, 0)),
                pl.BlockSpec((STEP, heads, BLOCK, 8 * BLOCK), lambda i, *_: (i, 0, 0, 0)),
                pl.BlockSpec((STEP * BLOCK, 2 * LANES), lambda i, *_: (i, 0)),
            ]
            + [pl.BlockSpec(memory_space=pl.ANY)] * many,
            out_specs=[
                pl.BlockSpec((STEP * BLOCK, heads * LANES), lambda i, *_: (i, 0)),
                pl.BlockSpec(shape, lambda i, *_: (0, 0, 0)),
                pl.BlockSpec(shape, lambda i, *_: (0, 0, 0)),
                pl.BlockSpec(shape, lambda i, *_: (0, 0, 0)),
                pl.BlockSpec((2,) + shape[1:], lambda i, *_: (0, 0, 0)),
            ],
            scratch_shapes=[
                pltpu.VMEM((3 * blocks + 2,) + shape[1:], BF16),
                pltpu.VMEM((3 * blocks + 2,) + shape[1:], F32),
                pltpu.SemaphoreType.DMA((many,)),
            ],
        ),
        compiler_params=pltpu.CompilerParams(vmem_limit_bytes=VMEM_LIMIT),
        cost_estimate=pl.CostEstimate(
            flops=40_000_000_000, bytes_accessed=30_000_000, transcendentals=0
        ),
        name="attend_backward",
    )(slots, queries, probs, context_grad, *pieces)


def norm_forward(value, gain, shift):
    center = value - jnp.mean(value, -1, keepdims=True)
    spread = jnp.mean(center * center, -1, keepdims=True)
    scale_row = lax.rsqrt(spread + NORM_EPS)
    normal = center * scale_row
    return (normal * gain + shift, normal, scale_row)


def norm_backward(grad, normal, scale_row, gain):
    gain_grad = jnp.sum(grad * normal, 0)
    shift_grad = jnp.sum(grad, 0)
    inner = grad * gain
    value_grad = scale_row * (
        inner
        - jnp.mean(inner, -1, keepdims=True)
        - normal * jnp.mean(inner * normal, -1, keepdims=True)
    )
    return (value_grad, gain_grad, shift_grad)


def slot_tables(place, global_blocks, random_blocks):
    ring = 2 * place.slabs
    half = 2 * place.n + place.c
    flip = 2 * place.x + place.h
    total = ring * 32
    found = []
    for j in range(2):
        arrived = place.to_heads(random_blocks, 0, j)
        arrived = lax.dynamic_slice_in_dim(arrived, 3 * place.x, 3, 0).reshape(3, 2, 8, 3)
        found.append(jnp.where(place.h == 0, arrived, arrived[:, ::-1]))
    chosen = jnp.concatenate(found, 1).reshape(3, 32, 3)
    order = jnp.arange(32, dtype=jnp.int32)
    query_ids = half * 32 + ((order // 8) ^ flip) * 8 + order % 8
    near = (query_ids[:, None] + jnp.arange(-1, 2, dtype=jnp.int32)) % total
    ids = jnp.concatenate(
        [
            jnp.broadcast_to(near[None], (3, 32, 3)),
            jnp.broadcast_to(global_blocks, (3, 32, 2)),
            chosen,
        ],
        -1,
    )
    earlier = jnp.arange(8)[None, :] < jnp.arange(8)[:, None]
    repeated = jnp.any((ids[..., :, None] == ids[..., None, :]) & earlier, -1)
    distance = (ids // 32 - half) % ring
    region = jnp.where(distance == 0, 0, jnp.where(distance == 1, 1, 2))
    within = ids % 32
    local = region * 32 + ((within // 8) ^ flip) * 8 + within % 8
    which = jnp.arange(8, dtype=jnp.int32)
    slots = jnp.where((which == 3) | (which == 4), 93 + which, local)
    marked = jnp.where(repeated, -1, ids)
    return slots.reshape(-1).astype(jnp.int32), marked.reshape(-1).astype(jnp.int32), query_ids.astype(jnp.int32)


def by_head(q, k, v):
    parts = [(m[..., :64], m[..., 64:128], m[..., 128:]) for m in (q, k, v)]
    (q0, q1, q2), (k0, k1, k2), (v0, v1, v2) = parts
    none = jnp.zeros_like(q0)
    return jnp.concatenate([none, q0, q1, none, none, q2, v0, k0, k1, v1, v2, k2], -1)


def from_head(value):
    parts = [value[..., 64 * i : 64 * i + 64] for i in range(12)]
    q = jnp.concatenate([parts[1], parts[2], parts[5]], -1)
    k = jnp.concatenate([parts[7], parts[8], parts[11]], -1)
    v = jnp.concatenate([parts[6], parts[9], parts[10]], -1)
    return q, k, v


def body(
    tokens,
    cotangent,
    doc_lengths,
    global_blocks,
    random_blocks,
    query_weight,
    query_bias,
    key_weight,
    value_weight,
    value_bias,
    output_weight,
    output_bias,
    first_gain,
    first_shift,
    up_weight,
    up_bias,
    down_weight,
    down_bias,
    second_gain,
    second_shift,
):
    place = Place()
    slabs = place.slabs
    devices = 8 * slabs
    tok_rows, width = tokens.shape
    share = query_weight.shape[0]
    hidden_width = up_weight.shape[1]
    scale = HEAD_DIM ** (-0.5)
    group = place.h * 2 + place.x
    flip = 2 * place.x + place.h
    order = ((0, 0), (1, 0), (0, 1), (1, 1))

    token_parts = [place.to_heads(tokens, i, j) for i, j in order]

    groups = by_head(
        (query_weight * BF16(scale)).reshape(share, 4, 192),
        key_weight.reshape(share, 4, 192),
        value_weight.reshape(share, 4, 192),
    ).transpose(1, 0, 2)
    vectors = jnp.concatenate(
        [query_bias, value_bias, output_bias, first_gain, first_shift, down_bias, second_gain, second_shift, up_bias]
    )
    vectors = jnp.pad(vectors, (0, width - vectors.shape[0]))
    groups = jnp.concatenate([groups, jnp.broadcast_to(vectors, (4, 1, width))], 1)
    arrived = gather_group(place, groups)
    w_heads = arrived[:, :share].reshape(width, width)
    rows = arrived[:, share]
    vec = rows[:, : 8 * share].reshape(devices, 8, share).transpose(1, 0, 2).reshape(8, width)
    vec = vec.astype(F32)
    b_query, b_value, b_output, gain_one, shift_one, b_down, gain_two, shift_two = (
        vec[i] for i in range(8)
    )
    b_up = rows[:, 8 * share : 12 * share].reshape(hidden_width).astype(F32)
    bq = pick(b_query.reshape(4, 192), group) * scale
    bv = pick(b_value.reshape(4, 192), group)
    b_heads = by_head(bq, jnp.zeros_like(bq), bv)

    owner = global_blocks // 8
    mine = owner == 2 * (4 * place.n + 2 * place.x + place.c) + place.h
    blocks_here = tokens.reshape(8, BLOCK, width)
    shown = jnp.stack(
        [jnp.where(mine[i], pick(blocks_here, global_blocks[i] % 8), 0) for i in range(2)]
    ).astype(BF16)
    total = shown
    for k in range(1, slabs):
        total = total + place.along_slabs(shown, k)
    shown = total
    for i, j in PAIRS[1:]:
        total = total + place.across(shown, i, j)
    global_tokens = (total + place.sibling(total)).reshape(2 * BLOCK, width)

    w_up = gather_shards(place, up_weight).reshape(width, hidden_width)
    w_down = gather_shards(place, down_weight).reshape(hidden_width, width)
    w_output = gather_shards(place, output_weight).reshape(width, width)

    query_parts, own, following, previous = [], [], [], []
    for part in token_parts:
        heads = (matmul(part, w_heads) + b_heads).astype(BF16)
        query_parts.append(heads[:, :384])
        kv = heads[:, 384:].reshape(8, BLOCK, 384)
        own.append(kv)
        following.append(place.to_previous(kv))
        previous.append(place.to_next(kv))
    shared = (matmul(global_tokens, w_heads[:, 384:]) + b_heads[384:]).astype(BF16)
    pieces = own + following + previous + [shared.reshape(2, BLOCK, 384)]
    queries = jnp.concatenate(query_parts, 0)

    which = jnp.arange(doc_lengths.shape[0])
    before = which[None, :] < which[:, None]
    starts = jnp.sum(jnp.where(before, doc_lengths[None, :], 0), 1).astype(jnp.int32)
    slots, ids, query_ids = slot_tables(place, global_blocks, random_blocks)
    context, probs = attend_forward(slots, ids, query_ids, starts, queries, pieces)

    context_tok = jnp.concatenate(
        [
            place.to_tokens(context[k * tok_rows : (k + 1) * tok_rows], i, j)
            for k, (i, j) in enumerate(order)
        ],
        1,
    )
    sources = [(place.h ^ i) * 2 + (place.c ^ j) for i, j in order]
    w_out = jnp.stack(
        [
            jnp.pad(pick(w_output.reshape(4, 192, width), source), ((0, 64), (0, 0)))
            for source in sources
        ]
    ).reshape(1024, width)

    first_sum = tokens.astype(F32) + matmul(context_tok, w_out) + b_output
    first, first_normal, first_scale = norm_forward(first_sum, gain_one, shift_one)
    first_low = first.astype(BF16)
    hidden = matmul(first_low, w_up) + b_up
    active, gelu_back = jax.vjp(partial(jax.nn.gelu, approximate=True), hidden)
    active_low = active.astype(BF16)
    second_sum = first + matmul(active_low, w_down) + b_down
    result, second_normal, second_scale = norm_forward(second_sum, gain_two, shift_two)
    second_grad, gain_two_grad, shift_two_grad = norm_backward(
        cotangent.astype(F32), second_normal, second_scale, gain_two
    )
    branch_grad = second_grad.astype(BF16)
    down_bias_grad = jnp.sum(branch_grad.astype(F32), 0)
    (hidden_grad,) = gelu_back(matmul(branch_grad, w_down.T))
    hidden_low = hidden_grad.astype(BF16)
    up_bias_grad = jnp.sum(hidden_low.astype(F32), 0)
    first_grad_in = second_grad + matmul(hidden_low, w_up.T)
    first_grad, gain_one_grad, shift_one_grad = norm_backward(
        first_grad_in, first_normal, first_scale, gain_one
    )
    attended_grad = first_grad.astype(BF16)
    output_bias_grad = jnp.sum(attended_grad.astype(F32), 0)
    context_grad = dot_lanes(attended_grad, w_out).astype(BF16)
    context_grad_parts = [
        place.to_heads(context_grad[:, 256 * k : 256 * k + 256], i, j)
        for k, (i, j) in enumerate(order)
    ]
    context_grad_rows = jnp.concatenate(context_grad_parts, 0)

    down_grad = dot_rows(active_low, branch_grad).astype(BF16)
    up_grad = dot_rows(first_low, hidden_low).astype(BF16)
    output_grad_parts = dot_rows(context_tok, attended_grad).astype(BF16).reshape(4, 256, width)[:, :192]
    output_grad_parts = jnp.stack(
        [output_grad_parts[0], output_grad_parts[2], output_grad_parts[1], output_grad_parts[3]]
    )
    token_group = place.h * 2 + place.c
    output_grad = jnp.stack([pick(output_grad_parts, token_group ^ g) for g in range(4)])
    chunked = (2, slabs, 2, 2)
    vector_grads = jnp.stack(
        [output_bias_grad, gain_one_grad, shift_one_grad, down_bias_grad, gain_two_grad, shift_two_grad]
    )
    vector_grads = vector_grads.reshape(6, devices, share).transpose(1, 0, 2).reshape(devices, 6 * share)
    vector_grads = jnp.concatenate([vector_grads, up_bias_grad.reshape(devices, 4 * share)], 1)
    vector_grads = jnp.pad(vector_grads, ((0, 0), (0, width - 10 * share))).astype(BF16)
    output_grad = jnp.concatenate(
        [output_grad.reshape(devices, share, width), vector_grads[:, None]], 1
    )
    down_share = scatter_sum(place, down_grad.reshape(chunked + (4 * share, width)))
    up_share = scatter_sum(place, up_grad.reshape(chunked + (share, hidden_width)))
    output_share = scatter_sum(place, output_grad.reshape(chunked + (share + 1, width)))

    query_grad, own_grad, next_grad, prev_grad, global_grad = attend_backward(
        slots, queries, probs, context_grad_rows, pieces
    )
    ring_sum = global_grad
    for k in range(1, slabs):
        ring_sum = ring_sum + place.along_slabs(global_grad, k)
    ring_sum = ring_sum + place.sibling(ring_sum)
    kv_grad = (
        own_grad + place.to_next(next_grad).astype(F32) + place.to_previous(prev_grad).astype(F32)
    )
    half = 2 * place.n + place.c
    for which in range(2):
        block = global_blocks[which]
        within = block % 32
        at = ((within // 8) ^ flip) * 8 + within % 8
        here = (jnp.arange(32) == at) & (block // 32 == half)
        kv_grad = kv_grad + jnp.where(here[:, None, None], ring_sum[which][None], 0.0)
    kv_grad = kv_grad.astype(BF16).reshape(2048, 384)
    heads_grad = jnp.concatenate([query_grad, kv_grad], 1)

    tokens_grad = first_grad
    for k, (i, j) in enumerate(order):
        part = dot_lanes(heads_grad[k * tok_rows : (k + 1) * tok_rows], w_heads).astype(BF16)
        tokens_grad = tokens_grad + place.to_tokens(part, i, j).astype(F32)

    token_rows = jnp.concatenate(token_parts, 0)
    heads_weight_grad = dot_rows(token_rows, heads_grad).astype(BF16)
    bias_grad = jnp.sum(heads_grad.astype(F32), 0).astype(BF16)
    chunks = jnp.concatenate(
        [
            heads_weight_grad.reshape(devices, share, width),
            jnp.broadcast_to(bias_grad, (devices, 1, width)),
        ],
        1,
    )
    found = scatter_group(place, chunks.reshape(chunked + (share + 1, width)))
    parts = [from_head(value) for value in found]
    query_all, key_all, value_all = (
        jnp.concatenate([part[i] for part in parts], -1) for i in range(3)
    )
    start = share * (place.h * 4 * slabs + 4 * place.n + 2 * place.x + place.c)
    query_all = query_all * scale
    query_bias_share = lax.dynamic_slice_in_dim(query_all[share], start, share)
    value_bias_share = lax.dynamic_slice_in_dim(value_all[share], start, share)
    small = output_share[share]
    pieces_of = [small[i * share : (i + 1) * share] for i in range(6)]

    return (
        result.astype(BF16),
        tokens_grad,
        query_all[:share],
        query_bias_share,
        key_all[:share],
        value_all[:share],
        value_bias_share,
        output_share[:share],
        pieces_of[0],
        pieces_of[1],
        pieces_of[2],
        up_share,
        small[6 * share : 10 * share],
        down_share,
        pieces_of[3],
        pieces_of[4],
        pieces_of[5],
    )


def solution(mesh):
    rows = P(("head", "blk"), None)
    vector = P(("head", "blk"))
    tokens = P(("blk", "head"), None)
    return jax.shard_map(
        body,
        mesh=mesh,
        in_specs=(
            tokens,
            tokens,
            P(),
            P(),
            P("head", "blk", None),
            rows,
            vector,
            rows,
            rows,
            vector,
            rows,
            vector,
            vector,
            vector,
            rows,
            vector,
            rows,
            vector,
            vector,
            vector,
        ),
        out_specs=(
            tokens,
            tokens,
            rows,
            vector,
            rows,
            rows,
            vector,
            rows,
            vector,
            vector,
            vector,
            rows,
            vector,
            rows,
            vector,
            vector,
            vector,
        ),
        check_vma=False,
    )
```

```python
from functools import partial

import jax
import jax.numpy as jnp
from jax import lax
from jax.experimental import pallas as pl
from jax.experimental.pallas import tpu as pltpu
from jax.sharding import Mesh
from jax.sharding import PartitionSpec as P

HEAD_DIM = 64
BLOCK = 64
LANES = 128
NORM_EPS = 1e-06
MASKED = -1e30
AXES = ("head", "slab", "x", "core")
CHIPS = ("head", "x")
BF16 = jnp.bfloat16
F32 = jnp.float32
PAIRS = ((0, 0), (0, 1), (1, 0), (1, 1))
VMEM_LIMIT = 60 * 1024 * 1024


def matmul(left, right):
    return jnp.dot(left, right, preferred_element_type=F32)


def dot_rows(left, right):
    return lax.dot_general(left, right, (((0,), (0,)), ((), ())), preferred_element_type=F32)


def dot_lanes(left, right):
    return lax.dot_general(left, right, (((1,), (1,)), ((), ())), preferred_element_type=F32)


class Place:
    def __init__(self):
        self.slabs = lax.axis_size("slab")
        self.size = 4 * self.slabs
        self.h, self.n, self.x, self.c = (lax.axis_index(axis) for axis in AXES)

    def send(self, value, target):
        def index(h, n, x, c):
            return h * self.size + 4 * n + 2 * x + c

        route = [
            (index(h, n, x, c), index(*target(h, n, x, c)))
            for h in range(2)
            for n in range(self.slabs)
            for x in range(2)
            for c in range(2)
        ]
        return lax.ppermute(value, AXES, route)

    def along_slabs(self, value, k):
        return self.send(value, lambda h, n, x, c: (h, n ^ k, x, c))

    def across(self, value, i, j):
        return self.send(value, lambda h, n, x, c: (h ^ i, n, x ^ j, c))

    def sibling(self, value):
        return self.send(value, lambda h, n, x, c: (h, n, x, 1 - c))

    def to_heads(self, value, i, j):
        return self.send(value, lambda h, n, x, c: (h ^ i, n, c ^ j, x))

    def to_tokens(self, value, i, j):
        return self.send(value, lambda h, n, x, c: (h ^ i, n, c, x ^ j))

    def to_next(self, value):
        def target(h, n, x, c):
            return (h, n, x, 1) if c == 0 else (h, (n + 1) % self.slabs, x, 0)

        return self.send(value, target)

    def to_previous(self, value):
        def target(h, n, x, c):
            return (h, n, x, 0) if c == 1 else (h, (n - 1) % self.slabs, x, 1)

        return self.send(value, target)


def exchange(value, axes):
    return lax.all_to_all(value, axes, split_axis=0, concat_axis=0, tiled=True)


def pick(value, index, axis=0):
    return lax.dynamic_index_in_dim(value, index, axis, keepdims=False)


def kernel_call(kernel, out_shape, name, flops=1000, **options):
    return pl.pallas_call(
        kernel,
        out_shape=out_shape,
        compiler_params=pltpu.CompilerParams(vmem_limit_bytes=VMEM_LIMIT),
        cost_estimate=pl.CostEstimate(
            flops=flops, bytes_accessed=1000, transcendentals=0
        ),
        name=name,
        **options,
    )


def whole(count):
    return [pl.BlockSpec(memory_space=pltpu.VMEM)] * count


def smem():
    return pl.BlockSpec(memory_space=pltpu.SMEM)


def after(value, *others):
    return lax.optimization_barrier((value,) + others)[0]


def side_of(head):
    return 1 - head % 2


def half_tile(value, start, side):
    tile = start // LANES * LANES
    found = value[:, tile : tile + LANES].astype(F32)
    if (start % LANES) // HEAD_DIM != side:
        found = pltpu.roll(found, HEAD_DIM, 1)
    return found


def left_lanes(rows):
    return lax.broadcasted_iota(jnp.int32, (rows, LANES), 1) < HEAD_DIM


def pack_heads(query_weight, key_weight, value_weight, biases, scale):
    share = query_weight.shape[0]

    def kernel(q_ref, k_ref, v_ref, b_ref, out_ref):
        left = left_lanes(share)
        for group in range(4):
            start = 3 * group * HEAD_DIM
            q = [half_tile(q_ref, start + t * HEAD_DIM, side_of(t)) * scale for t in range(3)]
            out_ref[group, :, :LANES] = jnp.where(left, q[1], q[0]).astype(BF16)
            extra = b_ref[...].astype(F32)
            out_ref[group, :, LANES : 2 * LANES] = jnp.where(left, extra, q[2]).astype(BF16)
            for t in range(3):
                side = side_of(t)
                k = half_tile(k_ref, start + t * HEAD_DIM, side)
                v = half_tile(v_ref, start + t * HEAD_DIM, 1 - side)
                both = jnp.where(left, k, v) if side == 0 else jnp.where(left, v, k)
                out_ref[group, :, (2 + t) * LANES : (3 + t) * LANES] = both.astype(BF16)

    return kernel_call(
        kernel,
        jax.ShapeDtypeStruct((4, share, 5 * LANES), BF16),
        "pack_heads",
        in_specs=whole(4),
        out_specs=whole(1)[0],
    )(query_weight, key_weight, value_weight, biases)


def pack_rest(up, down, output, vectors):
    share, width = output.shape
    height = -(-(9 * share + 8) // 16) * 16
    count = len(vectors)

    def kernel(up_ref, down_ref, output_ref, *refs):
        out_ref = refs[-1]
        for i in range(4):
            out_ref[i * share : (i + 1) * share] = up_ref[:, i * width : (i + 1) * width]
        out_ref[4 * share : 8 * share] = down_ref[...]
        out_ref[8 * share : 9 * share] = output_ref[...]
        row = lax.broadcasted_iota(jnp.int32, (height - 9 * share, LANES), 0)
        total = jnp.zeros(row.shape, F32)
        for i, ref in enumerate(refs[:count]):
            total = jnp.where(row == i, jnp.broadcast_to(ref[...].astype(F32), row.shape), total)
        out_ref[9 * share :, :LANES] = total.astype(BF16)
        out_ref[9 * share :, LANES:] = jnp.zeros((height - 9 * share, width - LANES), BF16)

    vectors = [jnp.pad(v, (0, LANES - v.shape[0]))[None] for v in vectors]
    return kernel_call(
        kernel,
        jax.ShapeDtypeStruct((height, width), BF16),
        "pack_rest",
        in_specs=whole(3 + count),
        out_specs=whole(1)[0],
    )(up, down, output, *vectors)


def stack_heads(parts):
    def kernel(*refs):
        for k, ref in enumerate(refs[:-1]):
            refs[-1][k] = ref[...]

    return kernel_call(
        kernel,
        jax.ShapeDtypeStruct((len(parts),) + parts[0].shape, BF16),
        "stack_heads",
        in_specs=whole(len(parts)),
        out_specs=whole(1)[0],
    )(*parts)


def assemble_heads(place, column, other):
    slabs, _, rows, columns = column.shape
    where = jnp.stack([place.h, place.n, place.x, place.c]).astype(jnp.int32)

    def kernel(where_ref, mine_ref, other_ref, out_ref, bias_ref):
        h, x, c = where_ref[0], where_ref[2], where_ref[3]
        left = left_lanes(rows)
        right = jnp.logical_not(left)
        for core, ref in enumerate((mine_ref, other_ref)):
            for p, (i, j) in enumerate(PAIRS):
                first = ref[0, p, :, :LANES].astype(F32)
                second = ref[0, p, :, LANES : 2 * LANES]
                q = (
                    jnp.where(right, first, 0.0),
                    jnp.where(left, first, 0.0),
                    jnp.where(right, second.astype(F32), 0.0),
                )
                at = (h ^ i, 0, x ^ j, c ^ core)
                for t in range(3):
                    out_ref[(*at, slice(None), slice(t * LANES, (t + 1) * LANES))] = q[t].astype(BF16)
                out_ref[(*at, slice(None), slice(3 * LANES, 6 * LANES))] = ref[0, p, :, 2 * LANES :]
                bias_ref[at] = second

    found = kernel_call(
        kernel,
        (
            jax.ShapeDtypeStruct((2, slabs, 2, 2, rows, 6 * LANES), BF16),
            jax.ShapeDtypeStruct((2, slabs, 2, 2, rows, LANES), BF16),
        ),
        "assemble_heads",
        grid_spec=pltpu.PrefetchScalarGridSpec(
            num_scalar_prefetch=1,
            grid=(slabs,),
            in_specs=[pl.BlockSpec((1, 4, rows, columns), lambda k, w: (k, 0, 0, 0))] * 2,
            out_specs=[
                pl.BlockSpec((2, 1, 2, 2, rows, 6 * LANES), lambda k, w: (0, k ^ w[1], 0, 0, 0, 0)),
                pl.BlockSpec((2, 1, 2, 2, rows, LANES), lambda k, w: (0, k ^ w[1], 0, 0, 0, 0)),
            ],
        ),
    )(where, column, other)
    return [value.reshape(8 * slabs, *value.shape[4:]) for value in found]


def assemble_rest(place, mine, other, share):
    _, slabs, rows, width = mine.shape
    where = place.c.reshape(1).astype(jnp.int32)

    def kernel(where_ref, mine_ref, other_ref, up_ref, down_ref, output_ref, vector_ref):
        for core, ref in ((where_ref[0], mine_ref), (1 - where_ref[0], other_ref)):
            for p in range(4):
                at = (p // 2, 0, p % 2, core)
                for q in range(4):
                    columns = slice(q * width, (q + 1) * width)
                    up_ref[(*at, slice(None), columns)] = ref[p, 0, q * share : (q + 1) * share]
                down_ref[at] = ref[p, 0, 4 * share : 8 * share]
                output_ref[at] = ref[p, 0, 8 * share : 9 * share]
                vector_ref[at] = ref[p, 0, 9 * share :]

    shapes = ((share, 4 * width), (4 * share, width), (share, width), (rows - 9 * share, width))
    found = kernel_call(
        kernel,
        tuple(jax.ShapeDtypeStruct((2, slabs, 2, 2) + shape, BF16) for shape in shapes),
        "assemble_rest",
        grid_spec=pltpu.PrefetchScalarGridSpec(
            num_scalar_prefetch=1,
            grid=(slabs,),
            in_specs=[pl.BlockSpec((4, 1, rows, width), lambda n, w: (0, n, 0, 0))] * 2,
            out_specs=[
                pl.BlockSpec((2, 1, 2, 2) + shape, lambda n, w: (0, n, 0, 0, 0, 0)) for shape in shapes
            ],
        ),
    )(where, mine, other)
    return [value.reshape(8 * slabs, *value.shape[4:]) for value in found]


def weight_grads(place, active, branch_grad, first, hidden_grad, context, attended_grad, vectors):
    devices = 8 * place.slabs
    step = devices // 4
    tokens, width = first.shape
    share = width // devices
    rows = -(-(9 * share + 8) // 16) * 16
    where = jnp.stack([place.h * 2 + place.c, place.c]).astype(jnp.int32)

    def kernel(where_ref, active_ref, branch_ref, first_ref, hidden_ref, context_ref, attended_ref, vector_ref, kept_ref, sent_ref):
        even = where_ref[1] == 0

        def put(start, stop, value):
            value = value.astype(BF16).reshape(step, stop - start, width)
            for p in range(step // 2):
                kept_ref[p, start:stop] = jnp.where(even, value[2 * p], value[2 * p + 1])
                sent_ref[p, start:stop] = jnp.where(even, value[2 * p + 1], value[2 * p])

        put(4 * share, 8 * share, dot_rows(active_ref[...], branch_ref[...]))
        columns = first_ref[...]
        for q in range(4):
            up = dot_rows(columns, hidden_ref[:, q * width : (q + 1) * width])
            put(q * share, (q + 1) * share, up[: step * share])
        put(8 * share, 9 * share, dot_rows(context_ref[...], attended_ref[...])[: step * share])
        for p in range(step // 2):
            for ref, at in ((kept_ref, 2 * p + where_ref[1]), (sent_ref, 2 * p + 1 - where_ref[1])):
                ref[p, 9 * share :] = jnp.zeros((rows - 9 * share, width), BF16)
                ref[p, 9 * share : 9 * share + 8, :LANES] = vector_ref[at].astype(BF16)

    first = jnp.pad(first.reshape(tokens, 4, 192), ((0, 0), (0, 0), (0, 64))).reshape(tokens, 1024)
    half = jax.ShapeDtypeStruct((devices // 2, rows, width), BF16)
    return kernel_call(
        kernel,
        (half, half),
        "weight_grads",
        15_000_000_000,
        grid_spec=pltpu.PrefetchScalarGridSpec(
            num_scalar_prefetch=1,
            grid=(4,),
            in_specs=[
                pl.BlockSpec((tokens, width), lambda g, w: (0, g)),
                pl.BlockSpec((tokens, width), lambda g, w: (0, 0)),
                pl.BlockSpec((tokens, 256), lambda g, w: (0, g)),
                pl.BlockSpec((tokens, 4 * width), lambda g, w: (0, 0)),
                pl.BlockSpec((tokens, 256), lambda g, w: (0, g ^ w[0])),
                pl.BlockSpec((tokens, width), lambda g, w: (0, 0)),
                pl.BlockSpec((step, 8, LANES), lambda g, w: (g, 0, 0)),
            ],
            out_specs=[pl.BlockSpec((step // 2, rows, width), lambda g, w: (g, 0, 0))] * 2,
        ),
    )(where, active, branch_grad, first, hidden_grad, context, attended_grad, vectors)


def heads_weight_grads(place, token_rows, heads_grads, bias_grads):
    slabs = place.slabs
    width = token_rows[0].shape[1]
    share = width // (8 * slabs)
    rows = -(-(share + 1) // 16) * 16
    where = place.c.reshape(1).astype(jnp.int32)

    def kernel(where_ref, x0_ref, x1_ref, g0_ref, g1_ref, b0_ref, b1_ref, kept_ref, sent_ref):
        even = where_ref[0] == 0
        bias = jnp.broadcast_to(b0_ref[...] + b1_ref[...], (rows - share, width)).astype(BF16)
        value = dot_rows(x0_ref[...], g0_ref[...]) + dot_rows(x1_ref[...], g1_ref[...])
        value = value.astype(BF16).reshape(8 * slabs, share, width)
        for p in range(4 * slabs):
            kept_ref[p, :share] = jnp.where(even, value[2 * p], value[2 * p + 1])
            sent_ref[p, :share] = jnp.where(even, value[2 * p + 1], value[2 * p])
            kept_ref[p, share:] = bias
            sent_ref[p, share:] = bias

    half = jax.ShapeDtypeStruct((4 * slabs, rows, width), BF16)
    kept, sent = kernel_call(
        kernel,
        (half, half),
        "heads_weight_grads",
        20_000_000_000,
        in_specs=[smem()] + whole(6),
        out_specs=whole(2),
    )(where, *token_rows, *heads_grads, *bias_grads)
    return kept, place.sibling(sent)


def scatter_across(place, kept, arrived):
    slabs = place.slabs
    _, rows, width = kept.shape

    def kernel(kept_ref, arrived_ref, out_ref):
        for h in range(2):
            for x in range(2):
                total = kept_ref[h, 0, x].astype(F32) + arrived_ref[h, 0, x].astype(F32)
                out_ref[2 * h + x, 0] = total.astype(BF16)

    parts = kernel_call(
        kernel,
        jax.ShapeDtypeStruct((4, slabs, rows, width), BF16),
        "scatter_across",
        grid=(slabs,),
        in_specs=[pl.BlockSpec((2, 1, 2, rows, width), lambda n: (0, n, 0, 0, 0))] * 2,
        out_specs=pl.BlockSpec((4, 1, rows, width), lambda n: (0, n, 0, 0)),
    )(*(value.reshape(2, slabs, 2, rows, width) for value in (kept, arrived)))
    return parts


def scatter_slabs(parts):
    slabs, rows, width = parts.shape[1:]

    def kernel(ref, out_ref):
        out_ref[0] = sum(ref[p, 0].astype(F32) for p in range(4)).astype(BF16)

    total = kernel_call(
        kernel,
        jax.ShapeDtypeStruct((slabs, rows, width), BF16),
        "scatter_slabs",
        20_000_000_000,
        grid=(slabs,),
        in_specs=[pl.BlockSpec((4, 1, rows, width), lambda n: (0, n, 0, 0))],
        out_specs=pl.BlockSpec((1, rows, width), lambda n: (n, 0, 0)),
    )(parts)
    return total


def added(parts):
    return sum(part.astype(F32) for part in parts)


def scatter_group(place, kept, arrived, returned):
    slabs = place.slabs
    _, rows, width = kept.shape
    where = jnp.stack([place.n, place.h, place.x]).astype(jnp.int32)

    def along(where_ref, kept_ref, arrived_ref, *outs):
        for k, out in enumerate(outs):
            at = where_ref[0] ^ k
            for h in range(2):
                for x in range(2):
                    pair = kept_ref[h, at, x].astype(F32) + arrived_ref[h, at, x].astype(F32)
                    out[h, x] = pair.astype(BF16)

    parts = kernel_call(
        along,
        [jax.ShapeDtypeStruct((2, 2, rows, width), BF16)] * slabs,
        "group_along",
        in_specs=[smem()] + whole(2),
        out_specs=whole(slabs),
    )(where, *(value.reshape(2, slabs, 2, rows, width) for value in (kept, arrived)))
    parts = [parts[0]] + [place.along_slabs(parts[k], k) for k in range(1, slabs)]

    *parts, returned[0], returned[1] = lax.optimization_barrier((*parts, *returned[:2]))

    def across(where_ref, *refs):
        for (i, j), out in zip(PAIRS, refs[slabs:]):
            at = (where_ref[1] ^ i, where_ref[2] ^ j)
            out[...] = sum(ref[at].astype(F32) for ref in refs[:slabs]).astype(BF16)

    parts = kernel_call(
        across,
        [jax.ShapeDtypeStruct((rows, width), BF16)] * 4,
        "group_across",
        in_specs=[smem()] + whole(slabs),
        out_specs=whole(4),
    )(where, *parts)
    return [parts[0]] + [place.across(part, i, j) for part, (i, j) in zip(parts[1:], PAIRS[1:])]


def finish_heads(place, parts, share, scale):
    rows, width = parts[0].shape
    where = (place.h * 2 + place.x).reshape(1).astype(jnp.int32)

    def kernel(where_ref, *refs):
        sources, outs, held = refs[:4], refs[4:9], refs[9]
        for p, ref in enumerate(sources):
            held[p] = ref[...].astype(F32)
        left = left_lanes(rows)
        for which, (out, bias) in enumerate(((outs[0], outs[3]), (outs[1], None), (outs[2], outs[4]))):
            for tile in range(width // LANES):
                sides = []
                for side in range(2):
                    head = 2 * tile + side
                    value = held[(head // 3) ^ where_ref[0]]
                    t = head % 3
                    if which == 0:
                        start = t * LANES + side_of(t) * HEAD_DIM
                    else:
                        at = side_of(t) if which == 1 else 1 - side_of(t)
                        start = (3 + t) * LANES + at * HEAD_DIM
                    sides.append(half_tile(value, start, side))
                value = jnp.where(left, sides[0], sides[1])
                if which == 0:
                    value = value * scale
                lanes = slice(tile * LANES, (tile + 1) * LANES)
                out[:, lanes] = value[:share]
                if bias is not None:
                    bias[:, lanes] = value[share : share + 1]

    weight = jax.ShapeDtypeStruct((share, width), F32)
    bias = jax.ShapeDtypeStruct((1, width), F32)
    return kernel_call(
        kernel,
        (weight, weight, weight, bias, bias),
        "finish_heads",
        in_specs=[smem()] + whole(4),
        out_specs=whole(5),
        scratch_shapes=[pltpu.VMEM((4, rows, width), F32)],
    )(where, *parts)


def heads_backward(place, results, halos, ring_sum, global_at, w_heads, part):
    dqs = [results[head][0][2 * part + u] for u in range(2) for head in range(3)]
    owns = [halos[head][0] for head in range(3)]
    arrived = [halos[head][side] for head in range(3) for side in (1, 2)]
    width = w_heads.shape[0]
    rows = 512

    def kernel(at_ref, *refs):
        dq_refs, own_refs, arrived_refs = refs[:6], refs[6:9], refs[9:15]
        ring_ref, w_ref = refs[15:17]
        heads_ref, bias_ref, out_refs, held = refs[17], refs[18], refs[19:21], refs[21]
        bias = jnp.zeros((1, width), F32)
        for u in range(2):
            row = slice(u * rows, (u + 1) * rows)
            for head in range(3):
                heads_ref[row, head * LANES : (head + 1) * LANES] = dq_refs[3 * u + head][...]
                blocks = slice(u * 8, (u + 1) * 8)
                held[...] = (
                    own_refs[head][blocks]
                    + arrived_refs[2 * head][blocks].astype(F32)
                    + arrived_refs[2 * head + 1][blocks].astype(F32)
                )
                for which in range(2):
                    at = at_ref[which] - (2 * part + u) * 8

                    @pl.when((at >= 0) & (at < 8))
                    def _():
                        held[jnp.clip(at, 0, 7)] += ring_ref[which, :, head * LANES : (head + 1) * LANES]

                lanes = slice((3 + head) * LANES, (4 + head) * LANES)
                heads_ref[row, lanes] = held[...].reshape(rows, LANES).astype(BF16)
            value = heads_ref[row]
            out_refs[u][...] = dot_lanes(value, w_ref[...]).astype(BF16)
            bias = bias + jnp.sum(value.astype(F32), 0, keepdims=True)
        bias_ref[...] = bias

    own_spec = pl.BlockSpec((16, BLOCK, LANES), lambda i: (part, 0, 0))
    full = [
        pl.BlockSpec(value.shape, lambda i, rank=value.ndim: (0,) * rank)
        for value in dqs + [ring_sum, w_heads]
    ]
    shard = jax.ShapeDtypeStruct((rows, width), BF16)
    return kernel_call(
        kernel,
        (
            jax.ShapeDtypeStruct((2 * rows, width), BF16),
            jax.ShapeDtypeStruct((1, width), F32),
            shard,
            shard,
        ),
        "heads_backward",
        grid=(1,),
        in_specs=[smem()] + full[:6] + [own_spec] * 9 + full[6:],
        out_specs=[
            pl.BlockSpec((2 * rows, width), lambda i: (0, 0)),
            pl.BlockSpec((1, width), lambda i: (0, 0)),
            pl.BlockSpec((rows, width), lambda i: (0, 0)),
            pl.BlockSpec((rows, width), lambda i: (0, 0)),
        ],
        scratch_shapes=[pltpu.VMEM((8, BLOCK, LANES), F32)],
    )(global_at, *dqs, *owns, *arrived, ring_sum, w_heads)


def doc_count(position, starts_ref, count):
    total = jnp.zeros(position.shape, jnp.int32)
    for which in range(count):
        total = total + (position >= starts_ref[which]).astype(jnp.int32)
    return total


def load_slots(kv, slots_ref, base, head):
    lanes = slice(head * LANES, (head + 1) * LANES)
    return jnp.concatenate([kv[slots_ref[base + s], :, lanes] for s in range(8)], 0)


def copy_in(sources, kv, sems):
    copies = []
    start = 0
    for which, source in enumerate(sources):
        stop = start + source.shape[0]
        copies.append(pltpu.make_async_copy(source, kv.at[start:stop], sems.at[which]))
        start = stop
    for copy in copies:
        copy.start()
    for copy in copies:
        copy.wait()


def attend_forward(slots, ids, query_ids, starts, queries, pieces, part):
    heads = 3
    blocks = 32
    docs = starts.shape[0]
    many = len(pieces)

    def kernel(slots_ref, ids_ref, query_ids_ref, starts_ref, q0_ref, q1_ref, *refs):
        sources = refs[:many]
        ctx0_ref, ctx1_ref, p0_ref, p1_ref, kv, sems = refs[many:]
        step = pl.program_id(0)

        @pl.when(step == 0)
        def _():
            copy_in(sources, kv, sems)

        lane = lax.broadcasted_iota(jnp.int32, (1, LANES), 1)
        row = lax.broadcasted_iota(jnp.int32, (BLOCK, LANES), 0)
        shards = ((q0_ref, ctx0_ref, p0_ref), (q1_ref, ctx1_ref, p1_ref))
        for u, (q_ref, ctx_ref, p_ref) in enumerate(shards):
            block = part * 16 + u * 8 + step
            query_doc = doc_count(query_ids_ref[block] * BLOCK + row, starts_ref, docs)
            contexts = []
            for head in range(heads):
                base = (head * blocks + block) * 8
                slot = load_slots(kv, slots_ref, base, head)
                q = q_ref[:, head * LANES : (head + 1) * LANES]
                scores = dot_lanes(q, slot)
                tiles = []
                for tile in range(4):
                    first = ids_ref[base + 2 * tile] * BLOCK
                    second = ids_ref[base + 2 * tile + 1] * BLOCK - BLOCK
                    key_doc = doc_count(
                        jnp.where(lane < BLOCK, first + lane, second + lane), starts_ref, docs
                    )
                    tiles.append(
                        jnp.where(
                            query_doc == key_doc,
                            scores[:, tile * LANES : (tile + 1) * LANES],
                            MASKED,
                        )
                    )
                top = jnp.maximum(
                    jnp.maximum(tiles[0], tiles[1]), jnp.maximum(tiles[2], tiles[3])
                )
                top = jnp.max(top, -1, keepdims=True)
                tiles = [jnp.exp(tile - top) for tile in tiles]
                total = (tiles[0] + tiles[1]) + (tiles[2] + tiles[3])
                inverse = 1.0 / jnp.sum(total, -1, keepdims=True)
                low = jnp.concatenate([(tile * inverse).astype(BF16) for tile in tiles], 1)
                p_ref[0, head] = low
                contexts.append(matmul(low, slot))
            ctx_ref[:, :LANES] = jnp.where(lane < BLOCK, contexts[0], contexts[1]).astype(BF16)
            ctx_ref[:, LANES:] = jnp.where(lane < BLOCK, contexts[2], 0.0).astype(BF16)

    context = jax.ShapeDtypeStruct((8 * BLOCK, 2 * LANES), BF16)
    context_spec = pl.BlockSpec((BLOCK, 2 * LANES), lambda i, *_: (i, 0))
    prob = jax.ShapeDtypeStruct((8, heads, BLOCK, 8 * BLOCK), BF16)
    prob_spec = pl.BlockSpec((1, heads, BLOCK, 8 * BLOCK), lambda i, *_: (i, 0, 0, 0))
    return pl.pallas_call(
        kernel,
        out_shape=(context, context, prob, prob),
        grid_spec=pltpu.PrefetchScalarGridSpec(
            num_scalar_prefetch=4,
            grid=(8,),
            in_specs=[
                pl.BlockSpec((BLOCK, heads * LANES), lambda i, *_: (i, 0)),
                pl.BlockSpec((BLOCK, heads * LANES), lambda i, *_: (8 + i, 0)),
            ]
            + [pl.BlockSpec(memory_space=pl.ANY)] * many,
            out_specs=[context_spec, context_spec, prob_spec, prob_spec],
            scratch_shapes=[
                pltpu.VMEM((3 * blocks + 2, BLOCK, heads * LANES), BF16),
                pltpu.SemaphoreType.DMA((many,)),
            ],
        ),
        compiler_params=pltpu.CompilerParams(vmem_limit_bytes=VMEM_LIMIT),
        cost_estimate=pl.CostEstimate(
            flops=18_000_000_000, bytes_accessed=1000, transcendentals=0
        ),
        name="attend_forward",
    )(slots, ids, query_ids, starts, queries, queries, *pieces)


def attend_backward(slots, queries, probs, grads, pieces, head):
    blocks = 32
    many = len(pieces)
    lanes = slice(head * LANES, (head + 1) * LANES)

    def kernel(slots_ref, *refs):
        q_refs, p_refs, grad_refs = refs[:4], refs[4:8], refs[8:12]
        sources = refs[12 : 12 + many]
        dq_refs = refs[12 + many : 16 + many]
        own_ref, next_ref, prev_ref, glob_ref, kv, acc, sems = refs[16 + many :]
        step = pl.program_id(0)

        @pl.when(step == 0)
        def _():
            copies = []
            start = 0
            for which, source in enumerate(sources):
                stop = start + source.shape[0]
                copies.append(
                    pltpu.make_async_copy(
                        source.at[:, :, lanes], kv.at[start:stop], sems.at[which]
                    )
                )
                start = stop
            for copy in copies:
                copy.start()

            def clear(i, _):
                acc[i] = jnp.zeros(acc.shape[1:], F32)
                return _

            lax.fori_loop(0, acc.shape[0], clear, 0)
            for copy in copies:
                copy.wait()

        lane = lax.broadcasted_iota(jnp.int32, (1, LANES), 1)
        left = lane < BLOCK
        value_side = left if head % 2 == 0 else jnp.logical_not(left)
        for u in range(4):
            base = (head * blocks + u * 8 + step) * 8
            slot = jnp.concatenate([kv[slots_ref[base + s]] for s in range(8)], 0)
            grad = jnp.where(value_side, grad_refs[u][...].astype(F32), 0.0).astype(BF16)
            low = p_refs[u][0, 0]
            probs_f = low.astype(F32)
            prob_grad = dot_lanes(grad, slot)
            both = probs_f * prob_grad
            inner = jnp.sum(both, -1, keepdims=True)
            score_grad = (both - probs_f * inner).astype(BF16)
            dq = matmul(score_grad, slot)
            dq_refs[u][...] = jnp.where(value_side, 0.0, dq).astype(BF16)
            slot_grad = dot_rows(
                jnp.concatenate([score_grad, low], 0),
                jnp.concatenate([q_refs[u][...], grad], 0),
            )
            for s in range(8):
                where = slots_ref[base + s]
                acc[where] += slot_grad[s * BLOCK : (s + 1) * BLOCK]

        @pl.when(step == 7)
        def _():
            def finish(i, _):
                own_ref[i] = acc[i]
                next_ref[i] = acc[blocks + i].astype(BF16)
                prev_ref[i] = acc[2 * blocks + i].astype(BF16)
                return _

            lax.fori_loop(0, blocks, finish, 0)
            glob_ref[...] = acc[3 * blocks :]

    shape = (blocks, BLOCK, LANES)
    rows = [pl.BlockSpec((BLOCK, LANES), lambda i, *_, u=u: (8 * (u % 2) + i, head)) for u in range(4)]
    dq_spec = pl.BlockSpec((BLOCK, LANES), lambda i, *_: (i, 0))
    whole = pl.BlockSpec(shape, lambda i, *_: (0, 0, 0))
    return pl.pallas_call(
        kernel,
        out_shape=[jax.ShapeDtypeStruct((8 * BLOCK, LANES), BF16)] * 4
        + [
            jax.ShapeDtypeStruct(shape, F32),
            jax.ShapeDtypeStruct(shape, BF16),
            jax.ShapeDtypeStruct(shape, BF16),
            jax.ShapeDtypeStruct((2,) + shape[1:], F32),
        ],
        grid_spec=pltpu.PrefetchScalarGridSpec(
            num_scalar_prefetch=1,
            grid=(8,),
            in_specs=rows
            + [pl.BlockSpec((1, 1, BLOCK, 8 * BLOCK), lambda i, *_: (i, head, 0, 0))] * 4
            + [pl.BlockSpec((BLOCK, LANES), lambda i, *_: (i, head // 2))] * 4
            + [pl.BlockSpec(memory_space=pl.ANY)] * many,
            out_specs=[dq_spec] * 4
            + [whole, whole, whole, pl.BlockSpec((2,) + shape[1:], lambda i, *_: (0, 0, 0))],
            scratch_shapes=[
                pltpu.VMEM((3 * blocks + 2,) + shape[1:], BF16),
                pltpu.VMEM((3 * blocks + 2,) + shape[1:], F32),
                pltpu.SemaphoreType.DMA((many,)),
            ],
        ),
        compiler_params=pltpu.CompilerParams(vmem_limit_bytes=VMEM_LIMIT),
        cost_estimate=pl.CostEstimate(
            flops=18_000_000_000, bytes_accessed=1000, transcendentals=0
        ),
        name="attend_backward",
    )(slots, queries[0], queries[0], queries[1], queries[1], *probs, *grads, *pieces)


def norm_forward(value, gain, shift):
    center = value - jnp.mean(value, -1, keepdims=True)
    spread = jnp.mean(center * center, -1, keepdims=True)
    scale_row = lax.rsqrt(spread + NORM_EPS)
    normal = center * scale_row
    return (normal * gain + shift, normal, scale_row)


def norm_backward(grad, normal, scale_row, gain):
    gain_grad = jnp.sum(grad * normal, 0)
    shift_grad = jnp.sum(grad, 0)
    inner = grad * gain
    value_grad = scale_row * (
        inner
        - jnp.mean(inner, -1, keepdims=True)
        - normal * jnp.mean(inner * normal, -1, keepdims=True)
    )
    return (value_grad, gain_grad, shift_grad)


def local_block(place, within):
    shard = within // 8
    return (((shard % 2) ^ place.h) * 2 + ((shard // 2) ^ place.x)) * 8 + within % 8


def slot_tables(place, global_blocks, random_parts):
    ring = 2 * place.slabs
    half = 2 * place.n + place.c
    total = ring * 32
    found = []
    for arrived in random_parts:
        found.append(lax.dynamic_slice_in_dim(arrived, 3 * place.x, 3, 0).reshape(3, 2, 8, 3))
    chosen = jnp.stack(found, 2)
    chosen = jnp.where(place.h == 0, chosen, chosen[:, ::-1]).reshape(3, 32, 3)
    order = jnp.arange(32, dtype=jnp.int32)
    shard = order // 8
    query_ids = half * 32 + (((shard % 2) ^ place.x) * 2 + ((shard // 2) ^ place.h)) * 8 + order % 8
    near = (query_ids[:, None] + jnp.arange(-1, 2, dtype=jnp.int32)) % total
    ids = jnp.concatenate(
        [
            jnp.broadcast_to(near[None], (3, 32, 3)),
            jnp.broadcast_to(global_blocks, (3, 32, 2)),
            chosen,
        ],
        -1,
    )
    earlier = jnp.arange(8)[None, :] < jnp.arange(8)[:, None]
    repeated = jnp.any((ids[..., :, None] == ids[..., None, :]) & earlier, -1)
    distance = (ids // 32 - half) % ring
    region = jnp.where(distance == 0, 0, jnp.where(distance == 1, 1, 2))
    local = region * 32 + local_block(place, ids % 32)
    which = jnp.arange(8, dtype=jnp.int32)
    slots = jnp.where((which == 3) | (which == 4), 93 + which, local)
    marked = jnp.where(repeated, -1, ids)
    return (
        slots.reshape(-1).astype(jnp.int32),
        marked.reshape(-1).astype(jnp.int32),
        query_ids.astype(jnp.int32),
    )


def by_head(q, k, v):
    parts = [(m[..., :64], m[..., 64:128], m[..., 128:]) for m in (q, k, v)]
    (q0, q1, q2), (k0, k1, k2), (v0, v1, v2) = parts
    none = jnp.zeros_like(q0)
    return jnp.concatenate([none, q0, q1, none, none, q2, v0, k0, k1, v1, v2, k2], -1)


def body(
    tokens,
    cotangent,
    doc_lengths,
    global_blocks,
    random_blocks,
    query_weight,
    query_bias,
    key_weight,
    value_weight,
    value_bias,
    output_weight,
    output_bias,
    first_gain,
    first_shift,
    up_weight,
    up_bias,
    down_weight,
    down_bias,
    second_gain,
    second_shift,
):
    place = Place()
    slabs = place.slabs
    devices = 8 * slabs
    width = tokens.shape[1]
    share = query_weight.shape[0]
    hidden_width = up_weight.shape[1]
    scale = HEAD_DIM ** (-0.5)
    group = place.h * 2 + place.x
    token_group = place.h * 2 + place.c

    biases = jnp.pad(jnp.stack([query_bias, value_bias], 1), ((0, 0), (0, LANES - 2)))
    groups = pack_heads(query_weight, key_weight, value_weight, biases, scale)
    parts = [pick(groups, group)] + [
        place.across(pick(groups, group ^ (2 * i + j)), i, j) for i, j in PAIRS[1:]
    ]
    random_parts = [place.to_heads(random_blocks, 0, j) for j in range(2)]

    vectors = [
        output_bias, first_gain, first_shift, down_bias, second_gain, second_shift, up_bias
    ]
    packed = pack_rest(after(up_weight, groups), down_weight, output_weight, vectors)
    *parts, packed, random_parts[0], random_parts[1] = lax.optimization_barrier(
        (*parts, packed, *random_parts)
    )
    stacked = stack_heads(parts)
    tokens_late = after(tokens, stacked)
    token_parts = [place.to_heads(tokens_late, i, j) for i, j in PAIRS]
    heads_column = jnp.stack([stacked] + [place.along_slabs(stacked, k) for k in range(1, slabs)])
    packed = after(packed, heads_column)
    packed_column = exchange(jnp.broadcast_to(packed, (slabs,) + packed.shape), "slab")
    heads_column, *token_parts[2:] = lax.optimization_barrier((heads_column, *token_parts[2:]))
    other, *token_parts[:2] = lax.optimization_barrier((place.sibling(heads_column), *token_parts[:2]))
    arrived, bias = assemble_heads(place, heads_column, other)
    w_heads = arrived.reshape(width, width)
    bias = lax.dynamic_slice_in_dim(bias[..., :2], 2 * slabs * group, 2 * slabs).astype(F32)
    bias_query = bias[..., 0].reshape(192) * scale
    bias_value = bias[..., 1].reshape(192)
    b_heads = by_head(bias_query, jnp.zeros_like(bias_query), bias_value)

    slots, ids, query_ids = slot_tables(place, global_blocks, random_parts)
    which = jnp.arange(doc_lengths.shape[0])
    before = which[None, :] < which[:, None]
    starts = jnp.sum(jnp.where(before, doc_lengths[None, :], 0), 1).astype(jnp.int32)

    half = 2 * place.n + place.c
    token_rows = [jnp.concatenate(token_parts[2 * i : 2 * i + 2], 0) for i in range(2)]
    queries, own, following, previous = [], [], [], []

    def project(part):
        heads = (matmul(part, w_heads) + b_heads).astype(BF16)
        queries.append(heads[:, :384])
        own.append(heads[:, 384:].reshape(16, BLOCK, 384))

    def send_halo(kv):
        following.append(place.to_previous(kv))
        previous.append(place.to_next(kv))

    project(token_rows[0])
    project(token_rows[1])

    shown = []
    for i in range(2):
        at = local_block(place, global_blocks[i] % 32)
        found = jnp.where(at < 16, pick(own[0], at % 16), pick(own[1], at % 16))
        shown.append(jnp.where(global_blocks[i] // 32 == half, found, 0).astype(BF16))
    shown = jnp.stack(shown)
    shown = shown + place.sibling(shown)
    *late, shown = lax.optimization_barrier((*own, shown))
    send_halo(late[0])
    send_halo(late[1])
    mine = pick(shown, place.c)
    for k in range(1, slabs):
        mine = mine + place.along_slabs(pick(shown, place.c), k)
    theirs = place.sibling(mine)
    shared = jnp.where(place.c == 0, jnp.stack([mine, theirs]), jnp.stack([theirs, mine]))
    pieces = own + following + previous + [shared]

    packed_column = after(packed_column, mine)
    rest_column = exchange(jnp.broadcast_to(packed_column, (4,) + packed_column.shape), CHIPS)
    c2, c3, p2, p3 = attend_forward(slots, ids, query_ids, starts, queries[1], pieces, 1)
    sent = [place.to_tokens(c, i, j) for c, (i, j) in zip((c2, c3), PAIRS[2:])]
    c0, c1, p0, p1 = attend_forward(after(slots, c2), ids, query_ids, starts, queries[0], pieces, 0)
    probs = (p0, p1, p2, p3)
    mine = after(rest_column, c0)
    other = place.sibling(mine)
    sent = [place.to_tokens(c, i, j) for c, (i, j) in zip((c0, c1), PAIRS[:2])] + sent

    w_up, w_down, w_output, rest = assemble_rest(place, mine, other, share)
    w_up = w_up.reshape(width, hidden_width)
    w_down = w_down.reshape(hidden_width, width)
    vec = rest[:, :6, :share].transpose(1, 0, 2).reshape(6, width).astype(F32)
    b_output, gain_one, shift_one, b_down, gain_two, shift_two = (vec[i] for i in range(6))
    b_up = rest[:, 6, : 4 * share].reshape(hidden_width).astype(F32)

    context_tok = jnp.concatenate(sent, 1)
    w_output = w_output.reshape(4, 192, width)
    w_out = jnp.stack(
        [jnp.pad(pick(w_output, token_group ^ k), ((0, 64), (0, 0))) for k in range(4)]
    ).reshape(1024, width)

    first_sum = tokens.astype(F32) + matmul(context_tok, w_out) + b_output
    first, first_normal, first_scale = norm_forward(first_sum, gain_one, shift_one)
    first_low = first.astype(BF16)
    hidden = matmul(first_low, w_up) + b_up
    active, gelu_back = jax.vjp(partial(jax.nn.gelu, approximate=True), hidden)
    active_low = active.astype(BF16)
    second_sum = first + matmul(active_low, w_down) + b_down
    result, second_normal, second_scale = norm_forward(second_sum, gain_two, shift_two)
    second_grad, gain_two_grad, shift_two_grad = norm_backward(
        cotangent.astype(F32), second_normal, second_scale, gain_two
    )
    branch_grad = second_grad.astype(BF16)
    (hidden_grad,) = gelu_back(matmul(branch_grad, w_down.T))
    hidden_low = hidden_grad.astype(BF16)
    first_grad_in = second_grad + matmul(hidden_low, w_up.T)
    first_grad, gain_one_grad, shift_one_grad = norm_backward(
        first_grad_in, first_normal, first_scale, gain_one
    )
    attended_grad = first_grad.astype(BF16)
    context_grad = dot_lanes(attended_grad, w_out).astype(BF16)
    context_grads = [
        place.to_heads(context_grad[:, 256 * k : 256 * k + 256], i, j)
        for k, (i, j) in enumerate(PAIRS)
    ]

    down_bias_grad = jnp.sum(branch_grad.astype(F32), 0)
    up_bias_grad = jnp.sum(hidden_low.astype(F32), 0)
    output_bias_grad = jnp.sum(attended_grad.astype(F32), 0)
    vector_grads = jnp.stack(
        [output_bias_grad, gain_one_grad, shift_one_grad, down_bias_grad, gain_two_grad, shift_two_grad]
    )
    vector_grads = jnp.pad(vector_grads.reshape(6, devices, share), ((0, 2), (0, 0), (0, LANES - share)))
    wide = jnp.pad(up_bias_grad.reshape(1, devices, 4 * share), ((6, 1), (0, 0), (0, LANES - 4 * share)))
    vector_grads = (vector_grads + wide).transpose(1, 0, 2)
    kept, sent = weight_grads(
        place,
        after(active_low, context_grad),
        branch_grad,
        first_low,
        hidden_low,
        context_tok,
        attended_grad,
        vector_grads,
    )
    rest_state = (kept, place.sibling(sent))

    def head_backward(head, table):
        found = attend_backward(table, queries, probs, context_grads, pieces, head)
        return found[:4], found[4:]

    def halo(found):
        own_grad, next_grad, prev_grad, _ = found
        return own_grad, place.to_next(next_grad), place.to_previous(prev_grad)

    rest_parts = scatter_across(place, *rest_state)
    table = after(slots, rest_parts)
    rest_parts = exchange(rest_parts, CHIPS)
    results, halos = [], []
    results.append(head_backward(0, table))
    halos.append(halo(results[0][1]))
    table = after(table, results[0][1][3])
    results.append(head_backward(1, table))
    halos.append(halo(results[1][1]))

    def ring_slabs(grads):
        low = grads.astype(BF16)
        total = grads
        for k in range(1, slabs):
            total = total + place.along_slabs(low, k).astype(F32)
        return total

    ring_sum = ring_slabs(jnp.concatenate([results[0][1][3], results[1][1][3]], -1))
    table, _, *first = lax.optimization_barrier((table, results[1][1][3], *halos[0][1:]))
    halos[0] = (halos[0][0], *first)
    dqs, found = head_backward(2, table)
    ring_sum, first, second, *found = lax.optimization_barrier((ring_sum, *halos[1][1:], *found))
    halos[1] = (halos[1][0], first, second)
    results.append((dqs, found))
    halos.append(halo(found))
    rest_last = scatter_slabs(after(rest_parts, found[3]))
    ring_sum = jnp.concatenate([ring_sum, ring_slabs(results[2][1][3])], -1)
    ring_sum = ring_sum + place.sibling(ring_sum.astype(BF16)).astype(F32)
    global_at = jnp.where(
        global_blocks // 32 == half, local_block(place, global_blocks % 32), -100
    ).astype(jnp.int32)

    global_at = after(global_at, rest_last)
    rest_last = exchange(rest_last, "slab")
    heads_late, bias_late, part2, part3 = heads_backward(
        place, results, halos, ring_sum, global_at, w_heads, 1
    )
    heads_early, bias_early, part0, part1 = heads_backward(
        place, results, halos, ring_sum, after(global_at, part3), w_heads, 0
    )
    returned = [place.to_tokens(part, *pair) for part, pair in zip((part0, part1, part2, part3), PAIRS)]
    kept, arrived = heads_weight_grads(
        place, token_rows, (heads_early, heads_late), (bias_early, bias_late)
    )
    kept, arrived, returned[2], returned[3] = lax.optimization_barrier(
        (kept, arrived, returned[2], returned[3])
    )
    group_parts = scatter_group(place, kept, arrived, returned)
    tokens_grad = first_grad
    for part in returned:
        tokens_grad = tokens_grad + part.astype(F32)
    query_all, key_all, value_all, query_sum, value_sum = finish_heads(place, group_parts, share, scale)
    start = share * (place.h * 4 * slabs + 4 * place.n + 2 * place.x + place.c)
    query_bias_share = lax.dynamic_slice_in_dim(query_sum[0], start, share)
    value_bias_share = lax.dynamic_slice_in_dim(value_sum[0], start, share)
    rest_share = jnp.sum(rest_last.astype(F32), 0)
    up_share = jnp.concatenate([rest_share[i * share : (i + 1) * share] for i in range(4)], 1)
    down_share = rest_share[4 * share : 8 * share]
    output_share = rest_share[8 * share : 9 * share]
    pieces_of = [rest_share[9 * share + i, :share] for i in range(6)]

    return (
        result.astype(BF16),
        tokens_grad,
        query_all,
        query_bias_share,
        key_all,
        value_all,
        value_bias_share,
        output_share,
        pieces_of[0],
        pieces_of[1],
        pieces_of[2],
        up_share,
        rest_share[9 * share + 6, : 4 * share],
        down_share,
        pieces_of[3],
        pieces_of[4],
        pieces_of[5],
    )


def solution(mesh):
    devices = mesh.devices
    mesh = Mesh(devices.reshape(devices.shape[0], -1, 2, 2), AXES)
    rows = P(AXES, None)
    vector = P(AXES)
    tokens = P(("slab", "x", "core", "head"), None)
    return jax.shard_map(
        body,
        mesh=mesh,
        in_specs=(
            tokens,
            tokens,
            P(),
            P(),
            P("head", ("slab", "x", "core"), None),
            rows,
            vector,
            rows,
            rows,
            vector,
            rows,
            vector,
            vector,
            vector,
            rows,
            vector,
            rows,
            vector,
            vector,
            vector,
        ),
        out_specs=(
            tokens,
            tokens,
            rows,
            vector,
            rows,
            rows,
            vector,
            rows,
            vector,
            vector,
            vector,
            rows,
            vector,
            rows,
            vector,
            vector,
            vector,
        ),
        check_vma=False,
    )
```

```python
from functools import partial

import jax
import jax.numpy as jnp
from jax import lax
from jax.experimental import pallas as pl
from jax.experimental.pallas import tpu as pltpu
from jax.sharding import Mesh
from jax.sharding import PartitionSpec as P

HEAD_DIM = 64
BLOCK = 64
LANES = 128
NORM_EPS = 1e-06
MASKED = -1e30
AXES = ("head", "slab", "x", "core")
CHIPS = ("head", "x")
BF16 = jnp.bfloat16
F32 = jnp.float32
PAIRS = ((0, 0), (0, 1), (1, 0), (1, 1))
VMEM_LIMIT = 60 * 1024 * 1024


def matmul(left, right):
    return jnp.dot(left, right, preferred_element_type=F32)


def dot_rows(left, right):
    return lax.dot_general(left, right, (((0,), (0,)), ((), ())), preferred_element_type=F32)


def dot_lanes(left, right):
    return lax.dot_general(left, right, (((1,), (1,)), ((), ())), preferred_element_type=F32)


class Place:
    def __init__(self):
        self.slabs = lax.axis_size("slab")
        self.size = 4 * self.slabs
        self.h, self.n, self.x, self.c = (lax.axis_index(axis) for axis in AXES)

    def send(self, value, target):
        def index(h, n, x, c):
            return h * self.size + 4 * n + 2 * x + c

        route = [
            (index(h, n, x, c), index(*target(h, n, x, c)))
            for h in range(2)
            for n in range(self.slabs)
            for x in range(2)
            for c in range(2)
        ]
        return lax.ppermute(value, AXES, route)

    def along_slabs(self, value, k):
        return self.send(value, lambda h, n, x, c: (h, n ^ k, x, c))

    def across(self, value, i, j):
        return self.send(value, lambda h, n, x, c: (h ^ i, n, x ^ j, c))

    def sibling(self, value):
        return self.send(value, lambda h, n, x, c: (h, n, x, 1 - c))

    def to_heads(self, value, i, j):
        return self.send(value, lambda h, n, x, c: (h ^ i, n, c ^ j, x))

    def to_tokens(self, value, i, j):
        return self.send(value, lambda h, n, x, c: (h ^ i, n, c, x ^ j))

    def to_next(self, value):
        def target(h, n, x, c):
            return (h, n, x, 1) if c == 0 else (h, (n + 1) % self.slabs, x, 0)

        return self.send(value, target)

    def to_previous(self, value):
        def target(h, n, x, c):
            return (h, n, x, 0) if c == 1 else (h, (n - 1) % self.slabs, x, 1)

        return self.send(value, target)


def exchange(value, axes):
    return lax.all_to_all(value, axes, split_axis=0, concat_axis=0, tiled=True)


def pick(value, index, axis=0):
    return lax.dynamic_index_in_dim(value, index, axis, keepdims=False)


def kernel_call(kernel, out_shape, name, flops=1000, **options):
    return pl.pallas_call(
        kernel,
        out_shape=out_shape,
        compiler_params=pltpu.CompilerParams(vmem_limit_bytes=VMEM_LIMIT),
        cost_estimate=pl.CostEstimate(
            flops=flops, bytes_accessed=1000, transcendentals=0
        ),
        name=name,
        **options,
    )


def whole(count):
    return [pl.BlockSpec(memory_space=pltpu.VMEM)] * count


def smem():
    return pl.BlockSpec(memory_space=pltpu.SMEM)


def after(value, *others):
    return lax.optimization_barrier((value,) + others)[0]


def side_of(head):
    return 1 - head % 2


def half_tile(value, start, side):
    tile = start // LANES * LANES
    found = value[:, tile : tile + LANES].astype(F32)
    if (start % LANES) // HEAD_DIM != side:
        found = pltpu.roll(found, HEAD_DIM, 1)
    return found


def left_lanes(rows):
    return lax.broadcasted_iota(jnp.int32, (rows, LANES), 1) < HEAD_DIM


def pack_heads(query_weight, key_weight, value_weight, biases, scale):
    share = query_weight.shape[0]

    def kernel(q_ref, k_ref, v_ref, b_ref, out_ref):
        left = left_lanes(share)
        for group in range(4):
            start = 3 * group * HEAD_DIM
            q = [half_tile(q_ref, start + t * HEAD_DIM, side_of(t)) * scale for t in range(3)]
            out_ref[group, :, :LANES] = jnp.where(left, q[1], q[0]).astype(BF16)
            extra = b_ref[...].astype(F32)
            out_ref[group, :, LANES : 2 * LANES] = jnp.where(left, extra, q[2]).astype(BF16)
            for t in range(3):
                side = side_of(t)
                k = half_tile(k_ref, start + t * HEAD_DIM, side)
                v = half_tile(v_ref, start + t * HEAD_DIM, 1 - side)
                both = jnp.where(left, k, v) if side == 0 else jnp.where(left, v, k)
                out_ref[group, :, (2 + t) * LANES : (3 + t) * LANES] = both.astype(BF16)

    return kernel_call(
        kernel,
        jax.ShapeDtypeStruct((4, share, 5 * LANES), BF16),
        "pack_heads",
        in_specs=whole(4),
        out_specs=whole(1)[0],
    )(query_weight, key_weight, value_weight, biases)


def pack_rest(up, down, output, vectors):
    share, width = output.shape
    height = -(-(9 * share + 8) // 16) * 16
    count = len(vectors)

    def kernel(up_ref, down_ref, output_ref, *refs):
        out_ref = refs[-1]
        for i in range(4):
            out_ref[i * share : (i + 1) * share] = up_ref[:, i * width : (i + 1) * width]
        out_ref[4 * share : 8 * share] = down_ref[...]
        out_ref[8 * share : 9 * share] = output_ref[...]
        row = lax.broadcasted_iota(jnp.int32, (height - 9 * share, LANES), 0)
        total = jnp.zeros(row.shape, F32)
        for i, ref in enumerate(refs[:count]):
            total = jnp.where(row == i, jnp.broadcast_to(ref[...].astype(F32), row.shape), total)
        out_ref[9 * share :, :LANES] = total.astype(BF16)
        out_ref[9 * share :, LANES:] = jnp.zeros((height - 9 * share, width - LANES), BF16)

    vectors = [jnp.pad(v, (0, LANES - v.shape[0]))[None] for v in vectors]
    return kernel_call(
        kernel,
        jax.ShapeDtypeStruct((height, width), BF16),
        "pack_rest",
        in_specs=whole(3 + count),
        out_specs=whole(1)[0],
    )(up, down, output, *vectors)


def stack_heads(parts):
    def kernel(*refs):
        for k, ref in enumerate(refs[:-1]):
            refs[-1][k] = ref[...]

    return kernel_call(
        kernel,
        jax.ShapeDtypeStruct((len(parts),) + parts[0].shape, BF16),
        "stack_heads",
        in_specs=whole(len(parts)),
        out_specs=whole(1)[0],
    )(*parts)


def assemble_heads(place, column, other):
    slabs, _, rows, columns = column.shape
    where = jnp.stack([place.h, place.n, place.x, place.c]).astype(jnp.int32)

    def kernel(where_ref, mine_ref, other_ref, out_ref, bias_ref):
        h, x, c = where_ref[0], where_ref[2], where_ref[3]
        left = left_lanes(rows)
        right = jnp.logical_not(left)
        for core, ref in enumerate((mine_ref, other_ref)):
            for p, (i, j) in enumerate(PAIRS):
                first = ref[0, p, :, :LANES].astype(F32)
                second = ref[0, p, :, LANES : 2 * LANES]
                q = (
                    jnp.where(right, first, 0.0),
                    jnp.where(left, first, 0.0),
                    jnp.where(right, second.astype(F32), 0.0),
                )
                at = (h ^ i, 0, x ^ j, c ^ core)
                for t in range(3):
                    out_ref[(*at, slice(None), slice(t * LANES, (t + 1) * LANES))] = q[t].astype(BF16)
                out_ref[(*at, slice(None), slice(3 * LANES, 6 * LANES))] = ref[0, p, :, 2 * LANES :]
                bias_ref[at] = second

    found = kernel_call(
        kernel,
        (
            jax.ShapeDtypeStruct((2, slabs, 2, 2, rows, 6 * LANES), BF16),
            jax.ShapeDtypeStruct((2, slabs, 2, 2, rows, LANES), BF16),
        ),
        "assemble_heads",
        grid_spec=pltpu.PrefetchScalarGridSpec(
            num_scalar_prefetch=1,
            grid=(slabs,),
            in_specs=[pl.BlockSpec((1, 4, rows, columns), lambda k, w: (k, 0, 0, 0))] * 2,
            out_specs=[
                pl.BlockSpec((2, 1, 2, 2, rows, 6 * LANES), lambda k, w: (0, k ^ w[1], 0, 0, 0, 0)),
                pl.BlockSpec((2, 1, 2, 2, rows, LANES), lambda k, w: (0, k ^ w[1], 0, 0, 0, 0)),
            ],
        ),
    )(where, column, other)
    return [value.reshape(8 * slabs, *value.shape[4:]) for value in found]


def assemble_rest(place, mine, other, share):
    _, slabs, rows, width = mine.shape
    where = place.c.reshape(1).astype(jnp.int32)

    def kernel(where_ref, mine_ref, other_ref, up_ref, down_ref, output_ref, vector_ref):
        for core, ref in ((where_ref[0], mine_ref), (1 - where_ref[0], other_ref)):
            for p in range(4):
                at = (p // 2, 0, p % 2, core)
                for q in range(4):
                    columns = slice(q * width, (q + 1) * width)
                    up_ref[(*at, slice(None), columns)] = ref[p, 0, q * share : (q + 1) * share]
                down_ref[at] = ref[p, 0, 4 * share : 8 * share]
                output_ref[at] = ref[p, 0, 8 * share : 9 * share]
                vector_ref[at] = ref[p, 0, 9 * share :]

    shapes = ((share, 4 * width), (4 * share, width), (share, width), (rows - 9 * share, width))
    found = kernel_call(
        kernel,
        tuple(jax.ShapeDtypeStruct((2, slabs, 2, 2) + shape, BF16) for shape in shapes),
        "assemble_rest",
        20_000_000_000,
        grid_spec=pltpu.PrefetchScalarGridSpec(
            num_scalar_prefetch=1,
            grid=(slabs,),
            in_specs=[pl.BlockSpec((4, 1, rows, width), lambda n, w: (0, n, 0, 0))] * 2,
            out_specs=[
                pl.BlockSpec((2, 1, 2, 2) + shape, lambda n, w: (0, n, 0, 0, 0, 0)) for shape in shapes
            ],
        ),
    )(where, mine, other)
    return [value.reshape(8 * slabs, *value.shape[4:]) for value in found]


def weight_grads(place, active, branch_grad, first, hidden_grad, context, attended_grad, vectors):
    devices = 8 * place.slabs
    step = devices // 4
    tokens, width = first.shape
    share = width // devices
    rows = -(-(9 * share + 8) // 16) * 16
    where = jnp.stack([place.h * 2 + place.c, place.c]).astype(jnp.int32)

    def kernel(where_ref, active_ref, branch_ref, first_ref, hidden_ref, context_ref, attended_ref, vector_ref, kept_ref, sent_ref):
        even = where_ref[1] == 0

        def put(start, stop, value):
            value = value.astype(BF16).reshape(step, stop - start, width)
            for p in range(step // 2):
                kept_ref[p, start:stop] = jnp.where(even, value[2 * p], value[2 * p + 1])
                sent_ref[p, start:stop] = jnp.where(even, value[2 * p + 1], value[2 * p])

        put(4 * share, 8 * share, dot_rows(active_ref[...], branch_ref[...]))
        columns = first_ref[...]
        for q in range(4):
            up = dot_rows(columns, hidden_ref[:, q * width : (q + 1) * width])
            put(q * share, (q + 1) * share, up[: step * share])
        put(8 * share, 9 * share, dot_rows(context_ref[...], attended_ref[...])[: step * share])
        for p in range(step // 2):
            for ref, at in ((kept_ref, 2 * p + where_ref[1]), (sent_ref, 2 * p + 1 - where_ref[1])):
                ref[p, 9 * share :] = jnp.zeros((rows - 9 * share, width), BF16)
                ref[p, 9 * share : 9 * share + 8, :LANES] = vector_ref[at].astype(BF16)

    first = jnp.pad(first.reshape(tokens, 4, 192), ((0, 0), (0, 0), (0, 64))).reshape(tokens, 1024)
    half = jax.ShapeDtypeStruct((devices // 2, rows, width), BF16)
    return kernel_call(
        kernel,
        (half, half),
        "weight_grads",
        15_000_000_000,
        grid_spec=pltpu.PrefetchScalarGridSpec(
            num_scalar_prefetch=1,
            grid=(4,),
            in_specs=[
                pl.BlockSpec((tokens, width), lambda g, w: (0, g)),
                pl.BlockSpec((tokens, width), lambda g, w: (0, 0)),
                pl.BlockSpec((tokens, 256), lambda g, w: (0, g)),
                pl.BlockSpec((tokens, 4 * width), lambda g, w: (0, 0)),
                pl.BlockSpec((tokens, 256), lambda g, w: (0, g ^ w[0])),
                pl.BlockSpec((tokens, width), lambda g, w: (0, 0)),
                pl.BlockSpec((step, 8, LANES), lambda g, w: (g, 0, 0)),
            ],
            out_specs=[pl.BlockSpec((step // 2, rows, width), lambda g, w: (g, 0, 0))] * 2,
        ),
    )(where, active, branch_grad, first, hidden_grad, context, attended_grad, vectors)


def heads_weight_grads(place, token_parts, heads_grads, bias_grad):
    slabs = place.slabs
    width = token_parts[0].shape[1]
    share = width // (8 * slabs)
    rows = max(share, 8)
    where = place.c.reshape(1).astype(jnp.int32)

    def kernel(where_ref, *refs):
        x_refs, g_refs, bias_ref, kept_ref, sent_ref = refs[:4], refs[4:8], *refs[8:]
        even = where_ref[0] == 0
        left = left_lanes(rows)
        row = lax.broadcasted_iota(jnp.int32, (rows, LANES), 0)
        extra = jnp.zeros((rows, LANES), F32)
        for which in range(6):
            head = which % 3
            if which < 3:
                start = head * LANES + side_of(head) * HEAD_DIM
            else:
                start = (3 + head) * LANES + (1 - side_of(head)) * HEAD_DIM
            value = jnp.broadcast_to(half_tile(bias_ref, start, 0)[0:1], (rows, LANES))
            extra = jnp.where(row == which, value, extra)

        def put(start, stop, value):
            value = value.astype(BF16).reshape(8 * slabs, share, stop - start)
            if rows > share:
                value = jnp.concatenate(
                    [value, jnp.zeros((8 * slabs, rows - share, stop - start), BF16)], 1
                )
            for p in range(4 * slabs):
                first, second = value[2 * p], value[2 * p + 1]
                if start == LANES:
                    first = jnp.where(left, extra, first.astype(F32)).astype(BF16)
                    second = jnp.where(left, extra, second.astype(F32)).astype(BF16)
                kept_ref[p, :, start:stop] = jnp.where(even, first, second)
                sent_ref[p, :, start:stop] = jnp.where(even, second, first)

        def product(start, stop):
            return sum(
                dot_rows(x_ref[...], g_ref[:, start:stop]) for x_ref, g_ref in zip(x_refs, g_refs)
            )

        q = product(0, 3 * LANES)
        put(0, LANES, q[:, :LANES] + q[:, LANES : 2 * LANES])
        put(LANES, 2 * LANES, q[:, 2 * LANES :])
        put(2 * LANES, 5 * LANES, product(3 * LANES, 6 * LANES))

    half = jax.ShapeDtypeStruct((4 * slabs, rows, 5 * LANES), BF16)
    return kernel_call(
        kernel,
        (half, half),
        "heads_weight_grads",
        in_specs=[smem()] + whole(9),
        out_specs=whole(2),
    )(where, *token_parts, *heads_grads, bias_grad)


def scatter_across(place, kept, arrived):
    slabs = place.slabs
    _, rows, width = kept.shape

    def kernel(kept_ref, arrived_ref, out_ref):
        for h in range(2):
            for x in range(2):
                total = kept_ref[h, 0, x].astype(F32) + arrived_ref[h, 0, x].astype(F32)
                out_ref[2 * h + x, 0] = total.astype(BF16)

    parts = kernel_call(
        kernel,
        jax.ShapeDtypeStruct((4, slabs, rows, width), BF16),
        "scatter_across",
        grid=(slabs,),
        in_specs=[pl.BlockSpec((2, 1, 2, rows, width), lambda n: (0, n, 0, 0, 0))] * 2,
        out_specs=pl.BlockSpec((4, 1, rows, width), lambda n: (0, n, 0, 0)),
    )(*(value.reshape(2, slabs, 2, rows, width) for value in (kept, arrived)))
    return parts


def scatter_slabs(parts):
    slabs, rows, width = parts.shape[1:]

    def kernel(ref, out_ref):
        out_ref[0] = sum(ref[p, 0].astype(F32) for p in range(4)).astype(BF16)

    total = kernel_call(
        kernel,
        jax.ShapeDtypeStruct((slabs, rows, width), BF16),
        "scatter_slabs",
        20_000_000_000,
        grid=(slabs,),
        in_specs=[pl.BlockSpec((4, 1, rows, width), lambda n: (0, n, 0, 0))],
        out_specs=pl.BlockSpec((1, rows, width), lambda n: (n, 0, 0)),
    )(parts)
    return total


def added(parts):
    return sum(part.astype(F32) for part in parts)


def group_along(place, kept, arrived):
    slabs = place.slabs
    _, rows, width = kept.shape

    def kernel(kept_ref, arrived_ref, out_ref):
        for h in range(2):
            for n in range(slabs):
                for x in range(2):
                    pair = kept_ref[h, n, x].astype(F32) + arrived_ref[h, n, x].astype(F32)
                    out_ref[n, 2 * h + x] = pair.astype(BF16)

    parts = kernel_call(
        kernel,
        jax.ShapeDtypeStruct((slabs, 4, rows, width), BF16),
        "group_along",
        in_specs=whole(2),
        out_specs=whole(1)[0],
    )(*(value.reshape(2, slabs, 2, rows, width) for value in (kept, arrived)))
    return exchange(parts, "slab")


def group_across(parts):
    slabs, _, rows, width = parts.shape

    def kernel(ref, out_ref):
        for p in range(4):
            out_ref[p] = sum(ref[n, p].astype(F32) for n in range(slabs)).astype(BF16)

    total = kernel_call(
        kernel,
        jax.ShapeDtypeStruct((4, rows, width), BF16),
        "group_across",
        in_specs=whole(1),
        out_specs=whole(1)[0],
    )(parts)
    return exchange(total, CHIPS)


def finish_heads(parts, share, scale):
    _, rows, _ = parts.shape
    width = 12 * HEAD_DIM

    def kernel(ref, q_ref, k_ref, v_ref, bias_ref):
        left = left_lanes(rows)
        bias_ref[...] = jnp.zeros(bias_ref.shape, F32)
        for which, out in enumerate((q_ref, k_ref, v_ref)):
            for tile in range(width // LANES):
                sides, sums = [], []
                for side in range(2):
                    head = 2 * tile + side
                    value = ref[head // 3]
                    t = head % 3
                    if which == 0:
                        start = (t // 2) * LANES + side_of(t) * HEAD_DIM
                    else:
                        at = side_of(t) if which == 1 else 1 - side_of(t)
                        start = (2 + t) * LANES + at * HEAD_DIM
                    sides.append(half_tile(value, start, side))
                    row = t if which == 0 else 3 + t
                    sums.append(half_tile(value, LANES, side)[row : row + 1])
                value = jnp.where(left, sides[0], sides[1])
                bias = jnp.where(left[0:1], sums[0], sums[1])
                if which == 0:
                    value, bias = value * scale, bias * scale
                lanes = slice(tile * LANES, (tile + 1) * LANES)
                out[:, lanes] = value[:share]
                if which != 1:
                    bias_ref[which // 2 : which // 2 + 1, lanes] = bias

    weight = jax.ShapeDtypeStruct((share, width), F32)
    return kernel_call(
        kernel,
        (weight, weight, weight, jax.ShapeDtypeStruct((8, width), F32)),
        "finish_heads",
        in_specs=whole(1),
        out_specs=whole(4),
    )(parts)


def join_heads(results, halos, ring_sum, global_at):
    dqs = [results[head][0][u] for u in range(4) for head in range(3)]
    owns = [halos[head][0] for head in range(3)]
    arrived = [halos[head][side] for head in range(3) for side in (1, 2)]
    rows, width = 8 * BLOCK, 6 * LANES

    def kernel(at_ref, *refs):
        dq_refs, own_refs, arrived_refs, ring_ref = refs[:12], refs[12:15], refs[15:21], refs[21]
        out_refs, bias_ref = refs[22:26], refs[26]

        def total(head, blocks):
            return (
                own_refs[head][blocks]
                + arrived_refs[2 * head][blocks].astype(F32)
                + arrived_refs[2 * head + 1][blocks].astype(F32)
            )

        bias = jnp.zeros((8, width), F32)
        for u in range(4):
            out = out_refs[u]
            for head in range(3):
                out[:, head * LANES : (head + 1) * LANES] = dq_refs[3 * u + head][...]
                lanes = slice((3 + head) * LANES, (4 + head) * LANES)
                value = total(head, slice(u * 8, (u + 1) * 8))
                out[:, lanes] = value.reshape(rows, LANES).astype(BF16)
            for which in range(2):
                at = at_ref[which] - 8 * u

                @pl.when((at >= 0) & (at < 8))
                def _():
                    block = jnp.clip(at, 0, 7)
                    row = pl.ds(pl.multiple_of(block * BLOCK, BLOCK), BLOCK)
                    for head in range(3):
                        lanes = slice(head * LANES, (head + 1) * LANES)
                        value = total(head, 8 * u + block)
                        for i in range(2):
                            same = at_ref[i] == at_ref[which]
                            value = value + jnp.where(same, ring_ref[i, :, lanes], 0.0)
                        out[row, (3 + head) * LANES : (4 + head) * LANES] = value.astype(BF16)

            bias = bias + matmul(jnp.ones((8, rows), BF16), out[...])
        bias_ref[...] = bias

    return kernel_call(
        kernel,
        [jax.ShapeDtypeStruct((rows, width), BF16)] * 4 + [jax.ShapeDtypeStruct((8, width), F32)],
        "join_heads",
        in_specs=[smem()] + whole(22),
        out_specs=whole(5),
    )(global_at, *dqs, *owns, *arrived, ring_sum)


def copy_all(sources, target, sems):
    copies = []
    start = 0
    for which, source in enumerate(sources):
        stop = start + source.shape[0]
        copies.append(pltpu.make_async_copy(source, target.at[start:stop], sems.at[which]))
        start = stop
    for copy in copies:
        copy.start()
    return copies


def shard_rows(column=0):
    return [pl.BlockSpec((BLOCK, LANES), lambda i, *_, u=u: (8 * u + i, column)) for u in range(4)]


def attend_forward(slots, query_doc, key_doc, queries, pieces, head, context=None):
    blocks = 32
    joined = 0 if context is None else 4
    columns = LANES if head < 2 else 2 * LANES

    def kernel(slots_ref, *refs):
        doc_refs, key_refs, q_refs = refs[:4], refs[4:8], refs[8:12]
        before = refs[12 : 12 + joined]
        sources = refs[12 + joined : 16 + joined]
        ctx_refs, p_refs = refs[16 + joined : 20 + joined], refs[20 + joined : 24 + joined]
        kv, sems = refs[24 + joined :]
        step = pl.program_id(0)

        @pl.when(step == 0)
        def _():
            for copy in copy_all(sources, kv, sems):
                copy.wait()

        left = lax.broadcasted_iota(jnp.int32, (1, LANES), 1) < BLOCK
        values = left if head % 2 == 0 else jnp.logical_not(left)
        slot, score = [], []
        for u in range(4):
            base = (head * blocks + u * 8 + step) * 8
            slot.append(jnp.concatenate([kv[slots_ref[base + s]] for s in range(8)], 0))
            score.append(dot_lanes(q_refs[u][...], slot[u]))
        low = []
        for u in range(4):
            query = doc_refs[u][...]
            tiles = []
            for tile in range(4):
                lanes = slice(tile * LANES, (tile + 1) * LANES)
                tiles.append(jnp.where(query == key_refs[u][0, :, lanes], score[u][:, lanes], MASKED))
            top = jnp.maximum(jnp.maximum(tiles[0], tiles[1]), jnp.maximum(tiles[2], tiles[3]))
            top = jnp.max(top, -1, keepdims=True)
            tiles = [jnp.exp(tile - top) for tile in tiles]
            total = (tiles[0] + tiles[1]) + (tiles[2] + tiles[3])
            inverse = 1.0 / jnp.sum(total, -1, keepdims=True)
            low.append(jnp.concatenate([(tile * inverse).astype(BF16) for tile in tiles], 1))
            p_refs[u][0] = low[u]
        for u in range(4):
            result = jnp.where(values, matmul(low[u], slot[u]), 0.0)
            if head == 1:
                result = jnp.where(values, result, before[u][...].astype(F32))
            if head == 2:
                ctx_refs[u][:, :LANES] = before[u][...]
            ctx_refs[u][:, columns - LANES :] = result.astype(BF16)

    return pl.pallas_call(
        kernel,
        out_shape=[jax.ShapeDtypeStruct((8 * BLOCK, columns), BF16)] * 4
        + [jax.ShapeDtypeStruct((8, BLOCK, 8 * BLOCK), BF16)] * 4,
        grid_spec=pltpu.PrefetchScalarGridSpec(
            num_scalar_prefetch=1,
            grid=(8,),
            in_specs=shard_rows()
            + [
                pl.BlockSpec((1, 1, 8 * BLOCK), lambda i, *_, u=u: (head * 32 + 8 * u + i, 0, 0))
                for u in range(4)
            ]
            + shard_rows()
            + [pl.BlockSpec((BLOCK, LANES), lambda i, *_: (i, 0))] * joined
            + [pl.BlockSpec(memory_space=pl.ANY)] * 4,
            out_specs=[pl.BlockSpec((BLOCK, columns), lambda i, *_: (i, 0))] * 4
            + [pl.BlockSpec((1, BLOCK, 8 * BLOCK), lambda i, *_: (i, 0, 0))] * 4,
            scratch_shapes=[
                pltpu.VMEM((3 * blocks + 2, BLOCK, LANES), BF16),
                pltpu.SemaphoreType.DMA((4,)),
            ],
        ),
        compiler_params=pltpu.CompilerParams(vmem_limit_bytes=VMEM_LIMIT),
        cost_estimate=pl.CostEstimate(
            flops=1_000_000_000, bytes_accessed=1000, transcendentals=0
        ),
        name="attend_forward",
    )(slots, *[query_doc] * 4, *[key_doc] * 4, *[queries] * 4, *(context or ()), *pieces)


def attend_backward(slots, queries, probs, grads, pieces, head):
    blocks = 32

    def kernel(slots_ref, *refs):
        q_refs, p_refs, grad_refs = refs[:4], refs[4:8], refs[8:12]
        sources = refs[12:16]
        dq_refs = refs[16:20]
        own_ref, next_ref, prev_ref, glob_ref, kv, acc, sems = refs[20:]
        step = pl.program_id(0)

        @pl.when(step == 0)
        def _():
            copies = copy_all(sources, kv, sems)

            def clear(i, _):
                acc[i] = jnp.zeros(acc.shape[1:], F32)
                return _

            lax.fori_loop(0, acc.shape[0], clear, 0)
            for copy in copies:
                copy.wait()

        left = lax.broadcasted_iota(jnp.int32, (1, LANES), 1) < BLOCK
        values = left if head % 2 == 0 else jnp.logical_not(left)
        slot, grad, prob_grad, score_grad = [], [], [], []
        for u in range(4):
            base = (head * blocks + u * 8 + step) * 8
            slot.append(jnp.concatenate([kv[slots_ref[base + s]] for s in range(8)], 0))
            grad.append(jnp.where(values, grad_refs[u][...].astype(F32), 0.0).astype(BF16))
            prob_grad.append(dot_lanes(grad[u], slot[u]))
        for u in range(4):
            probs_f = p_refs[u][0].astype(F32)
            both = probs_f * prob_grad[u]
            inner = jnp.sum(both, -1, keepdims=True)
            score_grad.append((both - probs_f * inner).astype(BF16))
        for u in range(4):
            dq = matmul(score_grad[u], slot[u])
            dq_refs[u][...] = jnp.where(values, 0.0, dq).astype(BF16)
        slot_grad = [
            dot_rows(
                jnp.concatenate([score_grad[u], p_refs[u][0]], 0),
                jnp.concatenate([q_refs[u][...], grad[u]], 0),
            )
            for u in range(4)
        ]
        for u in range(4):
            base = (head * blocks + u * 8 + step) * 8
            for s in range(8):
                where = slots_ref[base + s]
                acc[where] += slot_grad[u][s * BLOCK : (s + 1) * BLOCK]

        @pl.when(step == 7)
        def _():
            def finish(i, _):
                own_ref[i] = acc[i]
                next_ref[i] = acc[blocks + i].astype(BF16)
                prev_ref[i] = acc[2 * blocks + i].astype(BF16)
                return _

            lax.fori_loop(0, blocks, finish, 0)
            glob_ref[...] = acc[3 * blocks :]

    shape = (blocks, BLOCK, LANES)
    full = pl.BlockSpec(shape, lambda i, *_: (0, 0, 0))
    return pl.pallas_call(
        kernel,
        out_shape=[jax.ShapeDtypeStruct((8 * BLOCK, LANES), BF16)] * 4
        + [
            jax.ShapeDtypeStruct(shape, F32),
            jax.ShapeDtypeStruct(shape, BF16),
            jax.ShapeDtypeStruct(shape, BF16),
            jax.ShapeDtypeStruct((2,) + shape[1:], F32),
        ],
        grid_spec=pltpu.PrefetchScalarGridSpec(
            num_scalar_prefetch=1,
            grid=(8,),
            in_specs=shard_rows()
            + [pl.BlockSpec((1, BLOCK, 8 * BLOCK), lambda i, *_: (i, 0, 0))] * 4
            + [pl.BlockSpec((BLOCK, LANES), lambda i, *_: (i, head // 2))] * 4
            + [pl.BlockSpec(memory_space=pl.ANY)] * 4,
            out_specs=[pl.BlockSpec((BLOCK, LANES), lambda i, *_: (i, 0))] * 4
            + [full, full, full, pl.BlockSpec((2,) + shape[1:], lambda i, *_: (0, 0, 0))],
            scratch_shapes=[
                pltpu.VMEM((3 * blocks + 2,) + shape[1:], BF16),
                pltpu.VMEM((3 * blocks + 2,) + shape[1:], F32),
                pltpu.SemaphoreType.DMA((4,)),
            ],
        ),
        compiler_params=pltpu.CompilerParams(vmem_limit_bytes=VMEM_LIMIT),
        cost_estimate=pl.CostEstimate(
            flops=18_000_000_000, bytes_accessed=1000, transcendentals=0
        ),
        name="attend_backward",
    )(slots, *[queries] * 4, *probs, *grads, *pieces)


def project_heads(token_parts, w_heads, biases, group, shown_at, scale):
    width = w_heads.shape[0]
    rows = token_parts[0].shape[0]
    biases = biases.reshape(4, 192, LANES)

    def kernel(group_ref, at_ref, *refs):
        parts, (w_ref, b_ref) = refs[:4], refs[4:6]
        q_refs, kv_refs, shown_ref = refs[6:9], refs[9:12], refs[12]
        row = lax.broadcasted_iota(jnp.int32, (8, LANES), 0)
        lane = lax.broadcasted_iota(jnp.int32, (8, LANES), 1)
        select = jnp.where(row == lane, 1.0, 0.0).astype(BF16)
        column = jnp.concatenate([b_ref[0], jnp.zeros((64, LANES), BF16)], 0)
        vectors = dot_lanes(select, column)
        left = left_lanes(8)
        for part, ref in enumerate(parts):
            value = matmul(ref[...], w_ref[...])
            for head in range(3):
                side = side_of(head)
                q = half_tile(vectors, head * HEAD_DIM, side)[0:1] * scale
                v = half_tile(vectors, head * HEAD_DIM, 1 - side)[1:2]
                first = left[0:1] if side == 0 else jnp.logical_not(left[0:1])
                q = jnp.where(first, q, 0.0)
                v = jnp.where(first, 0.0, v)
                lanes = slice(head * LANES, (head + 1) * LANES)
                q_refs[head][part * rows : (part + 1) * rows] = (value[:, lanes] + q).astype(BF16)
                lanes = slice((3 + head) * LANES, (4 + head) * LANES)
                kv = (value[:, lanes] + v).astype(BF16).reshape(8, BLOCK, LANES)
                kv_refs[head][part * 8 : (part + 1) * 8] = kv
        for which in range(2):
            at = at_ref[which]
            for head in range(3):
                found = kv_refs[head][jnp.maximum(at, 0)]
                lanes = slice(head * LANES, (head + 1) * LANES)
                shown_ref[which, :, lanes] = jnp.where(at >= 0, found.astype(F32), 0.0).astype(BF16)

    return kernel_call(
        kernel,
        [jax.ShapeDtypeStruct((4 * rows, LANES), BF16)] * 3
        + [jax.ShapeDtypeStruct((32, BLOCK, LANES), BF16)] * 3
        + [jax.ShapeDtypeStruct((2, BLOCK, 3 * LANES), BF16)],
        "project_heads",
        grid_spec=pltpu.PrefetchScalarGridSpec(
            num_scalar_prefetch=2,
            grid=(1,),
            in_specs=[pl.BlockSpec((rows, width), lambda i, *_: (0, 0))] * 4
            + [
                pl.BlockSpec((width, width), lambda i, *_: (0, 0)),
                pl.BlockSpec((1, 192, LANES), lambda i, g, *_: (g[0], 0, 0)),
            ],
            out_specs=[pl.BlockSpec((4 * rows, LANES), lambda i, *_: (0, 0))] * 3
            + [pl.BlockSpec((32, BLOCK, LANES), lambda i, *_: (0, 0, 0))] * 3
            + [pl.BlockSpec((2, BLOCK, 3 * LANES), lambda i, *_: (0, 0, 0))],
        ),
    )(group.reshape(1).astype(jnp.int32), shown_at, *token_parts, w_heads, biases)


def norm_forward(value, gain, shift):
    center = value - jnp.mean(value, -1, keepdims=True)
    spread = jnp.mean(center * center, -1, keepdims=True)
    scale_row = lax.rsqrt(spread + NORM_EPS)
    normal = center * scale_row
    return (normal * gain + shift, normal, scale_row)


def norm_backward(grad, normal, scale_row, gain):
    gain_grad = jnp.sum(grad * normal, 0)
    shift_grad = jnp.sum(grad, 0)
    inner = grad * gain
    value_grad = scale_row * (
        inner
        - jnp.mean(inner, -1, keepdims=True)
        - normal * jnp.mean(inner * normal, -1, keepdims=True)
    )
    return (value_grad, gain_grad, shift_grad)


def local_block(place, within):
    shard = within // 8
    return (((shard % 2) ^ place.h) * 2 + ((shard // 2) ^ place.x)) * 8 + within % 8


def doc_number(positions, starts):
    return jnp.sum((positions[..., None] >= starts).astype(jnp.int32), -1)


def slot_tables(place, global_blocks, random_parts, starts):
    ring = 2 * place.slabs
    half = 2 * place.n + place.c
    total = ring * 32
    found = []
    for arrived in random_parts:
        found.append(lax.dynamic_slice_in_dim(arrived, 3 * place.x, 3, 0).reshape(3, 2, 8, 3))
    chosen = jnp.stack(found, 2)
    chosen = jnp.where(place.h == 0, chosen, chosen[:, ::-1]).reshape(3, 32, 3)
    order = jnp.arange(32, dtype=jnp.int32)
    shard = order // 8
    query_ids = half * 32 + (((shard % 2) ^ place.x) * 2 + ((shard // 2) ^ place.h)) * 8 + order % 8
    near = (query_ids[:, None] + jnp.arange(-1, 2, dtype=jnp.int32)) % total
    ids = jnp.concatenate(
        [
            jnp.broadcast_to(near[None], (3, 32, 3)),
            jnp.broadcast_to(global_blocks, (3, 32, 2)),
            chosen,
        ],
        -1,
    )
    earlier = jnp.arange(8)[None, :] < jnp.arange(8)[:, None]
    repeated = jnp.any((ids[..., :, None] == ids[..., None, :]) & earlier, -1)
    distance = (ids // 32 - half) % ring
    region = jnp.where(distance == 0, 0, jnp.where(distance == 1, 1, 2))
    local = region * 32 + local_block(place, ids % 32)
    which = jnp.arange(8, dtype=jnp.int32)
    slots = jnp.where((which == 3) | (which == 4), 93 + which, local)
    marked = jnp.where(repeated, -1, ids)
    token = jnp.arange(BLOCK, dtype=jnp.int32)
    query_doc = doc_number(query_ids[:, None] * BLOCK + token, starts).reshape(32 * BLOCK, 1)
    key_doc = doc_number(marked[..., None] * BLOCK + token, starts)
    return (
        slots.reshape(-1).astype(jnp.int32),
        jnp.broadcast_to(query_doc, (32 * BLOCK, LANES)),
        key_doc.reshape(96, 1, 8 * BLOCK),
    )


def body(
    tokens,
    cotangent,
    doc_lengths,
    global_blocks,
    random_blocks,
    query_weight,
    query_bias,
    key_weight,
    value_weight,
    value_bias,
    output_weight,
    output_bias,
    first_gain,
    first_shift,
    up_weight,
    up_bias,
    down_weight,
    down_bias,
    second_gain,
    second_shift,
):
    place = Place()
    slabs = place.slabs
    devices = 8 * slabs
    width = tokens.shape[1]
    share = query_weight.shape[0]
    hidden_width = up_weight.shape[1]
    scale = HEAD_DIM ** (-0.5)
    group = place.h * 2 + place.x
    token_group = place.h * 2 + place.c

    biases = jnp.pad(jnp.stack([query_bias, value_bias], 1), ((0, 0), (0, LANES - 2)))
    groups = pack_heads(query_weight, key_weight, value_weight, biases, scale)
    parts = [pick(groups, group)] + [
        place.across(pick(groups, group ^ (2 * i + j)), i, j) for i, j in PAIRS[1:]
    ]
    vectors = [
        output_bias, first_gain, first_shift, down_bias, second_gain, second_shift, up_bias
    ]
    random_late = after(random_blocks, groups)
    random_parts = [place.to_heads(random_late, 0, j) for j in range(2)]
    *parts, random_parts[0], random_parts[1] = lax.optimization_barrier((*parts, *random_parts))
    stacked = stack_heads(parts)
    packed = pack_rest(after(up_weight, stacked), down_weight, output_weight, vectors)
    tokens_late = after(tokens, stacked)
    token_parts = [place.to_heads(tokens_late, i, j) for i, j in PAIRS]
    column = [stacked] + [place.along_slabs(stacked, k) for k in range(1, slabs)]
    which = jnp.arange(doc_lengths.shape[0])
    before = which[None, :] < which[:, None]
    starts = jnp.sum(jnp.where(before, doc_lengths[None, :], 0), 1).astype(jnp.int32)
    slots, query_doc, key_doc = slot_tables(place, global_blocks, random_parts, starts)
    packed, *column = lax.optimization_barrier((packed, *column))
    heads_column = jnp.stack(column)
    heads_column, slots, query_doc, key_doc, *token_parts = lax.optimization_barrier(
        (heads_column, slots, query_doc, key_doc, *token_parts)
    )
    other, *token_parts = lax.optimization_barrier((place.sibling(heads_column), *token_parts))
    arrived, bias = assemble_heads(place, heads_column, other)
    w_heads = arrived.reshape(width, width)
    packed_column = exchange(jnp.broadcast_to(packed, (slabs,) + packed.shape), "slab")
    half = 2 * place.n + place.c
    global_at = local_block(place, global_blocks % 32)
    shown_at = jnp.where(global_blocks // 32 == half, global_at, -1).astype(jnp.int32)
    found = project_heads(token_parts, w_heads, bias, group, shown_at, scale)
    queries, own, shown = found[:3], found[3:6], found[6]
    shown = shown + place.sibling(shown)
    shown, *own = lax.optimization_barrier((shown, *own))
    following = [place.to_previous(kv) for kv in own]
    previous = [place.to_next(kv) for kv in own]
    mine = pick(shown, place.c)
    for k in range(1, slabs):
        mine = mine + place.along_slabs(pick(shown, place.c), k)
    theirs = place.sibling(mine)
    shared = jnp.where(place.c == 0, jnp.stack([mine, theirs]), jnp.stack([theirs, mine]))

    packed_column = after(packed_column, own[0])
    rest_column = exchange(jnp.broadcast_to(packed_column, (4,) + packed_column.shape), CHIPS)

    pieces, probs, context, table = [], [], None, slots
    for head in range(3):
        lanes = slice(head * LANES, (head + 1) * LANES)
        pieces.append((own[head], following[head], previous[head], shared[:, :, lanes]))
        found = attend_forward(table, query_doc, key_doc, queries[head], pieces[head], head, context)
        context = found[:4]
        probs.append(found[4:])
        table = after(table, context[0])
    mine = after(rest_column, context[0])
    other = place.sibling(mine)
    sent = [place.to_tokens(c, i, j) for c, (i, j) in zip(context, PAIRS)]
    w_up, w_down, w_output, rest = assemble_rest(place, mine, other, share)
    w_up = w_up.reshape(width, hidden_width)
    w_down = w_down.reshape(hidden_width, width)
    vec = rest[:, :6, :share].transpose(1, 0, 2).reshape(6, width).astype(F32)
    b_output, gain_one, shift_one, b_down, gain_two, shift_two = (vec[i] for i in range(6))
    b_up = rest[:, 6, : 4 * share].reshape(hidden_width).astype(F32)

    context_tok = jnp.concatenate(sent, 1)
    w_output = w_output.reshape(4, 192, width)
    w_out = jnp.stack(
        [jnp.pad(pick(w_output, token_group ^ k), ((0, 64), (0, 0))) for k in range(4)]
    ).reshape(1024, width)

    first_sum = tokens.astype(F32) + matmul(context_tok, w_out) + b_output
    first, first_normal, first_scale = norm_forward(first_sum, gain_one, shift_one)
    first_low = first.astype(BF16)
    hidden = matmul(first_low, w_up) + b_up
    active, gelu_back = jax.vjp(partial(jax.nn.gelu, approximate=True), hidden)
    active_low = active.astype(BF16)
    second_sum = first + matmul(active_low, w_down) + b_down
    result, second_normal, second_scale = norm_forward(second_sum, gain_two, shift_two)
    second_grad, gain_two_grad, shift_two_grad = norm_backward(
        cotangent.astype(F32), second_normal, second_scale, gain_two
    )
    branch_grad = second_grad.astype(BF16)
    (hidden_grad,) = gelu_back(matmul(branch_grad, w_down.T))
    hidden_low = hidden_grad.astype(BF16)
    first_grad_in = second_grad + matmul(hidden_low, w_up.T)
    first_grad, gain_one_grad, shift_one_grad = norm_backward(
        first_grad_in, first_normal, first_scale, gain_one
    )
    attended_grad = first_grad.astype(BF16)
    context_grad = dot_lanes(attended_grad, w_out).astype(BF16)
    context_grads = [
        place.to_heads(context_grad[:, 256 * k : 256 * k + 256], i, j)
        for k, (i, j) in enumerate(PAIRS)
    ]

    down_bias_grad = jnp.sum(branch_grad.astype(F32), 0)
    up_bias_grad = jnp.sum(hidden_low.astype(F32), 0)
    output_bias_grad = jnp.sum(attended_grad.astype(F32), 0)
    vector_grads = jnp.stack(
        [output_bias_grad, gain_one_grad, shift_one_grad, down_bias_grad, gain_two_grad, shift_two_grad]
    )
    vector_grads = jnp.pad(vector_grads.reshape(6, devices, share), ((0, 2), (0, 0), (0, LANES - share)))
    wide = jnp.pad(up_bias_grad.reshape(1, devices, 4 * share), ((6, 1), (0, 0), (0, LANES - 4 * share)))
    vector_grads = (vector_grads + wide).transpose(1, 0, 2)
    kept, sent = weight_grads(
        place,
        after(active_low, context_grad),
        branch_grad,
        first_low,
        hidden_low,
        context_tok,
        attended_grad,
        vector_grads,
    )
    rest_state = (kept, place.sibling(sent))

    def head_backward(head, table):
        found = attend_backward(
            table, queries[head], probs[head], context_grads, pieces[head], head
        )
        return found[:4], found[4:]

    def halo(found):
        own_grad, next_grad, prev_grad, _ = found
        return own_grad, place.to_next(next_grad), place.to_previous(prev_grad)

    rest_parts = scatter_across(place, *rest_state)
    table = after(slots, rest_parts)
    rest_parts = exchange(rest_parts, CHIPS)
    results, halos = [], []
    results.append(head_backward(0, table))
    halos.append(halo(results[0][1]))
    table = after(table, results[0][1][3])
    results.append(head_backward(1, table))
    halos.append(halo(results[1][1]))

    def ring_slabs(grads):
        low = grads.astype(BF16)
        total = grads
        for k in range(1, slabs):
            total = total + place.along_slabs(low, k).astype(F32)
        return total

    table, _, *first = lax.optimization_barrier((table, results[1][1][3], *halos[0][1:]))
    halos[0] = (halos[0][0], *first)
    dqs, found = head_backward(2, table)
    first, second, *found = lax.optimization_barrier((*halos[1][1:], *found))
    halos[1] = (halos[1][0], first, second)
    results.append((dqs, found))
    halos.append(halo(found))
    ring_sum = ring_slabs(jnp.concatenate([results[head][1][3] for head in range(3)], -1))
    rest_last = scatter_slabs(after(rest_parts, found[3]))
    ring_sum, first, second, rest_last = lax.optimization_barrier(
        (ring_sum, *halos[2][1:], rest_last)
    )
    halos[2] = (halos[2][0], first, second)
    ring_sum = ring_sum + place.sibling(ring_sum.astype(BF16)).astype(F32)
    global_at = jnp.where(
        global_blocks // 32 == half, local_block(place, global_blocks % 32), -100
    ).astype(jnp.int32)

    global_at = after(global_at, rest_last)
    rest_last = exchange(rest_last, "slab")
    *heads_grads, bias_grad = join_heads(results, halos, ring_sum, global_at)
    kept, sent = heads_weight_grads(place, token_parts, heads_grads, bias_grad)
    *heads_grads, _ = lax.optimization_barrier((*heads_grads, kept))
    late = [dot_lanes(grad, w_heads).astype(BF16) for grad in heads_grads[2:]]
    *early, _ = lax.optimization_barrier((*heads_grads[:2], *late))[:3]
    early = [dot_lanes(grad, w_heads).astype(BF16) for grad in early]
    returned = [place.to_tokens(part, *pair) for part, pair in zip(early + late, PAIRS)]
    arrived = place.sibling(sent)
    arrived, rest_last = lax.optimization_barrier((arrived, rest_last))
    chunks = group_along(place, kept, arrived)
    chunks, *returned = lax.optimization_barrier((chunks, *returned))
    group_parts = group_across(chunks)
    tokens_grad = first_grad
    for part in returned:
        tokens_grad = tokens_grad + part.astype(F32)
    query_all, key_all, value_all, bias_sums = finish_heads(group_parts, share, scale)
    start = share * (place.h * 4 * slabs + 4 * place.n + 2 * place.x + place.c)
    bias_share = lax.dynamic_slice_in_dim(bias_sums, start, share, 1)
    query_bias_share, value_bias_share = bias_share[0], bias_share[1]
    rest_share = jnp.sum(rest_last.astype(F32), 0)
    up_share = jnp.concatenate([rest_share[i * share : (i + 1) * share] for i in range(4)], 1)
    down_share = rest_share[4 * share : 8 * share]
    output_share = rest_share[8 * share : 9 * share]
    pieces_of = [rest_share[9 * share + i, :share] for i in range(6)]

    return (
        result.astype(BF16),
        tokens_grad,
        query_all,
        query_bias_share,
        key_all,
        value_all,
        value_bias_share,
        output_share,
        pieces_of[0],
        pieces_of[1],
        pieces_of[2],
        up_share,
        rest_share[9 * share + 6, : 4 * share],
        down_share,
        pieces_of[3],
        pieces_of[4],
        pieces_of[5],
    )


def solution(mesh):
    devices = mesh.devices
    mesh = Mesh(devices.reshape(devices.shape[0], -1, 2, 2), AXES)
    rows = P(AXES, None)
    vector = P(AXES)
    tokens = P(("slab", "x", "core", "head"), None)
    return jax.shard_map(
        body,
        mesh=mesh,
        in_specs=(
            tokens,
            tokens,
            P(),
            P(),
            P("head", ("slab", "x", "core"), None),
            rows,
            vector,
            rows,
            rows,
            vector,
            rows,
            vector,
            vector,
            vector,
            rows,
            vector,
            rows,
            vector,
            vector,
            vector,
        ),
        out_specs=(
            tokens,
            tokens,
            rows,
            vector,
            rows,
            rows,
            vector,
            rows,
            vector,
            vector,
            vector,
            rows,
            vector,
            rows,
            vector,
            vector,
            vector,
        ),
        check_vma=False,
    )
```

```python
import jax
import jax.numpy as jnp
from jax import lax
from jax.experimental import pallas as pl
from jax.experimental.pallas import tpu as pltpu
from jax.sharding import Mesh
from jax.sharding import PartitionSpec as P

HEAD_DIM = 64
BLOCK = 64
LANES = 128
NORM_EPS = 1e-06
MASKED = -1e30
AXES = ("head", "slab", "x", "core")
CHIPS = ("head", "x")
BF16 = jnp.bfloat16
F32 = jnp.float32
PAIRS = ((0, 0), (0, 1), (1, 0), (1, 1))
VMEM_LIMIT = 60 * 1024 * 1024


def matmul(left, right):
    return jnp.dot(left, right, preferred_element_type=F32)


def dot_rows(left, right):
    return lax.dot_general(left, right, (((0,), (0,)), ((), ())), preferred_element_type=F32)


def dot_lanes(left, right):
    return lax.dot_general(left, right, (((1,), (1,)), ((), ())), preferred_element_type=F32)


class Place:
    def __init__(self):
        self.slabs = lax.axis_size("slab")
        self.size = 4 * self.slabs
        self.h, self.n, self.x, self.c = (lax.axis_index(axis) for axis in AXES)

    def send(self, value, target):
        def index(h, n, x, c):
            return h * self.size + 4 * n + 2 * x + c

        route = [
            (index(h, n, x, c), index(*target(h, n, x, c)))
            for h in range(2)
            for n in range(self.slabs)
            for x in range(2)
            for c in range(2)
        ]
        return lax.ppermute(value, AXES, route)

    def along_slabs(self, value, k):
        return self.send(value, lambda h, n, x, c: (h, n ^ k, x, c))

    def across(self, value, i, j):
        return self.send(value, lambda h, n, x, c: (h ^ i, n, x ^ j, c))

    def sibling(self, value):
        return self.send(value, lambda h, n, x, c: (h, n, x, 1 - c))

    def to_heads(self, value, i, j):
        return self.send(value, lambda h, n, x, c: (h ^ i, n, c ^ j, x))

    def to_tokens(self, value, i, j):
        return self.send(value, lambda h, n, x, c: (h ^ i, n, c, x ^ j))

    def to_next(self, value):
        def target(h, n, x, c):
            return (h, n, x, 1) if c == 0 else (h, (n + 1) % self.slabs, x, 0)

        return self.send(value, target)

    def to_previous(self, value):
        def target(h, n, x, c):
            return (h, n, x, 0) if c == 1 else (h, (n - 1) % self.slabs, x, 1)

        return self.send(value, target)


def exchange(value, axes):
    return lax.all_to_all(value, axes, split_axis=0, concat_axis=0, tiled=True)


def pick(value, index, axis=0):
    return lax.dynamic_index_in_dim(value, index, axis, keepdims=False)


def kernel_call(kernel, out_shape, name, flops=1000, **options):
    return pl.pallas_call(
        kernel,
        out_shape=out_shape,
        compiler_params=pltpu.CompilerParams(vmem_limit_bytes=VMEM_LIMIT),
        cost_estimate=pl.CostEstimate(
            flops=flops, bytes_accessed=1000, transcendentals=0
        ),
        name=name,
        **options,
    )


def whole(count):
    return [pl.BlockSpec(memory_space=pltpu.VMEM)] * count


def smem():
    return pl.BlockSpec(memory_space=pltpu.SMEM)


def after(value, *others):
    return lax.optimization_barrier((value,) + others)[0]


def side_of(head):
    return 1 - head % 2


def half_tile(value, start, side):
    tile = start // LANES * LANES
    found = value[:, tile : tile + LANES].astype(F32)
    if (start % LANES) // HEAD_DIM != side:
        found = pltpu.roll(found, HEAD_DIM, 1)
    return found


def left_lanes(rows):
    return lax.broadcasted_iota(jnp.int32, (rows, LANES), 1) < HEAD_DIM


def pack_heads(query_weight, key_weight, value_weight, biases, scale):
    share = query_weight.shape[0]

    def kernel(q_ref, k_ref, v_ref, b_ref, out_ref):
        left = left_lanes(share)
        for group in range(4):
            start = 3 * group * HEAD_DIM
            q = [half_tile(q_ref, start + t * HEAD_DIM, side_of(t)) * scale for t in range(3)]
            out_ref[group, :, :LANES] = jnp.where(left, q[1], q[0]).astype(BF16)
            extra = b_ref[...].astype(F32)
            out_ref[group, :, LANES : 2 * LANES] = jnp.where(left, extra, q[2]).astype(BF16)
            for t in range(3):
                side = side_of(t)
                k = half_tile(k_ref, start + t * HEAD_DIM, side)
                v = half_tile(v_ref, start + t * HEAD_DIM, 1 - side)
                both = jnp.where(left, k, v) if side == 0 else jnp.where(left, v, k)
                out_ref[group, :, (2 + t) * LANES : (3 + t) * LANES] = both.astype(BF16)

    return kernel_call(
        kernel,
        jax.ShapeDtypeStruct((4, share, 5 * LANES), BF16),
        "pack_heads",
        in_specs=whole(4),
        out_specs=whole(1)[0],
    )(query_weight, key_weight, value_weight, biases)


def pack_rest(up, down, output, vectors):
    share, width = output.shape
    height = -(-(9 * share + 8) // 16) * 16
    count = len(vectors)

    def kernel(up_ref, down_ref, output_ref, *refs):
        out_ref = refs[-1]
        for i in range(4):
            out_ref[i * share : (i + 1) * share] = up_ref[:, i * width : (i + 1) * width]
        out_ref[4 * share : 8 * share] = down_ref[...]
        out_ref[8 * share : 9 * share] = output_ref[...]
        row = lax.broadcasted_iota(jnp.int32, (height - 9 * share, LANES), 0)
        total = jnp.zeros(row.shape, F32)
        for i, ref in enumerate(refs[:count]):
            total = jnp.where(row == i, jnp.broadcast_to(ref[...].astype(F32), row.shape), total)
        out_ref[9 * share :, :LANES] = total.astype(BF16)
        out_ref[9 * share :, LANES:] = jnp.zeros((height - 9 * share, width - LANES), BF16)

    vectors = [jnp.pad(v, (0, LANES - v.shape[0]))[None] for v in vectors]
    return kernel_call(
        kernel,
        jax.ShapeDtypeStruct((height, width), BF16),
        "pack_rest",
        in_specs=whole(3 + count),
        out_specs=whole(1)[0],
    )(up, down, output, *vectors)


def stack_heads(parts):
    def kernel(*refs):
        for k, ref in enumerate(refs[:-1]):
            refs[-1][k] = ref[...]

    return kernel_call(
        kernel,
        jax.ShapeDtypeStruct((len(parts),) + parts[0].shape, BF16),
        "stack_heads",
        in_specs=whole(len(parts)),
        out_specs=whole(1)[0],
    )(*parts)


def assemble_heads(place, column, other):
    slabs, _, rows, columns = column.shape
    where = jnp.stack([place.h, place.n, place.x, place.c]).astype(jnp.int32)

    def kernel(where_ref, mine_ref, other_ref, out_ref, bias_ref):
        h, x, c = where_ref[0], where_ref[2], where_ref[3]
        left = left_lanes(rows)
        right = jnp.logical_not(left)
        for core, ref in enumerate((mine_ref, other_ref)):
            for p, (i, j) in enumerate(PAIRS):
                first = ref[0, p, :, :LANES].astype(F32)
                second = ref[0, p, :, LANES : 2 * LANES]
                q = (
                    jnp.where(right, first, 0.0),
                    jnp.where(left, first, 0.0),
                    jnp.where(right, second.astype(F32), 0.0),
                )
                at = (h ^ i, 0, x ^ j, c ^ core)
                for t in range(3):
                    out_ref[(*at, slice(None), slice(t * LANES, (t + 1) * LANES))] = q[t].astype(BF16)
                out_ref[(*at, slice(None), slice(3 * LANES, 6 * LANES))] = ref[0, p, :, 2 * LANES :]
                bias_ref[at] = second

    found = kernel_call(
        kernel,
        (
            jax.ShapeDtypeStruct((2, slabs, 2, 2, rows, 6 * LANES), BF16),
            jax.ShapeDtypeStruct((2, slabs, 2, 2, rows, LANES), BF16),
        ),
        "assemble_heads",
        grid_spec=pltpu.PrefetchScalarGridSpec(
            num_scalar_prefetch=1,
            grid=(slabs,),
            in_specs=[pl.BlockSpec((1, 4, rows, columns), lambda k, w: (k, 0, 0, 0))] * 2,
            out_specs=[
                pl.BlockSpec((2, 1, 2, 2, rows, 6 * LANES), lambda k, w: (0, k ^ w[1], 0, 0, 0, 0)),
                pl.BlockSpec((2, 1, 2, 2, rows, LANES), lambda k, w: (0, k ^ w[1], 0, 0, 0, 0)),
            ],
        ),
    )(where, column, other)
    return [value.reshape(8 * slabs, *value.shape[4:]) for value in found]


def assemble_rest(place, mine, other, share):
    _, slabs, rows, width = mine.shape
    where = place.c.reshape(1).astype(jnp.int32)

    def kernel(where_ref, mine_ref, other_ref, up_ref, down_ref, output_ref, vector_ref):
        for core, ref in ((where_ref[0], mine_ref), (1 - where_ref[0], other_ref)):
            for p in range(4):
                at = (p // 2, 0, p % 2, core)
                for q in range(4):
                    columns = slice(q * width, (q + 1) * width)
                    up_ref[(*at, slice(None), columns)] = ref[p, 0, q * share : (q + 1) * share]
                down_ref[at] = ref[p, 0, 4 * share : 8 * share]
                output_ref[at] = ref[p, 0, 8 * share : 9 * share]
                vector_ref[at] = ref[p, 0, 9 * share :]

    shapes = ((share, 4 * width), (4 * share, width), (share, width), (rows - 9 * share, width))
    found = kernel_call(
        kernel,
        tuple(jax.ShapeDtypeStruct((2, slabs, 2, 2) + shape, BF16) for shape in shapes),
        "assemble_rest",
        20_000_000_000,
        grid_spec=pltpu.PrefetchScalarGridSpec(
            num_scalar_prefetch=1,
            grid=(slabs,),
            in_specs=[pl.BlockSpec((4, 1, rows, width), lambda n, w: (0, n, 0, 0))] * 2,
            out_specs=[
                pl.BlockSpec((2, 1, 2, 2) + shape, lambda n, w: (0, n, 0, 0, 0, 0)) for shape in shapes
            ],
        ),
    )(where, mine, other)
    return [value.reshape(8 * slabs, *value.shape[4:]) for value in found]


def weight_grads(place, active, branch_grad, first, hidden_grad, context, attended_grad, vectors):
    devices = 8 * place.slabs
    step = devices // 4
    tokens, width = first.shape
    share = width // devices
    rows = -(-(9 * share + 8) // 16) * 16
    where = jnp.stack([place.h * 2 + place.c, place.c]).astype(jnp.int32)

    def kernel(where_ref, active_ref, branch_ref, first_ref, hidden_ref, context_ref, attended_ref, vector_ref, kept_ref, sent_ref):
        even = where_ref[1] == 0

        def put(start, stop, value):
            value = value.astype(BF16).reshape(step, stop - start, width)
            for p in range(step // 2):
                kept_ref[p, start:stop] = jnp.where(even, value[2 * p], value[2 * p + 1])
                sent_ref[p, start:stop] = jnp.where(even, value[2 * p + 1], value[2 * p])

        put(4 * share, 8 * share, dot_rows(active_ref[...], branch_ref[...]))
        columns = first_ref[...]
        for q in range(4):
            up = dot_rows(columns, hidden_ref[:, q * width : (q + 1) * width])
            put(q * share, (q + 1) * share, up[: step * share])
        put(8 * share, 9 * share, dot_rows(context_ref[...], attended_ref[...])[: step * share])
        for p in range(step // 2):
            for ref, at in ((kept_ref, 2 * p + where_ref[1]), (sent_ref, 2 * p + 1 - where_ref[1])):
                ref[p, 9 * share :] = jnp.zeros((rows - 9 * share, width), BF16)
                ref[p, 9 * share : 9 * share + 8, :LANES] = vector_ref[at].astype(BF16)

    first = jnp.pad(first.reshape(tokens, 4, 192), ((0, 0), (0, 0), (0, 64))).reshape(tokens, 1024)
    half = jax.ShapeDtypeStruct((devices // 2, rows, width), BF16)
    return kernel_call(
        kernel,
        (half, half),
        "weight_grads",
        15_000_000_000,
        grid_spec=pltpu.PrefetchScalarGridSpec(
            num_scalar_prefetch=1,
            grid=(4,),
            in_specs=[
                pl.BlockSpec((tokens, width), lambda g, w: (0, g)),
                pl.BlockSpec((tokens, width), lambda g, w: (0, 0)),
                pl.BlockSpec((tokens, 256), lambda g, w: (0, g)),
                pl.BlockSpec((tokens, 4 * width), lambda g, w: (0, 0)),
                pl.BlockSpec((tokens, 256), lambda g, w: (0, g ^ w[0])),
                pl.BlockSpec((tokens, width), lambda g, w: (0, 0)),
                pl.BlockSpec((step, 8, LANES), lambda g, w: (g, 0, 0)),
            ],
            out_specs=[pl.BlockSpec((step // 2, rows, width), lambda g, w: (g, 0, 0))] * 2,
        ),
    )(where, active, branch_grad, first, hidden_grad, context, attended_grad, vectors)


def heads_weight_grads(place, token_parts, heads_grads, bias_grad):
    slabs = place.slabs
    width = token_parts[0].shape[1]
    share = width // (8 * slabs)
    rows = max(share, 8)
    where = place.c.reshape(1).astype(jnp.int32)

    def kernel(where_ref, *refs):
        x_refs, g_refs, bias_ref, kept_ref, sent_ref = refs[:4], refs[4:8], *refs[8:]
        even = where_ref[0] == 0
        left = left_lanes(rows)
        row = lax.broadcasted_iota(jnp.int32, (rows, LANES), 0)
        extra = jnp.zeros((rows, LANES), F32)
        for which in range(6):
            head = which % 3
            if which < 3:
                start = head * LANES + side_of(head) * HEAD_DIM
            else:
                start = (3 + head) * LANES + (1 - side_of(head)) * HEAD_DIM
            value = jnp.broadcast_to(half_tile(bias_ref, start, 0)[0:1], (rows, LANES))
            extra = jnp.where(row == which, value, extra)

        def put(start, stop, value):
            value = value.astype(BF16).reshape(8 * slabs, share, stop - start)
            if rows > share:
                value = jnp.concatenate(
                    [value, jnp.zeros((8 * slabs, rows - share, stop - start), BF16)], 1
                )
            for p in range(4 * slabs):
                first, second = value[2 * p], value[2 * p + 1]
                if start == LANES:
                    first = jnp.where(left, extra, first.astype(F32)).astype(BF16)
                    second = jnp.where(left, extra, second.astype(F32)).astype(BF16)
                kept_ref[p, :, start:stop] = jnp.where(even, first, second)
                sent_ref[p, :, start:stop] = jnp.where(even, second, first)

        def product(start, stop):
            return sum(
                dot_rows(x_ref[...], g_ref[:, start:stop]) for x_ref, g_ref in zip(x_refs, g_refs)
            )

        q = product(0, 3 * LANES)
        put(0, LANES, q[:, :LANES] + q[:, LANES : 2 * LANES])
        put(LANES, 2 * LANES, q[:, 2 * LANES :])
        put(2 * LANES, 5 * LANES, product(3 * LANES, 6 * LANES))

    half = jax.ShapeDtypeStruct((4 * slabs, rows, 5 * LANES), BF16)
    return kernel_call(
        kernel,
        (half, half),
        "heads_weight_grads",
        in_specs=[smem()] + whole(9),
        out_specs=whole(2),
    )(where, *token_parts, *heads_grads, bias_grad)


def scatter_across(place, kept, arrived):
    slabs = place.slabs
    _, rows, width = kept.shape

    def kernel(kept_ref, arrived_ref, out_ref):
        for h in range(2):
            for x in range(2):
                total = kept_ref[h, 0, x].astype(F32) + arrived_ref[h, 0, x].astype(F32)
                out_ref[2 * h + x, 0] = total.astype(BF16)

    parts = kernel_call(
        kernel,
        jax.ShapeDtypeStruct((4, slabs, rows, width), BF16),
        "scatter_across",
        grid=(slabs,),
        in_specs=[pl.BlockSpec((2, 1, 2, rows, width), lambda n: (0, n, 0, 0, 0))] * 2,
        out_specs=pl.BlockSpec((4, 1, rows, width), lambda n: (0, n, 0, 0)),
    )(*(value.reshape(2, slabs, 2, rows, width) for value in (kept, arrived)))
    return parts


def scatter_slabs(parts):
    slabs, rows, width = parts.shape[1:]

    def kernel(ref, out_ref):
        out_ref[0] = sum(ref[p, 0].astype(F32) for p in range(4)).astype(BF16)

    total = kernel_call(
        kernel,
        jax.ShapeDtypeStruct((slabs, rows, width), BF16),
        "scatter_slabs",
        20_000_000_000,
        grid=(slabs,),
        in_specs=[pl.BlockSpec((4, 1, rows, width), lambda n: (0, n, 0, 0))],
        out_specs=pl.BlockSpec((1, rows, width), lambda n: (n, 0, 0)),
    )(parts)
    return total


def added(parts):
    return sum(part.astype(F32) for part in parts)


def group_along(place, kept, arrived):
    slabs = place.slabs
    _, rows, width = kept.shape

    def kernel(kept_ref, arrived_ref, out_ref):
        for h in range(2):
            for n in range(slabs):
                for x in range(2):
                    pair = kept_ref[h, n, x].astype(F32) + arrived_ref[h, n, x].astype(F32)
                    out_ref[n, 2 * h + x] = pair.astype(BF16)

    parts = kernel_call(
        kernel,
        jax.ShapeDtypeStruct((slabs, 4, rows, width), BF16),
        "group_along",
        in_specs=whole(2),
        out_specs=whole(1)[0],
    )(*(value.reshape(2, slabs, 2, rows, width) for value in (kept, arrived)))
    return exchange(parts, "slab")


def group_across(parts):
    slabs, _, rows, width = parts.shape

    def kernel(ref, out_ref):
        for p in range(4):
            out_ref[p] = sum(ref[n, p].astype(F32) for n in range(slabs)).astype(BF16)

    total = kernel_call(
        kernel,
        jax.ShapeDtypeStruct((4, rows, width), BF16),
        "group_across",
        in_specs=whole(1),
        out_specs=whole(1)[0],
    )(parts)
    return exchange(total, CHIPS)


def finish_heads(parts, share, scale):
    _, rows, _ = parts.shape
    width = 12 * HEAD_DIM

    def kernel(ref, q_ref, k_ref, v_ref, bias_ref):
        left = left_lanes(rows)
        bias_ref[...] = jnp.zeros(bias_ref.shape, F32)
        for which, out in enumerate((q_ref, k_ref, v_ref)):
            for tile in range(width // LANES):
                sides, sums = [], []
                for side in range(2):
                    head = 2 * tile + side
                    value = ref[head // 3]
                    t = head % 3
                    if which == 0:
                        start = (t // 2) * LANES + side_of(t) * HEAD_DIM
                    else:
                        at = side_of(t) if which == 1 else 1 - side_of(t)
                        start = (2 + t) * LANES + at * HEAD_DIM
                    sides.append(half_tile(value, start, side))
                    row = t if which == 0 else 3 + t
                    sums.append(half_tile(value, LANES, side)[row : row + 1])
                value = jnp.where(left, sides[0], sides[1])
                bias = jnp.where(left[0:1], sums[0], sums[1])
                if which == 0:
                    value, bias = value * scale, bias * scale
                lanes = slice(tile * LANES, (tile + 1) * LANES)
                out[:, lanes] = value[:share]
                if which != 1:
                    bias_ref[which // 2 : which // 2 + 1, lanes] = bias

    weight = jax.ShapeDtypeStruct((share, width), F32)
    return kernel_call(
        kernel,
        (weight, weight, weight, jax.ShapeDtypeStruct((8, width), F32)),
        "finish_heads",
        in_specs=whole(1),
        out_specs=whole(4),
    )(parts)


def join_heads(results, halos, ring_sum, global_at):
    dqs = [results[head][0][u] for u in range(4) for head in range(3)]
    owns = [halos[head][0] for head in range(3)]
    arrived = [halos[head][side] for head in range(3) for side in (1, 2)]
    rows, width = 8 * BLOCK, 6 * LANES

    def kernel(at_ref, *refs):
        dq_refs, own_refs, arrived_refs, ring_ref = refs[:12], refs[12:15], refs[15:21], refs[21]
        out_refs, bias_ref = refs[22:26], refs[26]

        def total(head, blocks):
            return (
                own_refs[head][blocks]
                + arrived_refs[2 * head][blocks].astype(F32)
                + arrived_refs[2 * head + 1][blocks].astype(F32)
            )

        bias = jnp.zeros((8, width), F32)
        for u in range(4):
            out = out_refs[u]
            for head in range(3):
                out[:, head * LANES : (head + 1) * LANES] = dq_refs[3 * u + head][...]
                lanes = slice((3 + head) * LANES, (4 + head) * LANES)
                value = total(head, slice(u * 8, (u + 1) * 8))
                out[:, lanes] = value.reshape(rows, LANES).astype(BF16)
            for which in range(2):
                at = at_ref[which] - 8 * u

                @pl.when((at >= 0) & (at < 8))
                def _():
                    block = jnp.clip(at, 0, 7)
                    row = pl.ds(pl.multiple_of(block * BLOCK, BLOCK), BLOCK)
                    for head in range(3):
                        lanes = slice(head * LANES, (head + 1) * LANES)
                        value = total(head, 8 * u + block)
                        for i in range(2):
                            same = at_ref[i] == at_ref[which]
                            value = value + jnp.where(same, ring_ref[i, :, lanes], 0.0)
                        out[row, (3 + head) * LANES : (4 + head) * LANES] = value.astype(BF16)

            bias = bias + matmul(jnp.ones((8, rows), BF16), out[...])
        bias_ref[...] = bias

    return kernel_call(
        kernel,
        [jax.ShapeDtypeStruct((rows, width), BF16)] * 4 + [jax.ShapeDtypeStruct((8, width), F32)],
        "join_heads",
        in_specs=[smem()] + whole(22),
        out_specs=whole(5),
    )(global_at, *dqs, *owns, *arrived, ring_sum)


def copy_all(sources, target, sems):
    copies = []
    start = 0
    for which, source in enumerate(sources):
        stop = start + source.shape[0]
        copies.append(pltpu.make_async_copy(source, target.at[start:stop], sems.at[which]))
        start = stop
    for copy in copies:
        copy.start()
    return copies


def shard_rows(column=0):
    return [pl.BlockSpec((BLOCK, LANES), lambda i, *_, u=u: (8 * u + i, column)) for u in range(4)]


def attend_forward(slots, query_doc, key_doc, queries, pieces, head, context=None):
    blocks = 32
    joined = 0 if context is None else 4
    columns = LANES if head < 2 else 2 * LANES

    def kernel(slots_ref, *refs):
        doc_refs, key_refs, q_refs = refs[:4], refs[4:8], refs[8:12]
        before = refs[12 : 12 + joined]
        sources = refs[12 + joined : 16 + joined]
        ctx_refs, p_refs = refs[16 + joined : 20 + joined], refs[20 + joined : 24 + joined]
        kv, sems = refs[24 + joined :]
        step = pl.program_id(0)

        @pl.when(step == 0)
        def _():
            for copy in copy_all(sources, kv, sems):
                copy.wait()

        left = lax.broadcasted_iota(jnp.int32, (1, LANES), 1) < BLOCK
        values = left if head % 2 == 0 else jnp.logical_not(left)
        slot, score = [], []
        for u in range(4):
            base = (head * blocks + u * 8 + step) * 8
            slot.append(jnp.concatenate([kv[slots_ref[base + s]] for s in range(8)], 0))
            score.append(dot_lanes(q_refs[u][...], slot[u]))
        low = []
        for u in range(4):
            query = doc_refs[u][...]
            tiles = []
            for tile in range(4):
                lanes = slice(tile * LANES, (tile + 1) * LANES)
                tiles.append(jnp.where(query == key_refs[u][0, :, lanes], score[u][:, lanes], MASKED))
            top = jnp.maximum(jnp.maximum(tiles[0], tiles[1]), jnp.maximum(tiles[2], tiles[3]))
            top = jnp.max(top, -1, keepdims=True)
            tiles = [jnp.exp(tile - top) for tile in tiles]
            total = (tiles[0] + tiles[1]) + (tiles[2] + tiles[3])
            inverse = 1.0 / jnp.sum(total, -1, keepdims=True)
            low.append(jnp.concatenate([(tile * inverse).astype(BF16) for tile in tiles], 1))
            p_refs[u][0] = low[u]
        for u in range(4):
            result = jnp.where(values, matmul(low[u], slot[u]), 0.0)
            if head == 1:
                result = jnp.where(values, result, before[u][...].astype(F32))
            if head == 2:
                ctx_refs[u][:, :LANES] = before[u][...]
            ctx_refs[u][:, columns - LANES :] = result.astype(BF16)

    return pl.pallas_call(
        kernel,
        out_shape=[jax.ShapeDtypeStruct((8 * BLOCK, columns), BF16)] * 4
        + [jax.ShapeDtypeStruct((8, BLOCK, 8 * BLOCK), BF16)] * 4,
        grid_spec=pltpu.PrefetchScalarGridSpec(
            num_scalar_prefetch=1,
            grid=(8,),
            in_specs=shard_rows()
            + [
                pl.BlockSpec((1, 1, 8 * BLOCK), lambda i, *_, u=u: (head * 32 + 8 * u + i, 0, 0))
                for u in range(4)
            ]
            + shard_rows()
            + [pl.BlockSpec((BLOCK, LANES), lambda i, *_: (i, 0))] * joined
            + [pl.BlockSpec(memory_space=pl.ANY)] * 4,
            out_specs=[pl.BlockSpec((BLOCK, columns), lambda i, *_: (i, 0))] * 4
            + [pl.BlockSpec((1, BLOCK, 8 * BLOCK), lambda i, *_: (i, 0, 0))] * 4,
            scratch_shapes=[
                pltpu.VMEM((3 * blocks + 2, BLOCK, LANES), BF16),
                pltpu.SemaphoreType.DMA((4,)),
            ],
        ),
        compiler_params=pltpu.CompilerParams(vmem_limit_bytes=VMEM_LIMIT),
        cost_estimate=pl.CostEstimate(
            flops=1_000_000_000, bytes_accessed=1000, transcendentals=0
        ),
        name="attend_forward",
    )(slots, *[query_doc] * 4, *[key_doc] * 4, *[queries] * 4, *(context or ()), *pieces)


def attend_backward(slots, queries, probs, grads, pieces, head):
    blocks = 32

    def kernel(slots_ref, *refs):
        q_refs, p_refs, grad_refs = refs[:4], refs[4:8], refs[8:12]
        sources = refs[12:16]
        dq_refs = refs[16:20]
        own_ref, next_ref, prev_ref, glob_ref, kv, acc, sems = refs[20:]
        step = pl.program_id(0)

        @pl.when(step == 0)
        def _():
            copies = copy_all(sources, kv, sems)

            def clear(i, _):
                acc[i] = jnp.zeros(acc.shape[1:], F32)
                return _

            lax.fori_loop(0, acc.shape[0], clear, 0)
            for copy in copies:
                copy.wait()

        left = lax.broadcasted_iota(jnp.int32, (1, LANES), 1) < BLOCK
        values = left if head % 2 == 0 else jnp.logical_not(left)
        slot, grad, prob_grad, score_grad = [], [], [], []
        for u in range(4):
            base = (head * blocks + u * 8 + step) * 8
            slot.append(jnp.concatenate([kv[slots_ref[base + s]] for s in range(8)], 0))
            grad.append(jnp.where(values, grad_refs[u][...].astype(F32), 0.0).astype(BF16))
            prob_grad.append(dot_lanes(grad[u], slot[u]))
        for u in range(4):
            probs_f = p_refs[u][0].astype(F32)
            both = probs_f * prob_grad[u]
            inner = jnp.sum(both, -1, keepdims=True)
            score_grad.append((both - probs_f * inner).astype(BF16))
        for u in range(4):
            dq = matmul(score_grad[u], slot[u])
            dq_refs[u][...] = jnp.where(values, 0.0, dq).astype(BF16)
        slot_grad = [
            dot_rows(
                jnp.concatenate([score_grad[u], p_refs[u][0]], 0),
                jnp.concatenate([q_refs[u][...], grad[u]], 0),
            )
            for u in range(4)
        ]
        for u in range(4):
            base = (head * blocks + u * 8 + step) * 8
            for s in range(8):
                where = slots_ref[base + s]
                acc[where] += slot_grad[u][s * BLOCK : (s + 1) * BLOCK]

        @pl.when(step == 7)
        def _():
            def finish(i, _):
                own_ref[i] = acc[i]
                next_ref[i] = acc[blocks + i].astype(BF16)
                prev_ref[i] = acc[2 * blocks + i].astype(BF16)
                return _

            lax.fori_loop(0, blocks, finish, 0)
            glob_ref[...] = acc[3 * blocks :]

    shape = (blocks, BLOCK, LANES)
    full = pl.BlockSpec(shape, lambda i, *_: (0, 0, 0))
    return pl.pallas_call(
        kernel,
        out_shape=[jax.ShapeDtypeStruct((8 * BLOCK, LANES), BF16)] * 4
        + [
            jax.ShapeDtypeStruct(shape, F32),
            jax.ShapeDtypeStruct(shape, BF16),
            jax.ShapeDtypeStruct(shape, BF16),
            jax.ShapeDtypeStruct((2,) + shape[1:], F32),
        ],
        grid_spec=pltpu.PrefetchScalarGridSpec(
            num_scalar_prefetch=1,
            grid=(8,),
            in_specs=shard_rows()
            + [pl.BlockSpec((1, BLOCK, 8 * BLOCK), lambda i, *_: (i, 0, 0))] * 4
            + [pl.BlockSpec((BLOCK, LANES), lambda i, *_: (i, head // 2))] * 4
            + [pl.BlockSpec(memory_space=pl.ANY)] * 4,
            out_specs=[pl.BlockSpec((BLOCK, LANES), lambda i, *_: (i, 0))] * 4
            + [full, full, full, pl.BlockSpec((2,) + shape[1:], lambda i, *_: (0, 0, 0))],
            scratch_shapes=[
                pltpu.VMEM((3 * blocks + 2,) + shape[1:], BF16),
                pltpu.VMEM((3 * blocks + 2,) + shape[1:], F32),
                pltpu.SemaphoreType.DMA((4,)),
            ],
        ),
        compiler_params=pltpu.CompilerParams(vmem_limit_bytes=VMEM_LIMIT),
        cost_estimate=pl.CostEstimate(
            flops=18_000_000_000, bytes_accessed=1000, transcendentals=0
        ),
        name="attend_backward",
    )(slots, *[queries] * 4, *probs, *grads, *pieces)


def project_heads(token_parts, w_heads, biases, group, shown_at, scale):
    width = w_heads.shape[0]
    rows = token_parts[0].shape[0]
    biases = biases.reshape(4, 192, LANES)

    def kernel(group_ref, at_ref, *refs):
        parts, (w_ref, b_ref) = refs[:4], refs[4:6]
        q_refs, kv_refs, shown_ref = refs[6:9], refs[9:12], refs[12]
        row = lax.broadcasted_iota(jnp.int32, (8, LANES), 0)
        lane = lax.broadcasted_iota(jnp.int32, (8, LANES), 1)
        select = jnp.where(row == lane, 1.0, 0.0).astype(BF16)
        column = jnp.concatenate([b_ref[0], jnp.zeros((64, LANES), BF16)], 0)
        vectors = dot_lanes(select, column)
        left = left_lanes(8)
        for part, ref in enumerate(parts):
            value = matmul(ref[...], w_ref[...])
            for head in range(3):
                side = side_of(head)
                q = half_tile(vectors, head * HEAD_DIM, side)[0:1] * scale
                v = half_tile(vectors, head * HEAD_DIM, 1 - side)[1:2]
                first = left[0:1] if side == 0 else jnp.logical_not(left[0:1])
                q = jnp.where(first, q, 0.0)
                v = jnp.where(first, 0.0, v)
                lanes = slice(head * LANES, (head + 1) * LANES)
                q_refs[head][part * rows : (part + 1) * rows] = (value[:, lanes] + q).astype(BF16)
                lanes = slice((3 + head) * LANES, (4 + head) * LANES)
                kv = (value[:, lanes] + v).astype(BF16).reshape(8, BLOCK, LANES)
                kv_refs[head][part * 8 : (part + 1) * 8] = kv
        for which in range(2):
            at = at_ref[which]
            for head in range(3):
                found = kv_refs[head][jnp.maximum(at, 0)]
                lanes = slice(head * LANES, (head + 1) * LANES)
                shown_ref[which, :, lanes] = jnp.where(at >= 0, found.astype(F32), 0.0).astype(BF16)

    return kernel_call(
        kernel,
        [jax.ShapeDtypeStruct((4 * rows, LANES), BF16)] * 3
        + [jax.ShapeDtypeStruct((32, BLOCK, LANES), BF16)] * 3
        + [jax.ShapeDtypeStruct((2, BLOCK, 3 * LANES), BF16)],
        "project_heads",
        grid_spec=pltpu.PrefetchScalarGridSpec(
            num_scalar_prefetch=2,
            grid=(1,),
            in_specs=[pl.BlockSpec((rows, width), lambda i, *_: (0, 0))] * 4
            + [
                pl.BlockSpec((width, width), lambda i, *_: (0, 0)),
                pl.BlockSpec((1, 192, LANES), lambda i, g, *_: (g[0], 0, 0)),
            ],
            out_specs=[pl.BlockSpec((4 * rows, LANES), lambda i, *_: (0, 0))] * 3
            + [pl.BlockSpec((32, BLOCK, LANES), lambda i, *_: (0, 0, 0))] * 3
            + [pl.BlockSpec((2, BLOCK, 3 * LANES), lambda i, *_: (0, 0, 0))],
        ),
    )(group.reshape(1).astype(jnp.int32), shown_at, *token_parts, w_heads, biases)


def feed_forward(tokens, cotangent, context, w_out, w_up, w_down, vectors, up_bias):
    rows, width = tokens.shape
    hidden_width = w_up.shape[1]
    tile = 512
    strip = 128
    group = 2 * LANES

    def kernel(tokens_ref, cot_ref, c0, c1, c2, c3, w_out_ref, w_up_ref, w_down_ref, vec_ref, up_bias_ref, *refs):
        (
            result_ref,
            grad_ref,
            low_ref,
            active_ref,
            branch_ref,
            hidden_ref,
            attended_ref,
            joined_ref,
            d0,
            d1,
            d2,
            d3,
            sums_ref,
            up_sums_ref,
            first,
            normal,
            scale_row,
            slope,
            total,
        ) = refs
        b_output, gain_one, shift_one, b_down, gain_two, shift_two = (
            vec_ref[i : i + 1] for i in range(6)
        )

        def standard(value):
            center = value - jnp.mean(value, -1, keepdims=True)
            spread = jnp.mean(center * center, -1, keepdims=True)
            inverse = lax.rsqrt(spread + NORM_EPS)
            return center * inverse, inverse

        def back(grad, value, inverse, gain):
            inner = grad * gain
            return inverse * (
                inner
                - jnp.mean(inner, -1, keepdims=True)
                - value * jnp.mean(inner * value, -1, keepdims=True)
            )

        for start in range(0, rows, strip):
            at = slice(start, start + strip)
            for k, ref in enumerate((c0, c1, c2, c3)):
                joined_ref[at, k * group : (k + 1) * group] = ref[at]
            value = matmul(joined_ref[at], w_out_ref[...])
            value = tokens_ref[at].astype(F32) + value + b_output
            value, inverse = standard(value)
            normal[at] = value
            scale_row[at] = inverse
            value = value * gain_one + shift_one
            first[at] = value
            low_ref[at] = value.astype(BF16)
        for j in range(0, hidden_width, tile):
            at = slice(j, j + tile)
            x = matmul(low_ref[...], w_up_ref[:, at]) + up_bias_ref[:, at]
            square = x * x
            t = jnp.tanh(0.7978845608028654 * (x + 0.044715 * (square * x)))
            cdf = 0.5 + 0.5 * t
            active = (x * cdf).astype(BF16)
            active_ref[:, at] = active
            rise = 0.7978845608028654 * (0.5 + (0.5 * 3.0 * 0.044715) * square)
            slope[:, at] = (cdf + x * (1.0 - t * t) * rise).astype(BF16)
            part = matmul(active, w_down_ref[at])
            total[...] = part if j == 0 else total[...] + part
        gain_sum = jnp.zeros((1, width), F32)
        shift_sum = jnp.zeros((1, width), F32)
        for start in range(0, rows, strip):
            at = slice(start, start + strip)
            value, inverse = standard(first[at] + total[at] + b_down)
            result_ref[at] = (value * gain_two + shift_two).astype(BF16)
            grad = cot_ref[at].astype(F32)
            gain_sum = gain_sum + jnp.sum(grad * value, 0, keepdims=True)
            shift_sum = shift_sum + jnp.sum(grad, 0, keepdims=True)
            value = back(grad, value, inverse, gain_two)
            total[at] = value
            branch_ref[at] = value.astype(BF16)
        ones = jnp.ones((8, rows), BF16)
        sums_ref[3:4] = matmul(ones, branch_ref[...])[0:1]
        sums_ref[4:5] = gain_sum
        sums_ref[5:6] = shift_sum
        for j in range(0, hidden_width, tile):
            at = slice(j, j + tile)
            x = dot_lanes(branch_ref[...], w_down_ref[at])
            x = (x * slope[:, at].astype(F32)).astype(BF16)
            hidden_ref[:, at] = x
            up_sums_ref[:, at] = matmul(ones, x)[0:1]
            total[...] += dot_lanes(x, w_up_ref[:, at])
        gain_sum = jnp.zeros((1, width), F32)
        shift_sum = jnp.zeros((1, width), F32)
        for start in range(0, rows, strip):
            at = slice(start, start + strip)
            grad = total[at]
            value = normal[at]
            gain_sum = gain_sum + jnp.sum(grad * value, 0, keepdims=True)
            shift_sum = shift_sum + jnp.sum(grad, 0, keepdims=True)
            value = back(grad, value, scale_row[at], gain_one)
            grad_ref[at] = value
            attended_ref[at] = value.astype(BF16)
        sums_ref[0:1] = matmul(ones, attended_ref[...])[0:1]
        sums_ref[1:2] = gain_sum
        sums_ref[2:3] = shift_sum
        for k, ref in enumerate((d0, d1, d2, d3)):
            ref[...] = dot_lanes(attended_ref[...], w_out_ref[k * group : (k + 1) * group]).astype(BF16)

    def shape(columns, kind=BF16):
        return jax.ShapeDtypeStruct((rows, columns), kind)

    return kernel_call(
        kernel,
        [
            shape(width),
            shape(width, F32),
            shape(width),
            shape(hidden_width),
            shape(width),
            shape(hidden_width),
            shape(width),
            shape(4 * group),
        ]
        + [shape(group)] * 4
        + [jax.ShapeDtypeStruct((6, width), F32), jax.ShapeDtypeStruct((1, hidden_width), F32)],
        "feed_forward",
        30_000_000_000,
        in_specs=whole(11),
        out_specs=whole(14),
        scratch_shapes=[
            pltpu.VMEM((rows, width), F32),
            pltpu.VMEM((rows, width), F32),
            pltpu.VMEM((rows, 1), F32),
            pltpu.VMEM((rows, hidden_width), BF16),
            pltpu.VMEM((rows, width), F32),
        ],
    )(tokens, cotangent, *context, w_out, w_up, w_down, vectors, up_bias)


def local_block(place, within):
    shard = within // 8
    return (((shard % 2) ^ place.h) * 2 + ((shard // 2) ^ place.x)) * 8 + within % 8


def doc_number(positions, starts):
    return jnp.sum((positions[..., None] >= starts).astype(jnp.int32), -1)


def slot_tables(place, global_blocks, random_parts, starts):
    ring = 2 * place.slabs
    half = 2 * place.n + place.c
    total = ring * 32
    found = []
    for arrived in random_parts:
        found.append(lax.dynamic_slice_in_dim(arrived, 3 * place.x, 3, 0).reshape(3, 2, 8, 3))
    chosen = jnp.stack(found, 2)
    chosen = jnp.where(place.h == 0, chosen, chosen[:, ::-1]).reshape(3, 32, 3)
    order = jnp.arange(32, dtype=jnp.int32)
    shard = order // 8
    query_ids = half * 32 + (((shard % 2) ^ place.x) * 2 + ((shard // 2) ^ place.h)) * 8 + order % 8
    near = (query_ids[:, None] + jnp.arange(-1, 2, dtype=jnp.int32)) % total
    ids = jnp.concatenate(
        [
            jnp.broadcast_to(near[None], (3, 32, 3)),
            jnp.broadcast_to(global_blocks, (3, 32, 2)),
            chosen,
        ],
        -1,
    )
    earlier = jnp.arange(8)[None, :] < jnp.arange(8)[:, None]
    repeated = jnp.any((ids[..., :, None] == ids[..., None, :]) & earlier, -1)
    distance = (ids // 32 - half) % ring
    region = jnp.where(distance == 0, 0, jnp.where(distance == 1, 1, 2))
    local = region * 32 + local_block(place, ids % 32)
    which = jnp.arange(8, dtype=jnp.int32)
    slots = jnp.where((which == 3) | (which == 4), 93 + which, local)
    marked = jnp.where(repeated, -1, ids)
    token = jnp.arange(BLOCK, dtype=jnp.int32)
    query_doc = doc_number(query_ids[:, None] * BLOCK + token, starts).reshape(32 * BLOCK, 1)
    key_doc = doc_number(marked[..., None] * BLOCK + token, starts)
    return (
        slots.reshape(-1).astype(jnp.int32),
        jnp.broadcast_to(query_doc, (32 * BLOCK, LANES)),
        key_doc.reshape(96, 1, 8 * BLOCK),
    )


def body(
    tokens,
    cotangent,
    doc_lengths,
    global_blocks,
    random_blocks,
    query_weight,
    query_bias,
    key_weight,
    value_weight,
    value_bias,
    output_weight,
    output_bias,
    first_gain,
    first_shift,
    up_weight,
    up_bias,
    down_weight,
    down_bias,
    second_gain,
    second_shift,
):
    place = Place()
    slabs = place.slabs
    devices = 8 * slabs
    width = tokens.shape[1]
    share = query_weight.shape[0]
    hidden_width = up_weight.shape[1]
    scale = HEAD_DIM ** (-0.5)
    group = place.h * 2 + place.x
    token_group = place.h * 2 + place.c

    biases = jnp.pad(jnp.stack([query_bias, value_bias], 1), ((0, 0), (0, LANES - 2)))
    groups = pack_heads(query_weight, key_weight, value_weight, biases, scale)
    parts = [pick(groups, group)] + [
        place.across(pick(groups, group ^ (2 * i + j)), i, j) for i, j in PAIRS[1:]
    ]
    vectors = [
        output_bias, first_gain, first_shift, down_bias, second_gain, second_shift, up_bias
    ]
    random_late = after(random_blocks, groups)
    random_parts = [place.to_heads(random_late, 0, j) for j in range(2)]
    *parts, random_parts[0], random_parts[1] = lax.optimization_barrier((*parts, *random_parts))
    stacked = stack_heads(parts)
    packed = pack_rest(after(up_weight, stacked), down_weight, output_weight, vectors)
    tokens_late = after(tokens, stacked)
    token_parts = [place.to_heads(tokens_late, i, j) for i, j in PAIRS]
    column = [stacked] + [place.along_slabs(stacked, k) for k in range(1, slabs)]
    which = jnp.arange(doc_lengths.shape[0])
    before = which[None, :] < which[:, None]
    starts = jnp.sum(jnp.where(before, doc_lengths[None, :], 0), 1).astype(jnp.int32)
    slots, query_doc, key_doc = slot_tables(place, global_blocks, random_parts, starts)
    packed, *column = lax.optimization_barrier((packed, *column))
    heads_column = jnp.stack(column)
    heads_column, slots, query_doc, key_doc, *token_parts = lax.optimization_barrier(
        (heads_column, slots, query_doc, key_doc, *token_parts)
    )
    other, *token_parts = lax.optimization_barrier((place.sibling(heads_column), *token_parts))
    arrived, bias = assemble_heads(place, heads_column, other)
    w_heads = arrived.reshape(width, width)
    packed_column = exchange(jnp.broadcast_to(packed, (slabs,) + packed.shape), "slab")
    half = 2 * place.n + place.c
    global_at = local_block(place, global_blocks % 32)
    shown_at = jnp.where(global_blocks // 32 == half, global_at, -1).astype(jnp.int32)
    found = project_heads(token_parts, w_heads, bias, group, shown_at, scale)
    queries, own, shown = found[:3], found[3:6], found[6]
    shown = shown + place.sibling(shown)
    shown, *own = lax.optimization_barrier((shown, *own))
    following = [place.to_previous(kv) for kv in own]
    previous = [place.to_next(kv) for kv in own]
    mine = pick(shown, place.c)
    for k in range(1, slabs):
        mine = mine + place.along_slabs(pick(shown, place.c), k)
    theirs = place.sibling(mine)
    shared = jnp.where(place.c == 0, jnp.stack([mine, theirs]), jnp.stack([theirs, mine]))

    packed_column = after(packed_column, own[0])
    rest_column = exchange(jnp.broadcast_to(packed_column, (4,) + packed_column.shape), CHIPS)

    pieces, probs, context, table = [], [], None, slots
    for head in range(3):
        lanes = slice(head * LANES, (head + 1) * LANES)
        pieces.append((own[head], following[head], previous[head], shared[:, :, lanes]))
        found = attend_forward(table, query_doc, key_doc, queries[head], pieces[head], head, context)
        context = found[:4]
        probs.append(found[4:])
        table = after(table, context[0])
    mine = after(rest_column, context[0])
    other = place.sibling(mine)
    sent = [place.to_tokens(c, i, j) for c, (i, j) in zip(context, PAIRS)]
    w_up, w_down, w_output, rest = assemble_rest(place, mine, other, share)
    w_up = w_up.reshape(width, hidden_width)
    w_down = w_down.reshape(hidden_width, width)
    vec = rest[:, :6, :share].transpose(1, 0, 2).reshape(6, width).astype(F32)
    b_up = rest[:, 6, : 4 * share].reshape(1, hidden_width).astype(F32)

    w_output = w_output.reshape(4, 192, width)
    w_out = jnp.stack(
        [jnp.pad(pick(w_output, token_group ^ k), ((0, 64), (0, 0))) for k in range(4)]
    ).reshape(1024, width)

    found = feed_forward(tokens, cotangent, sent, w_out, w_up, w_down, vec, b_up)
    result, first_grad, first_low, active_low, branch_grad, hidden_low, attended_grad, context_tok = found[:8]
    context_grad, sums, up_sums = found[8:12], found[12], found[13]
    context_grads = [place.to_heads(part, i, j) for part, (i, j) in zip(context_grad, PAIRS)]

    vector_grads = jnp.pad(sums.reshape(6, devices, share), ((0, 2), (0, 0), (0, LANES - share)))
    wide = jnp.pad(up_sums.reshape(1, devices, 4 * share), ((6, 1), (0, 0), (0, LANES - 4 * share)))
    vector_grads = (vector_grads + wide).transpose(1, 0, 2)
    kept, sent = weight_grads(
        place,
        active_low,
        branch_grad,
        first_low,
        hidden_low,
        context_tok,
        attended_grad,
        vector_grads,
    )
    rest_state = (kept, place.sibling(sent))

    def head_backward(head, table):
        found = attend_backward(
            table, queries[head], probs[head], context_grads, pieces[head], head
        )
        return found[:4], found[4:]

    def halo(found):
        own_grad, next_grad, prev_grad, _ = found
        return own_grad, place.to_next(next_grad), place.to_previous(prev_grad)

    rest_parts = scatter_across(place, *rest_state)
    table = after(slots, rest_parts)
    rest_parts = exchange(rest_parts, CHIPS)
    results, halos = [], []
    results.append(head_backward(0, table))
    halos.append(halo(results[0][1]))
    table = after(table, results[0][1][3])
    results.append(head_backward(1, table))
    halos.append(halo(results[1][1]))

    def ring_slabs(grads):
        low = grads.astype(BF16)
        total = grads
        for k in range(1, slabs):
            total = total + place.along_slabs(low, k).astype(F32)
        return total

    table, _, *first = lax.optimization_barrier((table, results[1][1][3], *halos[0][1:]))
    halos[0] = (halos[0][0], *first)
    dqs, found = head_backward(2, table)
    first, second, *found = lax.optimization_barrier((*halos[1][1:], *found))
    halos[1] = (halos[1][0], first, second)
    results.append((dqs, found))
    halos.append(halo(found))
    ring_sum = ring_slabs(jnp.concatenate([results[head][1][3] for head in range(3)], -1))
    rest_last = scatter_slabs(after(rest_parts, found[3]))
    ring_sum, first, second, rest_last = lax.optimization_barrier(
        (ring_sum, *halos[2][1:], rest_last)
    )
    halos[2] = (halos[2][0], first, second)
    ring_sum = ring_sum + place.sibling(ring_sum.astype(BF16)).astype(F32)
    global_at = jnp.where(
        global_blocks // 32 == half, local_block(place, global_blocks % 32), -100
    ).astype(jnp.int32)

    global_at = after(global_at, rest_last)
    rest_last = exchange(rest_last, "slab")
    *heads_grads, bias_grad = join_heads(results, halos, ring_sum, global_at)
    kept, sent = heads_weight_grads(place, token_parts, heads_grads, bias_grad)
    *heads_grads, _ = lax.optimization_barrier((*heads_grads, kept))
    late = [dot_lanes(grad, w_heads).astype(BF16) for grad in heads_grads[2:]]
    *early, _ = lax.optimization_barrier((*heads_grads[:2], *late))[:3]
    early = [dot_lanes(grad, w_heads).astype(BF16) for grad in early]
    returned = [place.to_tokens(part, *pair) for part, pair in zip(early + late, PAIRS)]
    arrived = place.sibling(sent)
    arrived, rest_last = lax.optimization_barrier((arrived, rest_last))
    chunks = group_along(place, kept, arrived)
    chunks, *returned = lax.optimization_barrier((chunks, *returned))
    group_parts = group_across(chunks)
    tokens_grad = first_grad
    for part in returned:
        tokens_grad = tokens_grad + part.astype(F32)
    query_all, key_all, value_all, bias_sums = finish_heads(group_parts, share, scale)
    start = share * (place.h * 4 * slabs + 4 * place.n + 2 * place.x + place.c)
    bias_share = lax.dynamic_slice_in_dim(bias_sums, start, share, 1)
    query_bias_share, value_bias_share = bias_share[0], bias_share[1]
    rest_share = jnp.sum(rest_last.astype(F32), 0)
    up_share = jnp.concatenate([rest_share[i * share : (i + 1) * share] for i in range(4)], 1)
    down_share = rest_share[4 * share : 8 * share]
    output_share = rest_share[8 * share : 9 * share]
    pieces_of = [rest_share[9 * share + i, :share] for i in range(6)]

    return (
        result,
        tokens_grad,
        query_all,
        query_bias_share,
        key_all,
        value_all,
        value_bias_share,
        output_share,
        pieces_of[0],
        pieces_of[1],
        pieces_of[2],
        up_share,
        rest_share[9 * share + 6, : 4 * share],
        down_share,
        pieces_of[3],
        pieces_of[4],
        pieces_of[5],
    )


def solution(mesh):
    devices = mesh.devices
    mesh = Mesh(devices.reshape(devices.shape[0], -1, 2, 2), AXES)
    rows = P(AXES, None)
    vector = P(AXES)
    tokens = P(("slab", "x", "core", "head"), None)
    return jax.shard_map(
        body,
        mesh=mesh,
        in_specs=(
            tokens,
            tokens,
            P(),
            P(),
            P("head", ("slab", "x", "core"), None),
            rows,
            vector,
            rows,
            rows,
            vector,
            rows,
            vector,
            vector,
            vector,
            rows,
            vector,
            rows,
            vector,
            vector,
            vector,
        ),
        out_specs=(
            tokens,
            tokens,
            rows,
            vector,
            rows,
            rows,
            vector,
            rows,
            vector,
            vector,
            vector,
            rows,
            vector,
            rows,
            vector,
            vector,
            vector,
        ),
        check_vma=False,
    )
```

```python
import jax
import jax.numpy as jnp
from jax import lax
from jax.experimental import pallas as pl
from jax.experimental.pallas import tpu as pltpu
from jax.sharding import Mesh
from jax.sharding import PartitionSpec as P

HEAD_DIM = 64
BLOCK = 64
LANES = 128
NORM_EPS = 1e-06
MASKED = -1e30
AXES = ("head", "slab", "x", "core")
CHIPS = ("head", "x")
BF16 = jnp.bfloat16
F32 = jnp.float32
PAIRS = ((0, 0), (0, 1), (1, 0), (1, 1))
VMEM_LIMIT = 60 * 1024 * 1024


def matmul(left, right):
    return jnp.dot(left, right, preferred_element_type=F32)


def dot_rows(left, right):
    return lax.dot_general(left, right, (((0,), (0,)), ((), ())), preferred_element_type=F32)


def dot_lanes(left, right):
    return lax.dot_general(left, right, (((1,), (1,)), ((), ())), preferred_element_type=F32)


class Place:
    def __init__(self):
        self.slabs = lax.axis_size("slab")
        self.size = 4 * self.slabs
        self.h, self.n, self.x, self.c = (lax.axis_index(axis) for axis in AXES)

    def send(self, value, target):
        def index(h, n, x, c):
            return h * self.size + 4 * n + 2 * x + c

        route = [
            (index(h, n, x, c), index(*target(h, n, x, c)))
            for h in range(2)
            for n in range(self.slabs)
            for x in range(2)
            for c in range(2)
        ]
        return lax.ppermute(value, AXES, route)

    def along_slabs(self, value, k):
        return self.send(value, lambda h, n, x, c: (h, n ^ k, x, c))

    def across(self, value, i, j):
        return self.send(value, lambda h, n, x, c: (h ^ i, n, x ^ j, c))

    def sibling(self, value):
        return self.send(value, lambda h, n, x, c: (h, n, x, 1 - c))

    def to_heads(self, value, i, j):
        return self.send(value, lambda h, n, x, c: (h ^ i, n, c ^ j, x))

    def to_tokens(self, value, i, j):
        return self.send(value, lambda h, n, x, c: (h ^ i, n, c, x ^ j))

    def to_next(self, value):
        def target(h, n, x, c):
            return (h, n, x, 1) if c == 0 else (h, (n + 1) % self.slabs, x, 0)

        return self.send(value, target)

    def to_previous(self, value):
        def target(h, n, x, c):
            return (h, n, x, 0) if c == 1 else (h, (n - 1) % self.slabs, x, 1)

        return self.send(value, target)


def exchange(value, axes):
    return lax.all_to_all(value, axes, split_axis=0, concat_axis=0, tiled=True)


def pick(value, index, axis=0):
    return lax.dynamic_index_in_dim(value, index, axis, keepdims=False)


def kernel_call(kernel, out_shape, name, flops=1000, **options):
    return pl.pallas_call(
        kernel,
        out_shape=out_shape,
        compiler_params=pltpu.CompilerParams(vmem_limit_bytes=VMEM_LIMIT),
        cost_estimate=pl.CostEstimate(
            flops=flops, bytes_accessed=1000, transcendentals=0
        ),
        name=name,
        **options,
    )


def whole(count):
    return [pl.BlockSpec(memory_space=pltpu.VMEM)] * count


def smem():
    return pl.BlockSpec(memory_space=pltpu.SMEM)


def after(value, *others):
    return lax.optimization_barrier((value,) + others)[0]


def side_of(head):
    return 1 - head % 2


def half_tile(value, start, side):
    tile = start // LANES * LANES
    found = value[:, tile : tile + LANES].astype(F32)
    if (start % LANES) // HEAD_DIM != side:
        found = pltpu.roll(found, HEAD_DIM, 1)
    return found


def left_lanes(rows):
    return lax.broadcasted_iota(jnp.int32, (rows, LANES), 1) < HEAD_DIM


def pack_heads(query_weight, key_weight, value_weight, biases, scale):
    share = query_weight.shape[0]

    def kernel(q_ref, k_ref, v_ref, b_ref, out_ref):
        left = left_lanes(share)
        for group in range(4):
            start = 3 * group * HEAD_DIM
            q = [half_tile(q_ref, start + t * HEAD_DIM, side_of(t)) * scale for t in range(3)]
            out_ref[group, :, :LANES] = jnp.where(left, q[1], q[0]).astype(BF16)
            extra = b_ref[...].astype(F32)
            out_ref[group, :, LANES : 2 * LANES] = jnp.where(left, extra, q[2]).astype(BF16)
            for t in range(3):
                side = side_of(t)
                k = half_tile(k_ref, start + t * HEAD_DIM, side)
                v = half_tile(v_ref, start + t * HEAD_DIM, 1 - side)
                both = jnp.where(left, k, v) if side == 0 else jnp.where(left, v, k)
                out_ref[group, :, (2 + t) * LANES : (3 + t) * LANES] = both.astype(BF16)

    return kernel_call(
        kernel,
        jax.ShapeDtypeStruct((4, share, 5 * LANES), BF16),
        "pack_heads",
        in_specs=whole(4),
        out_specs=whole(1)[0],
    )(query_weight, key_weight, value_weight, biases)


def pack_rest(up, down, output, vectors):
    share, width = output.shape
    height = -(-(9 * share + 8) // 16) * 16
    count = len(vectors)

    def kernel(up_ref, down_ref, output_ref, *refs):
        out_ref, held = refs[-2:]
        for i in range(4):
            out_ref[i * share : (i + 1) * share] = up_ref[:, i * width : (i + 1) * width]
        out_ref[4 * share : 8 * share] = down_ref[...]
        out_ref[8 * share : 9 * share] = output_ref[...]
        held[...] = jnp.zeros(held.shape, F32)
        for i, ref in enumerate(refs[:count]):
            held[i : i + 1, : ref.shape[1]] = ref[...].astype(F32)
        out_ref[9 * share :, :LANES] = held[...].astype(BF16)
        out_ref[9 * share :, LANES:] = jnp.zeros((height - 9 * share, width - LANES), BF16)

    vectors = [v[None] for v in vectors]
    return kernel_call(
        kernel,
        jax.ShapeDtypeStruct((height, width), BF16),
        "pack_rest",
        in_specs=whole(3 + count),
        out_specs=whole(1)[0],
        scratch_shapes=[pltpu.VMEM((height - 9 * share, LANES), F32)],
    )(up, down, output, *vectors)


def stack_heads(parts):
    def kernel(*refs):
        for k, ref in enumerate(refs[:-1]):
            refs[-1][k] = ref[...]

    return kernel_call(
        kernel,
        jax.ShapeDtypeStruct((len(parts),) + parts[0].shape, BF16),
        "stack_heads",
        in_specs=whole(len(parts)),
        out_specs=whole(1)[0],
    )(*parts)


def assemble_heads(place, column, other):
    slabs, _, rows, columns = column.shape
    where = jnp.stack([place.h, place.n, place.x, place.c]).astype(jnp.int32)

    def kernel(where_ref, mine_ref, other_ref, out_ref, bias_ref):
        h, x, c = where_ref[0], where_ref[2], where_ref[3]
        left = left_lanes(rows)
        right = jnp.logical_not(left)
        for core, ref in enumerate((mine_ref, other_ref)):
            for p, (i, j) in enumerate(PAIRS):
                first = ref[0, p, :, :LANES].astype(F32)
                second = ref[0, p, :, LANES : 2 * LANES]
                q = (
                    jnp.where(right, first, 0.0),
                    jnp.where(left, first, 0.0),
                    jnp.where(right, second.astype(F32), 0.0),
                )
                at = (h ^ i, 0, x ^ j, c ^ core)
                for t in range(3):
                    out_ref[(*at, slice(None), slice(t * LANES, (t + 1) * LANES))] = q[t].astype(BF16)
                out_ref[(*at, slice(None), slice(3 * LANES, 6 * LANES))] = ref[0, p, :, 2 * LANES :]
                bias_ref[at] = second

    found = kernel_call(
        kernel,
        (
            jax.ShapeDtypeStruct((2, slabs, 2, 2, rows, 6 * LANES), BF16),
            jax.ShapeDtypeStruct((2, slabs, 2, 2, rows, LANES), BF16),
        ),
        "assemble_heads",
        grid_spec=pltpu.PrefetchScalarGridSpec(
            num_scalar_prefetch=1,
            grid=(slabs,),
            in_specs=[pl.BlockSpec((1, 4, rows, columns), lambda k, w: (k, 0, 0, 0))] * 2,
            out_specs=[
                pl.BlockSpec((2, 1, 2, 2, rows, 6 * LANES), lambda k, w: (0, k ^ w[1], 0, 0, 0, 0)),
                pl.BlockSpec((2, 1, 2, 2, rows, LANES), lambda k, w: (0, k ^ w[1], 0, 0, 0, 0)),
            ],
        ),
    )(where, column, other)
    return [value.reshape(8 * slabs, *value.shape[4:]) for value in found]


def assemble_rest(place, mine, other, share):
    _, slabs, rows, width = mine.shape
    where = place.c.reshape(1).astype(jnp.int32)

    def kernel(where_ref, mine_ref, other_ref, up_ref, down_ref, output_ref, vector_ref):
        for core, ref in ((where_ref[0], mine_ref), (1 - where_ref[0], other_ref)):
            for p in range(4):
                at = (p // 2, 0, p % 2, core)
                for q in range(4):
                    columns = slice(q * width, (q + 1) * width)
                    up_ref[(*at, slice(None), columns)] = ref[p, 0, q * share : (q + 1) * share]
                down_ref[at] = ref[p, 0, 4 * share : 8 * share]
                output_ref[at] = ref[p, 0, 8 * share : 9 * share]
                vector_ref[at] = ref[p, 0, 9 * share :, :LANES]

    shapes = ((share, 4 * width), (4 * share, width), (share, width), (rows - 9 * share, LANES))
    found = kernel_call(
        kernel,
        tuple(jax.ShapeDtypeStruct((2, slabs, 2, 2) + shape, BF16) for shape in shapes),
        "assemble_rest",
        20_000_000_000,
        grid_spec=pltpu.PrefetchScalarGridSpec(
            num_scalar_prefetch=1,
            grid=(slabs,),
            in_specs=[pl.BlockSpec((4, 1, rows, width), lambda n, w: (0, n, 0, 0))] * 2,
            out_specs=[
                pl.BlockSpec((2, 1, 2, 2) + shape, lambda n, w: (0, n, 0, 0, 0, 0)) for shape in shapes
            ],
        ),
    )(where, mine, other)
    return [value.reshape(8 * slabs, *value.shape[4:]) for value in found]


def weight_grads(place, active, branch_grad, first, hidden_grad, context, attended_grad, vectors):
    devices = 8 * place.slabs
    step = devices // 4
    tokens, width = branch_grad.shape
    share = width // devices
    rows = -(-(9 * share + 8) // 16) * 16
    where = jnp.stack([place.h * 2 + place.c, place.c]).astype(jnp.int32)

    def kernel(where_ref, active_ref, branch_ref, first_ref, hidden_ref, context_ref, attended_ref, vector_ref, kept_ref, sent_ref):
        even = where_ref[1] == 0

        def put(start, stop, value):
            value = value.astype(BF16).reshape(step, stop - start, width)
            for p in range(step // 2):
                kept_ref[p, start:stop] = jnp.where(even, value[2 * p], value[2 * p + 1])
                sent_ref[p, start:stop] = jnp.where(even, value[2 * p + 1], value[2 * p])

        put(4 * share, 8 * share, dot_rows(active_ref[...], branch_ref[...]))
        columns = first_ref[...]
        for q in range(4):
            up = dot_rows(columns, hidden_ref[:, q * width : (q + 1) * width])
            put(q * share, (q + 1) * share, up[: step * share])
        put(8 * share, 9 * share, dot_rows(context_ref[...], attended_ref[...])[: step * share])
        for p in range(step // 2):
            for ref, at in ((kept_ref, 2 * p + where_ref[1]), (sent_ref, 2 * p + 1 - where_ref[1])):
                ref[p, 9 * share :] = jnp.zeros((rows - 9 * share, width), BF16)
                ref[p, 9 * share : 9 * share + 8, :LANES] = vector_ref[at].astype(BF16)

    half = jax.ShapeDtypeStruct((devices // 2, rows, width), BF16)
    return kernel_call(
        kernel,
        (half, half),
        "weight_grads",
        15_000_000_000,
        grid_spec=pltpu.PrefetchScalarGridSpec(
            num_scalar_prefetch=1,
            grid=(4,),
            in_specs=[
                pl.BlockSpec((tokens, width), lambda g, w: (0, g)),
                pl.BlockSpec((tokens, width), lambda g, w: (0, 0)),
                pl.BlockSpec((tokens, 256), lambda g, w: (0, g)),
                pl.BlockSpec((tokens, 4 * width), lambda g, w: (0, 0)),
                pl.BlockSpec((tokens, 256), lambda g, w: (0, g ^ w[0])),
                pl.BlockSpec((tokens, width), lambda g, w: (0, 0)),
                pl.BlockSpec((step, 8, LANES), lambda g, w: (g, 0, 0)),
            ],
            out_specs=[pl.BlockSpec((step // 2, rows, width), lambda g, w: (g, 0, 0))] * 2,
        ),
    )(where, active, branch_grad, first, hidden_grad, context, attended_grad, vectors)


def heads_weight_grads(place, token_parts, heads_grads, bias_grad):
    slabs = place.slabs
    width = token_parts[0].shape[1]
    share = width // (8 * slabs)
    rows = max(share, 8)
    where = place.c.reshape(1).astype(jnp.int32)

    def kernel(where_ref, *refs):
        x_refs, g_refs, bias_ref, kept_ref, sent_ref = refs[:4], refs[4:8], *refs[8:]
        even = where_ref[0] == 0
        left = left_lanes(rows)
        row = lax.broadcasted_iota(jnp.int32, (rows, LANES), 0)
        extra = jnp.zeros((rows, LANES), F32)
        for which in range(6):
            head = which % 3
            if which < 3:
                start = head * LANES + side_of(head) * HEAD_DIM
            else:
                start = (3 + head) * LANES + (1 - side_of(head)) * HEAD_DIM
            value = jnp.broadcast_to(half_tile(bias_ref, start, 0)[0:1], (rows, LANES))
            extra = jnp.where(row == which, value, extra)

        def put(start, stop, value):
            value = value.astype(BF16).reshape(8 * slabs, share, stop - start)
            if rows > share:
                value = jnp.concatenate(
                    [value, jnp.zeros((8 * slabs, rows - share, stop - start), BF16)], 1
                )
            for p in range(4 * slabs):
                first, second = value[2 * p], value[2 * p + 1]
                if start == LANES:
                    first = jnp.where(left, extra, first.astype(F32)).astype(BF16)
                    second = jnp.where(left, extra, second.astype(F32)).astype(BF16)
                kept_ref[p, :, start:stop] = jnp.where(even, first, second)
                sent_ref[p, :, start:stop] = jnp.where(even, second, first)

        def product(start, stop):
            return sum(
                dot_rows(x_ref[...], g_ref[:, start:stop]) for x_ref, g_ref in zip(x_refs, g_refs)
            )

        q = product(0, 3 * LANES)
        put(0, LANES, q[:, :LANES] + q[:, LANES : 2 * LANES])
        put(LANES, 2 * LANES, q[:, 2 * LANES :])
        put(2 * LANES, 5 * LANES, product(3 * LANES, 6 * LANES))

    half = jax.ShapeDtypeStruct((4 * slabs, rows, 5 * LANES), BF16)
    return kernel_call(
        kernel,
        (half, half),
        "heads_weight_grads",
        in_specs=[smem()] + whole(9),
        out_specs=whole(2),
    )(where, *token_parts, *heads_grads, bias_grad)


def scatter_across(place, kept, arrived):
    slabs = place.slabs
    _, rows, width = kept.shape

    def kernel(kept_ref, arrived_ref, out_ref):
        for h in range(2):
            for x in range(2):
                total = kept_ref[h, 0, x].astype(F32) + arrived_ref[h, 0, x].astype(F32)
                out_ref[2 * h + x, 0] = total.astype(BF16)

    parts = kernel_call(
        kernel,
        jax.ShapeDtypeStruct((4, slabs, rows, width), BF16),
        "scatter_across",
        grid=(slabs,),
        in_specs=[pl.BlockSpec((2, 1, 2, rows, width), lambda n: (0, n, 0, 0, 0))] * 2,
        out_specs=pl.BlockSpec((4, 1, rows, width), lambda n: (0, n, 0, 0)),
    )(*(value.reshape(2, slabs, 2, rows, width) for value in (kept, arrived)))
    return parts


def scatter_slabs(parts):
    slabs, rows, width = parts.shape[1:]

    def kernel(ref, out_ref):
        out_ref[0] = sum(ref[p, 0].astype(F32) for p in range(4)).astype(BF16)

    total = kernel_call(
        kernel,
        jax.ShapeDtypeStruct((slabs, rows, width), BF16),
        "scatter_slabs",
        20_000_000_000,
        grid=(slabs,),
        in_specs=[pl.BlockSpec((4, 1, rows, width), lambda n: (0, n, 0, 0))],
        out_specs=pl.BlockSpec((1, rows, width), lambda n: (n, 0, 0)),
    )(parts)
    return total


def added(parts):
    return sum(part.astype(F32) for part in parts)


def group_along(place, kept, arrived):
    slabs = place.slabs
    _, rows, width = kept.shape

    def kernel(kept_ref, arrived_ref, out_ref):
        for h in range(2):
            for n in range(slabs):
                for x in range(2):
                    pair = kept_ref[h, n, x].astype(F32) + arrived_ref[h, n, x].astype(F32)
                    out_ref[n, 2 * h + x] = pair.astype(BF16)

    parts = kernel_call(
        kernel,
        jax.ShapeDtypeStruct((slabs, 4, rows, width), BF16),
        "group_along",
        in_specs=whole(2),
        out_specs=whole(1)[0],
    )(*(value.reshape(2, slabs, 2, rows, width) for value in (kept, arrived)))
    return exchange(parts, "slab")


def group_across(parts):
    slabs, _, rows, width = parts.shape

    def kernel(ref, out_ref):
        for p in range(4):
            out_ref[p] = sum(ref[n, p].astype(F32) for n in range(slabs)).astype(BF16)

    total = kernel_call(
        kernel,
        jax.ShapeDtypeStruct((4, rows, width), BF16),
        "group_across",
        in_specs=whole(1),
        out_specs=whole(1)[0],
    )(parts)
    return exchange(total, CHIPS)


def finish_heads(parts, share, scale):
    _, rows, _ = parts.shape
    width = 12 * HEAD_DIM

    def kernel(ref, q_ref, k_ref, v_ref, bias_ref):
        left = left_lanes(rows)
        bias_ref[...] = jnp.zeros(bias_ref.shape, F32)
        for which, out in enumerate((q_ref, k_ref, v_ref)):
            for tile in range(width // LANES):
                sides, sums = [], []
                for side in range(2):
                    head = 2 * tile + side
                    value = ref[head // 3]
                    t = head % 3
                    if which == 0:
                        start = (t // 2) * LANES + side_of(t) * HEAD_DIM
                    else:
                        at = side_of(t) if which == 1 else 1 - side_of(t)
                        start = (2 + t) * LANES + at * HEAD_DIM
                    sides.append(half_tile(value, start, side))
                    row = t if which == 0 else 3 + t
                    sums.append(half_tile(value, LANES, side)[row : row + 1])
                value = jnp.where(left, sides[0], sides[1])
                bias = jnp.where(left[0:1], sums[0], sums[1])
                if which == 0:
                    value, bias = value * scale, bias * scale
                lanes = slice(tile * LANES, (tile + 1) * LANES)
                out[:, lanes] = value[:share]
                if which != 1:
                    bias_ref[which // 2 : which // 2 + 1, lanes] = bias

    weight = jax.ShapeDtypeStruct((share, width), F32)
    return kernel_call(
        kernel,
        (weight, weight, weight, jax.ShapeDtypeStruct((8, width), F32)),
        "finish_heads",
        in_specs=whole(1),
        out_specs=whole(4),
    )(parts)


def join_heads(results, halos, ring_sum, global_at):
    dqs = [results[head][0][u] for u in range(4) for head in range(3)]
    owns = [halos[head][0] for head in range(3)]
    arrived = [halos[head][side] for head in range(3) for side in (1, 2)]
    rows, width = 8 * BLOCK, 6 * LANES

    def kernel(at_ref, *refs):
        dq_refs, own_refs, arrived_refs, ring_ref = refs[:12], refs[12:15], refs[15:21], refs[21]
        out_refs, bias_ref = refs[22:26], refs[26]

        def total(head, blocks):
            return (
                own_refs[head][blocks]
                + arrived_refs[2 * head][blocks].astype(F32)
                + arrived_refs[2 * head + 1][blocks].astype(F32)
            )

        bias = jnp.zeros((8, width), F32)
        for u in range(4):
            out = out_refs[u]
            for head in range(3):
                out[:, head * LANES : (head + 1) * LANES] = dq_refs[3 * u + head][...]
                lanes = slice((3 + head) * LANES, (4 + head) * LANES)
                value = total(head, slice(u * 8, (u + 1) * 8))
                out[:, lanes] = value.reshape(rows, LANES).astype(BF16)
            for which in range(2):
                at = at_ref[which] - 8 * u

                @pl.when((at >= 0) & (at < 8))
                def _():
                    block = jnp.clip(at, 0, 7)
                    row = pl.ds(pl.multiple_of(block * BLOCK, BLOCK), BLOCK)
                    for head in range(3):
                        lanes = slice(head * LANES, (head + 1) * LANES)
                        value = total(head, 8 * u + block)
                        for i in range(2):
                            same = at_ref[i] == at_ref[which]
                            value = value + jnp.where(same, ring_ref[i, :, lanes], 0.0)
                        out[row, (3 + head) * LANES : (4 + head) * LANES] = value.astype(BF16)

            bias = bias + matmul(jnp.ones((8, rows), BF16), out[...])
        bias_ref[...] = bias

    return kernel_call(
        kernel,
        [jax.ShapeDtypeStruct((rows, width), BF16)] * 4 + [jax.ShapeDtypeStruct((8, width), F32)],
        "join_heads",
        in_specs=[smem()] + whole(22),
        out_specs=whole(5),
    )(global_at, *dqs, *owns, *arrived, ring_sum)


def copy_all(sources, target, sems):
    copies = []
    start = 0
    for which, source in enumerate(sources):
        stop = start + source.shape[0]
        copies.append(pltpu.make_async_copy(source, target.at[start:stop], sems.at[which]))
        start = stop
    for copy in copies:
        copy.start()
    return copies


def shard_rows(column=0):
    return [pl.BlockSpec((BLOCK, LANES), lambda i, *_, u=u: (8 * u + i, column)) for u in range(4)]


def attend_forward(slots, query_doc, key_doc, queries, pieces, head, context=None):
    blocks = 32
    joined = 0 if context is None else 4
    columns = LANES if head < 2 else 2 * LANES

    def kernel(slots_ref, *refs):
        doc_refs, key_refs, q_refs = refs[:4], refs[4:8], refs[8:12]
        before = refs[12 : 12 + joined]
        sources = refs[12 + joined : 16 + joined]
        ctx_refs, p_refs = refs[16 + joined : 20 + joined], refs[20 + joined : 24 + joined]
        kv, sems = refs[24 + joined :]
        step = pl.program_id(0)

        @pl.when(step == 0)
        def _():
            for copy in copy_all(sources, kv, sems):
                copy.wait()

        left = lax.broadcasted_iota(jnp.int32, (1, LANES), 1) < BLOCK
        values = left if head % 2 == 0 else jnp.logical_not(left)
        slot, score = [], []
        for u in range(4):
            base = (head * blocks + u * 8 + step) * 8
            slot.append(jnp.concatenate([kv[slots_ref[base + s]] for s in range(8)], 0))
            score.append(dot_lanes(q_refs[u][...], slot[u]))
        low = []
        for u in range(4):
            query = doc_refs[u][...]
            tiles = []
            for tile in range(4):
                lanes = slice(tile * LANES, (tile + 1) * LANES)
                tiles.append(jnp.where(query == key_refs[u][0, :, lanes], score[u][:, lanes], MASKED))
            top = jnp.maximum(jnp.maximum(tiles[0], tiles[1]), jnp.maximum(tiles[2], tiles[3]))
            top = jnp.max(top, -1, keepdims=True)
            tiles = [jnp.exp(tile - top) for tile in tiles]
            total = (tiles[0] + tiles[1]) + (tiles[2] + tiles[3])
            inverse = 1.0 / jnp.sum(total, -1, keepdims=True)
            low.append(jnp.concatenate([(tile * inverse).astype(BF16) for tile in tiles], 1))
            p_refs[u][0] = low[u]
        for u in range(4):
            result = jnp.where(values, matmul(low[u], slot[u]), 0.0)
            if head == 1:
                result = jnp.where(values, result, before[u][...].astype(F32))
            if head == 2:
                ctx_refs[u][:, :LANES] = before[u][...]
            ctx_refs[u][:, columns - LANES :] = result.astype(BF16)

    return pl.pallas_call(
        kernel,
        out_shape=[jax.ShapeDtypeStruct((8 * BLOCK, columns), BF16)] * 4
        + [jax.ShapeDtypeStruct((8, BLOCK, 8 * BLOCK), BF16)] * 4,
        grid_spec=pltpu.PrefetchScalarGridSpec(
            num_scalar_prefetch=1,
            grid=(8,),
            in_specs=shard_rows()
            + [
                pl.BlockSpec((1, 1, 8 * BLOCK), lambda i, *_, u=u: (head * 32 + 8 * u + i, 0, 0))
                for u in range(4)
            ]
            + shard_rows()
            + [pl.BlockSpec((BLOCK, LANES), lambda i, *_: (i, 0))] * joined
            + [pl.BlockSpec(memory_space=pl.ANY)] * 4,
            out_specs=[pl.BlockSpec((BLOCK, columns), lambda i, *_: (i, 0))] * 4
            + [pl.BlockSpec((1, BLOCK, 8 * BLOCK), lambda i, *_: (i, 0, 0))] * 4,
            scratch_shapes=[
                pltpu.VMEM((3 * blocks + 2, BLOCK, LANES), BF16),
                pltpu.SemaphoreType.DMA((4,)),
            ],
        ),
        compiler_params=pltpu.CompilerParams(vmem_limit_bytes=VMEM_LIMIT),
        cost_estimate=pl.CostEstimate(
            flops=1_000_000_000, bytes_accessed=1000, transcendentals=0
        ),
        name="attend_forward",
    )(slots, *[query_doc] * 4, *[key_doc] * 4, *[queries] * 4, *(context or ()), *pieces)


def attend_backward(slots, queries, probs, grads, pieces, head):
    blocks = 32

    def kernel(slots_ref, *refs):
        q_refs, p_refs, grad_refs = refs[:4], refs[4:8], refs[8:12]
        sources = refs[12:16]
        dq_refs = refs[16:20]
        own_ref, next_ref, prev_ref, glob_ref, kv, acc, sems = refs[20:]
        step = pl.program_id(0)

        @pl.when(step == 0)
        def _():
            copies = copy_all(sources, kv, sems)

            def clear(i, _):
                acc[i] = jnp.zeros(acc.shape[1:], F32)
                return _

            lax.fori_loop(0, acc.shape[0], clear, 0)
            for copy in copies:
                copy.wait()

        left = lax.broadcasted_iota(jnp.int32, (1, LANES), 1) < BLOCK
        values = left if head % 2 == 0 else jnp.logical_not(left)
        slot, grad, prob_grad, score_grad = [], [], [], []
        for u in range(4):
            base = (head * blocks + u * 8 + step) * 8
            slot.append(jnp.concatenate([kv[slots_ref[base + s]] for s in range(8)], 0))
            grad.append(jnp.where(values, grad_refs[u][...].astype(F32), 0.0).astype(BF16))
            prob_grad.append(dot_lanes(grad[u], slot[u]))
        for u in range(4):
            probs_f = p_refs[u][0].astype(F32)
            both = probs_f * prob_grad[u]
            inner = jnp.sum(both, -1, keepdims=True)
            score_grad.append((both - probs_f * inner).astype(BF16))
        for u in range(4):
            dq = matmul(score_grad[u], slot[u])
            dq_refs[u][...] = jnp.where(values, 0.0, dq).astype(BF16)
        slot_grad = [
            dot_rows(
                jnp.concatenate([score_grad[u], p_refs[u][0]], 0),
                jnp.concatenate([q_refs[u][...], grad[u]], 0),
            )
            for u in range(4)
        ]
        for u in range(4):
            base = (head * blocks + u * 8 + step) * 8
            for s in range(8):
                where = slots_ref[base + s]
                acc[where] += slot_grad[u][s * BLOCK : (s + 1) * BLOCK]

        @pl.when(step == 7)
        def _():
            def finish(i, _):
                own_ref[i] = acc[i]
                next_ref[i] = acc[blocks + i].astype(BF16)
                prev_ref[i] = acc[2 * blocks + i].astype(BF16)
                return _

            lax.fori_loop(0, blocks, finish, 0)
            glob_ref[...] = acc[3 * blocks :]

    shape = (blocks, BLOCK, LANES)
    full = pl.BlockSpec(shape, lambda i, *_: (0, 0, 0))
    return pl.pallas_call(
        kernel,
        out_shape=[jax.ShapeDtypeStruct((8 * BLOCK, LANES), BF16)] * 4
        + [
            jax.ShapeDtypeStruct(shape, F32),
            jax.ShapeDtypeStruct(shape, BF16),
            jax.ShapeDtypeStruct(shape, BF16),
            jax.ShapeDtypeStruct((2,) + shape[1:], F32),
        ],
        grid_spec=pltpu.PrefetchScalarGridSpec(
            num_scalar_prefetch=1,
            grid=(8,),
            in_specs=shard_rows()
            + [pl.BlockSpec((1, BLOCK, 8 * BLOCK), lambda i, *_: (i, 0, 0))] * 4
            + [pl.BlockSpec((BLOCK, LANES), lambda i, *_: (i, head // 2))] * 4
            + [pl.BlockSpec(memory_space=pl.ANY)] * 4,
            out_specs=[pl.BlockSpec((BLOCK, LANES), lambda i, *_: (i, 0))] * 4
            + [full, full, full, pl.BlockSpec((2,) + shape[1:], lambda i, *_: (0, 0, 0))],
            scratch_shapes=[
                pltpu.VMEM((3 * blocks + 2,) + shape[1:], BF16),
                pltpu.VMEM((3 * blocks + 2,) + shape[1:], F32),
                pltpu.SemaphoreType.DMA((4,)),
            ],
        ),
        compiler_params=pltpu.CompilerParams(vmem_limit_bytes=VMEM_LIMIT),
        cost_estimate=pl.CostEstimate(
            flops=18_000_000_000, bytes_accessed=1000, transcendentals=0
        ),
        name="attend_backward",
    )(slots, *[queries] * 4, *probs, *grads, *pieces)


def project_heads(token_parts, w_heads, biases, group, shown_at, scale):
    width = w_heads.shape[0]
    rows = token_parts[0].shape[0]
    biases = biases.reshape(4, 192, LANES)

    def kernel(group_ref, at_ref, *refs):
        parts, (w_ref, b_ref) = refs[:4], refs[4:6]
        q_refs, kv_refs, shown_ref = refs[6:9], refs[9:12], refs[12]
        row = lax.broadcasted_iota(jnp.int32, (8, LANES), 0)
        lane = lax.broadcasted_iota(jnp.int32, (8, LANES), 1)
        select = jnp.where(row == lane, 1.0, 0.0).astype(BF16)
        column = jnp.concatenate([b_ref[0], jnp.zeros((64, LANES), BF16)], 0)
        vectors = dot_lanes(select, column)
        left = left_lanes(8)
        for part, ref in enumerate(parts):
            value = matmul(ref[...], w_ref[...])
            for head in range(3):
                side = side_of(head)
                q = half_tile(vectors, head * HEAD_DIM, side)[0:1] * scale
                v = half_tile(vectors, head * HEAD_DIM, 1 - side)[1:2]
                first = left[0:1] if side == 0 else jnp.logical_not(left[0:1])
                q = jnp.where(first, q, 0.0)
                v = jnp.where(first, 0.0, v)
                lanes = slice(head * LANES, (head + 1) * LANES)
                q_refs[head][part * rows : (part + 1) * rows] = (value[:, lanes] + q).astype(BF16)
                lanes = slice((3 + head) * LANES, (4 + head) * LANES)
                kv = (value[:, lanes] + v).astype(BF16).reshape(8, BLOCK, LANES)
                kv_refs[head][part * 8 : (part + 1) * 8] = kv
        for which in range(2):
            at = at_ref[which]
            for head in range(3):
                found = kv_refs[head][jnp.maximum(at, 0)]
                lanes = slice(head * LANES, (head + 1) * LANES)
                shown_ref[which, :, lanes] = jnp.where(at >= 0, found.astype(F32), 0.0).astype(BF16)

    return kernel_call(
        kernel,
        [jax.ShapeDtypeStruct((4 * rows, LANES), BF16)] * 3
        + [jax.ShapeDtypeStruct((32, BLOCK, LANES), BF16)] * 3
        + [jax.ShapeDtypeStruct((2, BLOCK, 3 * LANES), BF16)],
        "project_heads",
        grid_spec=pltpu.PrefetchScalarGridSpec(
            num_scalar_prefetch=2,
            grid=(1,),
            in_specs=[pl.BlockSpec((rows, width), lambda i, *_: (0, 0))] * 4
            + [
                pl.BlockSpec((width, width), lambda i, *_: (0, 0)),
                pl.BlockSpec((1, 192, LANES), lambda i, g, *_: (g[0], 0, 0)),
            ],
            out_specs=[pl.BlockSpec((4 * rows, LANES), lambda i, *_: (0, 0))] * 3
            + [pl.BlockSpec((32, BLOCK, LANES), lambda i, *_: (0, 0, 0))] * 3
            + [pl.BlockSpec((2, BLOCK, 3 * LANES), lambda i, *_: (0, 0, 0))],
        ),
    )(group.reshape(1).astype(jnp.int32), shown_at, *token_parts, w_heads, biases)


def feed_forward(token_group, tokens, cotangent, context, w_output, w_up, w_down, vectors):
    rows, width = tokens.shape
    hidden_width = w_up.shape[1]
    tile = 512
    strip = 128
    group = 2 * LANES
    devices = vectors.shape[0]
    share = width // devices
    pair = 2 * LANES

    def kernel(group_ref, tokens_ref, cot_ref, c0, c1, c2, c3, w_output_ref, w_up_ref, w_down_ref, parts_ref, *refs):
        (
            result_ref,
            grad_ref,
            padded_ref,
            active_ref,
            branch_ref,
            hidden_ref,
            attended_ref,
            joined_ref,
            d0,
            d1,
            d2,
            d3,
            parts_out_ref,
            first,
            normal,
            scale_row,
            slope,
            total,
            w_out_ref,
            vec_ref,
            up_bias_ref,
            sums_ref,
            up_sums_ref,
            low_ref,
        ) = refs
        used = lax.broadcasted_iota(jnp.int32, (strip, group), 1) < 192
        row = lax.broadcasted_iota(jnp.int32, (8, LANES), 0)
        lane = lax.broadcasted_iota(jnp.int32, (8, LANES), 1)
        vec_ref[...] = jnp.zeros(vec_ref.shape, F32)
        up_bias_ref[...] = jnp.zeros(up_bias_ref.shape, F32)
        sums_ref[...] = jnp.zeros(sums_ref.shape, F32)
        up_sums_ref[...] = jnp.zeros(up_sums_ref.shape, F32)
        for d in range(devices):
            part = parts_ref[d, :8].astype(F32)
            for wide, target in ((share, vec_ref), (4 * share, up_bias_ref)):
                tile_start, shift = d * wide // LANES * LANES, d * wide % LANES
                value = jnp.where(lane < wide, part, 0.0)
                value = jnp.concatenate([value, jnp.zeros_like(value)], 1)
                value = pltpu.roll(value, shift, 1) if shift else value
                target[:, tile_start : tile_start + pair] += value
        for k in range(4):
            w_out_ref[k * group : k * group + 192] = w_output_ref[group_ref[0] ^ k]
            w_out_ref[k * group + 192 : (k + 1) * group] = jnp.zeros((group - 192, width), BF16)
        b_output, gain_one, shift_one, b_down, gain_two, shift_two = (
            vec_ref[i : i + 1, :width] for i in range(6)
        )

        def standard(value):
            center = value - jnp.mean(value, -1, keepdims=True)
            spread = jnp.mean(center * center, -1, keepdims=True)
            inverse = lax.rsqrt(spread + NORM_EPS)
            return center * inverse, inverse

        def back(grad, value, inverse, gain):
            inner = grad * gain
            return inverse * (
                inner
                - jnp.mean(inner, -1, keepdims=True)
                - value * jnp.mean(inner * value, -1, keepdims=True)
            )

        for start in range(0, rows, strip):
            at = slice(start, start + strip)
            for k, ref in enumerate((c0, c1, c2, c3)):
                joined_ref[at, k * group : (k + 1) * group] = ref[at]
            value = matmul(joined_ref[at], w_out_ref[...])
            value = tokens_ref[at].astype(F32) + value + b_output
            value, inverse = standard(value)
            normal[at] = value
            scale_row[at] = inverse
            value = value * gain_one + shift_one
            first[at] = value
            low_ref[at] = value.astype(BF16)
            for k in range(4):
                begin, shift = 192 * k // LANES * LANES, 192 * k % LANES
                part = value[:, begin : begin + group]
                part = pltpu.roll(part, group - shift, 1) if shift else part
                part = jnp.where(used, part, 0.0)
                padded_ref[at, k * group : (k + 1) * group] = part.astype(BF16)
        for j in range(0, hidden_width, tile):
            at = slice(j, j + tile)
            x = matmul(low_ref[...], w_up_ref[:, at]) + up_bias_ref[6:7, at]
            square = x * x
            t = jnp.tanh(0.7978845608028654 * (x + 0.044715 * (square * x)))
            cdf = 0.5 + 0.5 * t
            active = (x * cdf).astype(BF16)
            active_ref[:, at] = active
            rise = 0.7978845608028654 * (0.5 + (0.5 * 3.0 * 0.044715) * square)
            slope[:, at] = (cdf + x * (1.0 - t * t) * rise).astype(BF16)
            part = matmul(active, w_down_ref[at])
            total[...] = part if j == 0 else total[...] + part
        gain_sum = jnp.zeros((1, width), F32)
        shift_sum = jnp.zeros((1, width), F32)
        for start in range(0, rows, strip):
            at = slice(start, start + strip)
            value, inverse = standard(first[at] + total[at] + b_down)
            result_ref[at] = (value * gain_two + shift_two).astype(BF16)
            grad = cot_ref[at].astype(F32)
            gain_sum = gain_sum + jnp.sum(grad * value, 0, keepdims=True)
            shift_sum = shift_sum + jnp.sum(grad, 0, keepdims=True)
            value = back(grad, value, inverse, gain_two)
            total[at] = value
            branch_ref[at] = value.astype(BF16)
        ones = jnp.ones((8, rows), BF16)
        sums_ref[3:4, :width] = matmul(ones, branch_ref[...])[0:1]
        sums_ref[4:5, :width] = gain_sum
        sums_ref[5:6, :width] = shift_sum
        for j in range(0, hidden_width, tile):
            at = slice(j, j + tile)
            x = dot_lanes(branch_ref[...], w_down_ref[at])
            x = (x * slope[:, at].astype(F32)).astype(BF16)
            hidden_ref[:, at] = x
            up_sums_ref[:, at] = matmul(ones, x)
            total[...] += dot_lanes(x, w_up_ref[:, at])
        gain_sum = jnp.zeros((1, width), F32)
        shift_sum = jnp.zeros((1, width), F32)
        for start in range(0, rows, strip):
            at = slice(start, start + strip)
            grad = total[at]
            value = normal[at]
            gain_sum = gain_sum + jnp.sum(grad * value, 0, keepdims=True)
            shift_sum = shift_sum + jnp.sum(grad, 0, keepdims=True)
            value = back(grad, value, scale_row[at], gain_one)
            grad_ref[at] = value
            attended_ref[at] = value.astype(BF16)
        sums_ref[0:1, :width] = matmul(ones, attended_ref[...])[0:1]
        sums_ref[1:2, :width] = gain_sum
        sums_ref[2:3, :width] = shift_sum
        for k, ref in enumerate((d0, d1, d2, d3)):
            ref[...] = dot_lanes(attended_ref[...], w_out_ref[k * group : (k + 1) * group]).astype(BF16)
        for d in range(devices):
            found = []
            for wide, source in ((share, sums_ref), (4 * share, up_sums_ref)):
                tile_start, shift = d * wide // LANES * LANES, d * wide % LANES
                value = source[:, tile_start : tile_start + pair]
                value = pltpu.roll(value, pair - shift, 1) if shift else value
                found.append(jnp.where(lane < wide, value[:, :LANES], 0.0))
            parts_out_ref[d] = jnp.where(row < 6, found[0], jnp.where(row == 6, found[1], 0.0))

    def shape(columns, kind=BF16):
        return jax.ShapeDtypeStruct((rows, columns), kind)

    return kernel_call(
        kernel,
        [
            shape(width),
            shape(width, F32),
            shape(4 * group),
            shape(hidden_width),
            shape(width),
            shape(hidden_width),
            shape(width),
            shape(4 * group),
        ]
        + [shape(group)] * 4
        + [jax.ShapeDtypeStruct((devices, 8, LANES), F32)],
        "feed_forward",
        30_000_000_000,
        in_specs=[smem()] + whole(10),
        out_specs=whole(13),
        scratch_shapes=[
            pltpu.VMEM((rows, width), F32),
            pltpu.VMEM((rows, width), F32),
            pltpu.VMEM((rows, 1), F32),
            pltpu.VMEM((rows, hidden_width), BF16),
            pltpu.VMEM((rows, width), F32),
            pltpu.VMEM((4 * group, width), BF16),
            pltpu.VMEM((8, width + LANES), F32),
            pltpu.VMEM((8, hidden_width + LANES), F32),
            pltpu.VMEM((8, width + LANES), F32),
            pltpu.VMEM((8, hidden_width + LANES), F32),
            pltpu.VMEM((rows, width), BF16),
        ],
    )(
        token_group.reshape(1).astype(jnp.int32),
        tokens,
        cotangent,
        *context,
        w_output,
        w_up,
        w_down,
        vectors,
    )


def local_block(place, within):
    shard = within // 8
    return (((shard % 2) ^ place.h) * 2 + ((shard // 2) ^ place.x)) * 8 + within % 8


def doc_number(positions, starts):
    return jnp.sum((positions[..., None] >= starts).astype(jnp.int32), -1)


def slot_tables(place, global_blocks, random_parts, starts):
    ring = 2 * place.slabs
    half = 2 * place.n + place.c
    total = ring * 32
    found = []
    for arrived in random_parts:
        found.append(lax.dynamic_slice_in_dim(arrived, 3 * place.x, 3, 0).reshape(3, 2, 8, 3))
    chosen = jnp.stack(found, 2)
    chosen = jnp.where(place.h == 0, chosen, chosen[:, ::-1]).reshape(3, 32, 3)
    order = jnp.arange(32, dtype=jnp.int32)
    shard = order // 8
    query_ids = half * 32 + (((shard % 2) ^ place.x) * 2 + ((shard // 2) ^ place.h)) * 8 + order % 8
    near = (query_ids[:, None] + jnp.arange(-1, 2, dtype=jnp.int32)) % total
    ids = jnp.concatenate(
        [
            jnp.broadcast_to(near[None], (3, 32, 3)),
            jnp.broadcast_to(global_blocks, (3, 32, 2)),
            chosen,
        ],
        -1,
    )
    earlier = jnp.arange(8)[None, :] < jnp.arange(8)[:, None]
    repeated = jnp.any((ids[..., :, None] == ids[..., None, :]) & earlier, -1)
    distance = (ids // 32 - half) % ring
    region = jnp.where(distance == 0, 0, jnp.where(distance == 1, 1, 2))
    local = region * 32 + local_block(place, ids % 32)
    which = jnp.arange(8, dtype=jnp.int32)
    slots = jnp.where((which == 3) | (which == 4), 93 + which, local)
    marked = jnp.where(repeated, -1, ids)
    token = jnp.arange(BLOCK, dtype=jnp.int32)
    query_doc = doc_number(query_ids[:, None] * BLOCK + token, starts).reshape(32 * BLOCK, 1)
    key_doc = doc_number(marked[..., None] * BLOCK + token, starts)
    return (
        slots.reshape(-1).astype(jnp.int32),
        jnp.broadcast_to(query_doc, (32 * BLOCK, LANES)),
        key_doc.reshape(96, 1, 8 * BLOCK),
    )


def body(
    tokens,
    cotangent,
    doc_lengths,
    global_blocks,
    random_blocks,
    query_weight,
    query_bias,
    key_weight,
    value_weight,
    value_bias,
    output_weight,
    output_bias,
    first_gain,
    first_shift,
    up_weight,
    up_bias,
    down_weight,
    down_bias,
    second_gain,
    second_shift,
):
    place = Place()
    slabs = place.slabs
    devices = 8 * slabs
    width = tokens.shape[1]
    share = query_weight.shape[0]
    hidden_width = up_weight.shape[1]
    scale = HEAD_DIM ** (-0.5)
    group = place.h * 2 + place.x
    token_group = place.h * 2 + place.c

    biases = jnp.pad(jnp.stack([query_bias, value_bias], 1), ((0, 0), (0, LANES - 2)))
    groups = pack_heads(query_weight, key_weight, value_weight, biases, scale)
    parts = [pick(groups, group)] + [
        place.across(pick(groups, group ^ (2 * i + j)), i, j) for i, j in PAIRS[1:]
    ]
    vectors = [
        output_bias, first_gain, first_shift, down_bias, second_gain, second_shift, up_bias
    ]
    random_late = after(random_blocks, groups)
    random_parts = [place.to_heads(random_late, 0, j) for j in range(2)]
    *parts, random_parts[0], random_parts[1] = lax.optimization_barrier((*parts, *random_parts))
    stacked = stack_heads(parts)
    packed = pack_rest(after(up_weight, stacked), down_weight, output_weight, vectors)
    tokens_late = after(tokens, stacked)
    token_parts = [place.to_heads(tokens_late, i, j) for i, j in PAIRS]
    column = [stacked] + [place.along_slabs(stacked, k) for k in range(1, slabs)]
    which = jnp.arange(doc_lengths.shape[0])
    before = which[None, :] < which[:, None]
    starts = jnp.sum(jnp.where(before, doc_lengths[None, :], 0), 1).astype(jnp.int32)
    slots, query_doc, key_doc = slot_tables(place, global_blocks, random_parts, starts)
    packed, *column = lax.optimization_barrier((packed, *column))
    heads_column = jnp.stack(column)
    heads_column, slots, query_doc, key_doc, *token_parts = lax.optimization_barrier(
        (heads_column, slots, query_doc, key_doc, *token_parts)
    )
    other, *token_parts = lax.optimization_barrier((place.sibling(heads_column), *token_parts))
    arrived, bias = assemble_heads(place, heads_column, other)
    w_heads = arrived.reshape(width, width)
    packed_column = exchange(jnp.broadcast_to(packed, (slabs,) + packed.shape), "slab")
    half = 2 * place.n + place.c
    global_at = local_block(place, global_blocks % 32)
    shown_at = jnp.where(global_blocks // 32 == half, global_at, -1).astype(jnp.int32)
    found = project_heads(token_parts, w_heads, bias, group, shown_at, scale)
    queries, own, shown = found[:3], found[3:6], found[6]
    shown = shown + place.sibling(shown)
    shown, *own = lax.optimization_barrier((shown, *own))
    mine = pick(shown, place.c)
    for k in range(1, slabs):
        mine = mine + place.along_slabs(pick(shown, place.c), k)
    following, previous = [], []

    def send_halo(kv):
        following.append(place.to_previous(kv))
        previous.append(place.to_next(kv))

    send_halo(own[0])
    late, mine, following[0], previous[0] = lax.optimization_barrier(
        (own[1], mine, following[0], previous[0])
    )
    send_halo(late)
    theirs = place.sibling(mine)
    shared = jnp.where(place.c == 0, jnp.stack([mine, theirs]), jnp.stack([theirs, mine]))

    packed_column = after(packed_column, own[0])
    rest_column = exchange(jnp.broadcast_to(packed_column, (4,) + packed_column.shape), CHIPS)

    pieces, probs, context, table = [], [], None, slots
    for head in range(3):
        lanes = slice(head * LANES, (head + 1) * LANES)
        pieces.append((own[head], following[head], previous[head], shared[:, :, lanes]))
        found = attend_forward(table, query_doc, key_doc, queries[head], pieces[head], head, context)
        context = found[:4]
        if head == 0:
            send_halo(after(own[2], context[0]))
        probs.append(found[4:])
        table = after(table, context[0])
    mine = after(rest_column, context[0])
    other = place.sibling(mine)
    sent = [place.to_tokens(c, i, j) for c, (i, j) in zip(context, PAIRS)]
    w_up, w_down, w_output, rest = assemble_rest(place, mine, other, share)
    w_up = w_up.reshape(width, hidden_width)
    w_down = w_down.reshape(hidden_width, width)
    w_output = w_output.reshape(4, 192, width)
    found = feed_forward(token_group, tokens, cotangent, sent, w_output, w_up, w_down, rest)
    result, first_grad, first_low, active_low, branch_grad, hidden_low, attended_grad, context_tok = found[:8]
    context_grad, vector_grads = found[8:12], found[12]
    context_grads = [place.to_heads(part, i, j) for part, (i, j) in zip(context_grad, PAIRS)]

    kept, sent = weight_grads(
        place,
        active_low,
        branch_grad,
        first_low,
        hidden_low,
        context_tok,
        attended_grad,
        vector_grads,
    )
    rest_state = (kept, place.sibling(sent))

    def head_backward(head, table):
        found = attend_backward(
            table, queries[head], probs[head], context_grads, pieces[head], head
        )
        return found[:4], found[4:]

    def halo(found):
        own_grad, next_grad, prev_grad, _ = found
        return own_grad, place.to_next(next_grad), place.to_previous(prev_grad)

    rest_parts = scatter_across(place, *rest_state)
    table = after(slots, rest_parts)
    rest_parts = exchange(rest_parts, CHIPS)
    results, halos = [], []
    results.append(head_backward(0, table))
    halos.append(halo(results[0][1]))
    table = after(table, results[0][1][3])
    results.append(head_backward(1, table))
    halos.append(halo(results[1][1]))

    def ring_slabs(grads):
        low = grads.astype(BF16)
        total = grads
        for k in range(1, slabs):
            total = total + place.along_slabs(low, k).astype(F32)
        return total

    table, _, *first = lax.optimization_barrier((table, results[1][1][3], *halos[0][1:]))
    halos[0] = (halos[0][0], *first)
    dqs, found = head_backward(2, table)
    first, second, *found = lax.optimization_barrier((*halos[1][1:], *found))
    halos[1] = (halos[1][0], first, second)
    results.append((dqs, found))
    halos.append(halo(found))
    ring_sum = ring_slabs(jnp.concatenate([results[head][1][3] for head in range(3)], -1))
    rest_last = scatter_slabs(after(rest_parts, found[3]))
    ring_sum, first, second, rest_last = lax.optimization_barrier(
        (ring_sum, *halos[2][1:], rest_last)
    )
    halos[2] = (halos[2][0], first, second)
    ring_sum = ring_sum + place.sibling(ring_sum.astype(BF16)).astype(F32)
    global_at = jnp.where(
        global_blocks // 32 == half, local_block(place, global_blocks % 32), -100
    ).astype(jnp.int32)

    global_at = after(global_at, rest_last)
    rest_last = exchange(rest_last, "slab")
    *heads_grads, bias_grad = join_heads(results, halos, ring_sum, global_at)
    kept, sent = heads_weight_grads(place, token_parts, heads_grads, bias_grad)
    *heads_grads, _ = lax.optimization_barrier((*heads_grads, kept))
    late = [dot_lanes(grad, w_heads).astype(BF16) for grad in heads_grads[2:]]
    *early, _ = lax.optimization_barrier((*heads_grads[:2], *late))[:3]
    early = [dot_lanes(grad, w_heads).astype(BF16) for grad in early]
    returned = [place.to_tokens(part, *pair) for part, pair in zip(early + late, PAIRS)]
    arrived = place.sibling(sent)
    arrived, rest_last = lax.optimization_barrier((arrived, rest_last))
    chunks = group_along(place, kept, arrived)
    chunks, *returned = lax.optimization_barrier((chunks, *returned))
    group_parts = group_across(chunks)
    tokens_grad = first_grad
    for part in returned:
        tokens_grad = tokens_grad + part.astype(F32)
    query_all, key_all, value_all, bias_sums = finish_heads(group_parts, share, scale)
    start = share * (place.h * 4 * slabs + 4 * place.n + 2 * place.x + place.c)
    bias_share = lax.dynamic_slice_in_dim(bias_sums, start, share, 1)
    query_bias_share, value_bias_share = bias_share[0], bias_share[1]
    rest_share = jnp.sum(rest_last.astype(F32), 0)
    up_share = jnp.concatenate([rest_share[i * share : (i + 1) * share] for i in range(4)], 1)
    down_share = rest_share[4 * share : 8 * share]
    output_share = rest_share[8 * share : 9 * share]
    pieces_of = [rest_share[9 * share + i, :share] for i in range(6)]

    return (
        result,
        tokens_grad,
        query_all,
        query_bias_share,
        key_all,
        value_all,
        value_bias_share,
        output_share,
        pieces_of[0],
        pieces_of[1],
        pieces_of[2],
        up_share,
        rest_share[9 * share + 6, : 4 * share],
        down_share,
        pieces_of[3],
        pieces_of[4],
        pieces_of[5],
    )


def solution(mesh):
    devices = mesh.devices
    mesh = Mesh(devices.reshape(devices.shape[0], -1, 2, 2), AXES)
    rows = P(AXES, None)
    vector = P(AXES)
    tokens = P(("slab", "x", "core", "head"), None)
    return jax.shard_map(
        body,
        mesh=mesh,
        in_specs=(
            tokens,
            tokens,
            P(),
            P(),
            P("head", ("slab", "x", "core"), None),
            rows,
            vector,
            rows,
            rows,
            vector,
            rows,
            vector,
            vector,
            vector,
            rows,
            vector,
            rows,
            vector,
            vector,
            vector,
        ),
        out_specs=(
            tokens,
            tokens,
            rows,
            vector,
            rows,
            rows,
            vector,
            rows,
            vector,
            vector,
            vector,
            rows,
            vector,
            rows,
            vector,
            vector,
            vector,
        ),
        check_vma=False,
    )
```

```python
import jax
import jax.numpy as jnp
from jax import lax
from jax.experimental import pallas as pl
from jax.experimental.pallas import tpu as pltpu
from jax.sharding import Mesh
from jax.sharding import PartitionSpec as P

HEAD_DIM = 64
BLOCK = 64
LANES = 128
NORM_EPS = 1e-06
MASKED = -1e30
AXES = ("head", "slab", "x", "core")
CHIPS = ("head", "x")
BF16 = jnp.bfloat16
F32 = jnp.float32
PAIRS = ((0, 0), (0, 1), (1, 0), (1, 1))
VMEM_LIMIT = 60 * 1024 * 1024


def matmul(left, right):
    return jnp.dot(left, right, preferred_element_type=F32)


def dot_rows(left, right):
    return lax.dot_general(left, right, (((0,), (0,)), ((), ())), preferred_element_type=F32)


def dot_lanes(left, right):
    return lax.dot_general(left, right, (((1,), (1,)), ((), ())), preferred_element_type=F32)


class Place:
    def __init__(self):
        self.slabs = lax.axis_size("slab")
        self.size = 4 * self.slabs
        self.h, self.n, self.x, self.c = (lax.axis_index(axis) for axis in AXES)

    def send(self, value, target):
        def index(h, n, x, c):
            return h * self.size + 4 * n + 2 * x + c

        route = [
            (index(h, n, x, c), index(*target(h, n, x, c)))
            for h in range(2)
            for n in range(self.slabs)
            for x in range(2)
            for c in range(2)
        ]
        return lax.ppermute(value, AXES, route)

    def along_slabs(self, value, k):
        return self.send(value, lambda h, n, x, c: (h, n ^ k, x, c))

    def across(self, value, i, j):
        return self.send(value, lambda h, n, x, c: (h ^ i, n, x ^ j, c))

    def sibling(self, value):
        return self.send(value, lambda h, n, x, c: (h, n, x, 1 - c))

    def to_heads(self, value, i, j):
        return self.send(value, lambda h, n, x, c: (h ^ i, n, c ^ j, x))

    def to_tokens(self, value, i, j):
        return self.send(value, lambda h, n, x, c: (h ^ i, n, c, x ^ j))

    def to_next(self, value):
        def target(h, n, x, c):
            return (h, n, x, 1) if c == 0 else (h, (n + 1) % self.slabs, x, 0)

        return self.send(value, target)

    def to_previous(self, value):
        def target(h, n, x, c):
            return (h, n, x, 0) if c == 1 else (h, (n - 1) % self.slabs, x, 1)

        return self.send(value, target)


def exchange(value, axes):
    return lax.all_to_all(value, axes, split_axis=0, concat_axis=0, tiled=True)


def pick(value, index, axis=0):
    return lax.dynamic_index_in_dim(value, index, axis, keepdims=False)


def kernel_call(kernel, out_shape, name, flops=1000, **options):
    return pl.pallas_call(
        kernel,
        out_shape=out_shape,
        compiler_params=pltpu.CompilerParams(vmem_limit_bytes=VMEM_LIMIT),
        cost_estimate=pl.CostEstimate(
            flops=flops, bytes_accessed=1000, transcendentals=0
        ),
        name=name,
        **options,
    )


def whole(count):
    return [pl.BlockSpec(memory_space=pltpu.VMEM)] * count


def smem():
    return pl.BlockSpec(memory_space=pltpu.SMEM)


def after(value, *others):
    return lax.optimization_barrier((value,) + others)[0]


def side_of(head):
    return 1 - head % 2


def half_tile(value, start, side):
    tile = start // LANES * LANES
    found = value[:, tile : tile + LANES].astype(F32)
    if (start % LANES) // HEAD_DIM != side:
        found = pltpu.roll(found, HEAD_DIM, 1)
    return found


def left_lanes(rows):
    return lax.broadcasted_iota(jnp.int32, (rows, LANES), 1) < HEAD_DIM


def pack_heads(query_weight, key_weight, value_weight, biases, scale):
    share = query_weight.shape[0]

    def kernel(q_ref, k_ref, v_ref, b_ref, out_ref):
        left = left_lanes(share)
        for group in range(4):
            start = 3 * group * HEAD_DIM
            q = [half_tile(q_ref, start + t * HEAD_DIM, side_of(t)) * scale for t in range(3)]
            out_ref[group, :, :LANES] = jnp.where(left, q[1], q[0]).astype(BF16)
            extra = b_ref[...].astype(F32)
            out_ref[group, :, LANES : 2 * LANES] = jnp.where(left, extra, q[2]).astype(BF16)
            for t in range(3):
                side = side_of(t)
                k = half_tile(k_ref, start + t * HEAD_DIM, side)
                v = half_tile(v_ref, start + t * HEAD_DIM, 1 - side)
                both = jnp.where(left, k, v) if side == 0 else jnp.where(left, v, k)
                out_ref[group, :, (2 + t) * LANES : (3 + t) * LANES] = both.astype(BF16)

    return kernel_call(
        kernel,
        jax.ShapeDtypeStruct((4, share, 5 * LANES), BF16),
        "pack_heads",
        in_specs=whole(4),
        out_specs=whole(1)[0],
    )(query_weight, key_weight, value_weight, biases)


def pack_rest(up, down, output, vectors):
    share, width = output.shape
    height = -(-(9 * share + 8) // 16) * 16
    count = len(vectors)

    def kernel(up_ref, down_ref, output_ref, *refs):
        out_ref, held = refs[-2:]
        for i in range(4):
            out_ref[i * share : (i + 1) * share] = up_ref[:, i * width : (i + 1) * width]
        out_ref[4 * share : 8 * share] = down_ref[...]
        out_ref[8 * share : 9 * share] = output_ref[...]
        held[...] = jnp.zeros(held.shape, F32)
        for i, ref in enumerate(refs[:count]):
            held[i : i + 1, : ref.shape[1]] = ref[...].astype(F32)
        out_ref[9 * share :, :LANES] = held[...].astype(BF16)
        out_ref[9 * share :, LANES:] = jnp.zeros((height - 9 * share, width - LANES), BF16)

    vectors = [v[None] for v in vectors]
    return kernel_call(
        kernel,
        jax.ShapeDtypeStruct((height, width), BF16),
        "pack_rest",
        in_specs=whole(3 + count),
        out_specs=whole(1)[0],
        scratch_shapes=[pltpu.VMEM((height - 9 * share, LANES), F32)],
    )(up, down, output, *vectors)


def stack_heads(parts):
    def kernel(*refs):
        for k, ref in enumerate(refs[:-1]):
            refs[-1][k] = ref[...]

    return kernel_call(
        kernel,
        jax.ShapeDtypeStruct((len(parts),) + parts[0].shape, BF16),
        "stack_heads",
        in_specs=whole(len(parts)),
        out_specs=whole(1)[0],
    )(*parts)


def assemble_heads(place, column, other):
    slabs, _, rows, columns = column.shape
    where = jnp.stack([place.h, place.n, place.x, place.c]).astype(jnp.int32)

    def kernel(where_ref, mine_ref, other_ref, out_ref, bias_ref):
        h, x, c = where_ref[0], where_ref[2], where_ref[3]
        left = left_lanes(rows)
        right = jnp.logical_not(left)
        for core, ref in enumerate((mine_ref, other_ref)):
            for p, (i, j) in enumerate(PAIRS):
                first = ref[0, p, :, :LANES].astype(F32)
                second = ref[0, p, :, LANES : 2 * LANES]
                q = (
                    jnp.where(right, first, 0.0),
                    jnp.where(left, first, 0.0),
                    jnp.where(right, second.astype(F32), 0.0),
                )
                at = (h ^ i, 0, x ^ j, c ^ core)
                for t in range(3):
                    out_ref[(*at, slice(None), slice(t * LANES, (t + 1) * LANES))] = q[t].astype(BF16)
                out_ref[(*at, slice(None), slice(3 * LANES, 6 * LANES))] = ref[0, p, :, 2 * LANES :]
                bias_ref[at] = second

    found = kernel_call(
        kernel,
        (
            jax.ShapeDtypeStruct((2, slabs, 2, 2, rows, 6 * LANES), BF16),
            jax.ShapeDtypeStruct((2, slabs, 2, 2, rows, LANES), BF16),
        ),
        "assemble_heads",
        grid_spec=pltpu.PrefetchScalarGridSpec(
            num_scalar_prefetch=1,
            grid=(slabs,),
            in_specs=[pl.BlockSpec((1, 4, rows, columns), lambda k, w: (k, 0, 0, 0))] * 2,
            out_specs=[
                pl.BlockSpec((2, 1, 2, 2, rows, 6 * LANES), lambda k, w: (0, k ^ w[1], 0, 0, 0, 0)),
                pl.BlockSpec((2, 1, 2, 2, rows, LANES), lambda k, w: (0, k ^ w[1], 0, 0, 0, 0)),
            ],
        ),
    )(where, column, other)
    return [value.reshape(8 * slabs, *value.shape[4:]) for value in found]


def assemble_rest(place, mine, other, share):
    _, slabs, rows, width = mine.shape
    where = place.c.reshape(1).astype(jnp.int32)

    def kernel(where_ref, mine_ref, other_ref, up_ref, down_ref, output_ref, vector_ref):
        for core, ref in ((where_ref[0], mine_ref), (1 - where_ref[0], other_ref)):
            for p in range(4):
                at = (p // 2, 0, p % 2, core)
                for q in range(4):
                    columns = slice(q * width, (q + 1) * width)
                    up_ref[(*at, slice(None), columns)] = ref[p, 0, q * share : (q + 1) * share]
                down_ref[at] = ref[p, 0, 4 * share : 8 * share]
                output_ref[at] = ref[p, 0, 8 * share : 9 * share]
                vector_ref[at] = ref[p, 0, 9 * share :, :LANES]

    shapes = ((share, 4 * width), (4 * share, width), (share, width), (rows - 9 * share, LANES))
    found = kernel_call(
        kernel,
        tuple(jax.ShapeDtypeStruct((2, slabs, 2, 2) + shape, BF16) for shape in shapes),
        "assemble_rest",
        20_000_000_000,
        grid_spec=pltpu.PrefetchScalarGridSpec(
            num_scalar_prefetch=1,
            grid=(slabs,),
            in_specs=[pl.BlockSpec((4, 1, rows, width), lambda n, w: (0, n, 0, 0))] * 2,
            out_specs=[
                pl.BlockSpec((2, 1, 2, 2) + shape, lambda n, w: (0, n, 0, 0, 0, 0)) for shape in shapes
            ],
        ),
    )(where, mine, other)
    return [value.reshape(8 * slabs, *value.shape[4:]) for value in found]


def weight_grads(place, active, branch_grad, first, hidden_grad, context, attended_grad, vectors):
    devices = 8 * place.slabs
    step = devices // 4
    tokens, width = branch_grad.shape
    share = width // devices
    rows = -(-(9 * share + 8) // 16) * 16
    where = jnp.stack([place.h * 2 + place.c, place.c]).astype(jnp.int32)

    def kernel(where_ref, active_ref, branch_ref, first_ref, hidden_ref, context_ref, attended_ref, vector_ref, kept_ref, sent_ref):
        even = where_ref[1] == 0

        def put(start, stop, value):
            value = value.astype(BF16).reshape(step, stop - start, width)
            for p in range(step // 2):
                kept_ref[p, start:stop] = jnp.where(even, value[2 * p], value[2 * p + 1])
                sent_ref[p, start:stop] = jnp.where(even, value[2 * p + 1], value[2 * p])

        put(4 * share, 8 * share, dot_rows(active_ref[...], branch_ref[...]))
        columns = first_ref[...]
        for q in range(4):
            up = dot_rows(columns, hidden_ref[:, q * width : (q + 1) * width])
            put(q * share, (q + 1) * share, up[: step * share])
        put(8 * share, 9 * share, dot_rows(context_ref[...], attended_ref[...])[: step * share])
        for p in range(step // 2):
            for ref, at in ((kept_ref, 2 * p + where_ref[1]), (sent_ref, 2 * p + 1 - where_ref[1])):
                ref[p, 9 * share :] = jnp.zeros((rows - 9 * share, width), BF16)
                ref[p, 9 * share : 9 * share + 8, :LANES] = vector_ref[at].astype(BF16)

    half = jax.ShapeDtypeStruct((devices // 2, rows, width), BF16)
    return kernel_call(
        kernel,
        (half, half),
        "weight_grads",
        15_000_000_000,
        grid_spec=pltpu.PrefetchScalarGridSpec(
            num_scalar_prefetch=1,
            grid=(4,),
            in_specs=[
                pl.BlockSpec((tokens, width), lambda g, w: (0, g)),
                pl.BlockSpec((tokens, width), lambda g, w: (0, 0)),
                pl.BlockSpec((tokens, 256), lambda g, w: (0, g)),
                pl.BlockSpec((tokens, 4 * width), lambda g, w: (0, 0)),
                pl.BlockSpec((tokens, 256), lambda g, w: (0, g ^ w[0])),
                pl.BlockSpec((tokens, width), lambda g, w: (0, 0)),
                pl.BlockSpec((step, 8, LANES), lambda g, w: (g, 0, 0)),
            ],
            out_specs=[pl.BlockSpec((step // 2, rows, width), lambda g, w: (g, 0, 0))] * 2,
        ),
    )(where, active, branch_grad, first, hidden_grad, context, attended_grad, vectors)


def heads_weight_grads(place, token_parts, heads_grads, bias_grad):
    slabs = place.slabs
    width = token_parts[0].shape[1]
    share = width // (8 * slabs)
    rows = max(share, 8)
    where = place.c.reshape(1).astype(jnp.int32)

    def kernel(where_ref, *refs):
        x_refs, g_refs, bias_ref, kept_ref, sent_ref = refs[:4], refs[4:8], *refs[8:]
        even = where_ref[0] == 0
        left = left_lanes(rows)
        row = lax.broadcasted_iota(jnp.int32, (rows, LANES), 0)
        extra = jnp.zeros((rows, LANES), F32)
        for which in range(6):
            head = which % 3
            if which < 3:
                start = head * LANES + side_of(head) * HEAD_DIM
            else:
                start = (3 + head) * LANES + (1 - side_of(head)) * HEAD_DIM
            value = jnp.broadcast_to(half_tile(bias_ref, start, 0)[0:1], (rows, LANES))
            extra = jnp.where(row == which, value, extra)

        def put(start, stop, value):
            value = value.astype(BF16).reshape(8 * slabs, share, stop - start)
            if rows > share:
                value = jnp.concatenate(
                    [value, jnp.zeros((8 * slabs, rows - share, stop - start), BF16)], 1
                )
            for p in range(4 * slabs):
                first, second = value[2 * p], value[2 * p + 1]
                if start == LANES:
                    first = jnp.where(left, extra, first.astype(F32)).astype(BF16)
                    second = jnp.where(left, extra, second.astype(F32)).astype(BF16)
                kept_ref[p, :, start:stop] = jnp.where(even, first, second)
                sent_ref[p, :, start:stop] = jnp.where(even, second, first)

        def product(start, stop):
            return sum(
                dot_rows(x_ref[...], g_ref[:, start:stop]) for x_ref, g_ref in zip(x_refs, g_refs)
            )

        q = product(0, 3 * LANES)
        put(0, LANES, q[:, :LANES] + q[:, LANES : 2 * LANES])
        put(LANES, 2 * LANES, q[:, 2 * LANES :])
        put(2 * LANES, 5 * LANES, product(3 * LANES, 6 * LANES))

    half = jax.ShapeDtypeStruct((4 * slabs, rows, 5 * LANES), BF16)
    return kernel_call(
        kernel,
        (half, half),
        "heads_weight_grads",
        in_specs=[smem()] + whole(9),
        out_specs=whole(2),
    )(where, *token_parts, *heads_grads, bias_grad)


def scatter_across(place, kept, arrived):
    slabs = place.slabs
    _, rows, width = kept.shape

    def kernel(kept_ref, arrived_ref, out_ref):
        for h in range(2):
            for x in range(2):
                total = kept_ref[h, 0, x].astype(F32) + arrived_ref[h, 0, x].astype(F32)
                out_ref[2 * h + x, 0] = total.astype(BF16)

    parts = kernel_call(
        kernel,
        jax.ShapeDtypeStruct((4, slabs, rows, width), BF16),
        "scatter_across",
        grid=(slabs,),
        in_specs=[pl.BlockSpec((2, 1, 2, rows, width), lambda n: (0, n, 0, 0, 0))] * 2,
        out_specs=pl.BlockSpec((4, 1, rows, width), lambda n: (0, n, 0, 0)),
    )(*(value.reshape(2, slabs, 2, rows, width) for value in (kept, arrived)))
    return parts


def scatter_slabs(parts):
    slabs, rows, width = parts.shape[1:]

    def kernel(ref, out_ref):
        out_ref[0] = sum(ref[p, 0].astype(F32) for p in range(4)).astype(BF16)

    total = kernel_call(
        kernel,
        jax.ShapeDtypeStruct((slabs, rows, width), BF16),
        "scatter_slabs",
        20_000_000_000,
        grid=(slabs,),
        in_specs=[pl.BlockSpec((4, 1, rows, width), lambda n: (0, n, 0, 0))],
        out_specs=pl.BlockSpec((1, rows, width), lambda n: (n, 0, 0)),
    )(parts)
    return total


def added(parts):
    return sum(part.astype(F32) for part in parts)


def group_along(place, kept, arrived):
    slabs = place.slabs
    _, rows, width = kept.shape

    def kernel(kept_ref, arrived_ref, out_ref):
        for h in range(2):
            for n in range(slabs):
                for x in range(2):
                    pair = kept_ref[h, n, x].astype(F32) + arrived_ref[h, n, x].astype(F32)
                    out_ref[n, 2 * h + x] = pair.astype(BF16)

    parts = kernel_call(
        kernel,
        jax.ShapeDtypeStruct((slabs, 4, rows, width), BF16),
        "group_along",
        in_specs=whole(2),
        out_specs=whole(1)[0],
    )(*(value.reshape(2, slabs, 2, rows, width) for value in (kept, arrived)))
    return exchange(parts, "slab")


def group_across(parts):
    slabs, _, rows, width = parts.shape

    def kernel(ref, out_ref):
        for p in range(4):
            out_ref[p] = sum(ref[n, p].astype(F32) for n in range(slabs)).astype(BF16)

    total = kernel_call(
        kernel,
        jax.ShapeDtypeStruct((4, rows, width), BF16),
        "group_across",
        in_specs=whole(1),
        out_specs=whole(1)[0],
    )(parts)
    return exchange(total, CHIPS)


def finish_heads(parts, share, scale):
    _, rows, _ = parts.shape
    width = 12 * HEAD_DIM

    def kernel(ref, q_ref, k_ref, v_ref, bias_ref):
        left = left_lanes(rows)
        bias_ref[...] = jnp.zeros(bias_ref.shape, F32)
        for which, out in enumerate((q_ref, k_ref, v_ref)):
            for tile in range(width // LANES):
                sides, sums = [], []
                for side in range(2):
                    head = 2 * tile + side
                    value = ref[head // 3]
                    t = head % 3
                    if which == 0:
                        start = (t // 2) * LANES + side_of(t) * HEAD_DIM
                    else:
                        at = side_of(t) if which == 1 else 1 - side_of(t)
                        start = (2 + t) * LANES + at * HEAD_DIM
                    sides.append(half_tile(value, start, side))
                    row = t if which == 0 else 3 + t
                    sums.append(half_tile(value, LANES, side)[row : row + 1])
                value = jnp.where(left, sides[0], sides[1])
                bias = jnp.where(left[0:1], sums[0], sums[1])
                if which == 0:
                    value, bias = value * scale, bias * scale
                lanes = slice(tile * LANES, (tile + 1) * LANES)
                out[:, lanes] = value[:share]
                if which != 1:
                    bias_ref[which // 2 : which // 2 + 1, lanes] = bias

    weight = jax.ShapeDtypeStruct((share, width), F32)
    return kernel_call(
        kernel,
        (weight, weight, weight, jax.ShapeDtypeStruct((8, width), F32)),
        "finish_heads",
        in_specs=whole(1),
        out_specs=whole(4),
    )(parts)


def join_heads(results, halos, ring_sum, global_at):
    dqs = [results[head][0][u] for u in range(4) for head in range(3)]
    owns = [halos[head][0] for head in range(3)]
    arrived = [halos[head][side] for head in range(3) for side in (1, 2)]
    rows, width = 8 * BLOCK, 6 * LANES

    def kernel(at_ref, *refs):
        dq_refs, own_refs, arrived_refs, ring_ref = refs[:12], refs[12:15], refs[15:21], refs[21]
        out_refs, bias_ref = refs[22:26], refs[26]

        def total(head, blocks):
            return (
                own_refs[head][blocks]
                + arrived_refs[2 * head][blocks].astype(F32)
                + arrived_refs[2 * head + 1][blocks].astype(F32)
            )

        bias = jnp.zeros((8, width), F32)
        for u in range(4):
            out = out_refs[u]
            for head in range(3):
                out[:, head * LANES : (head + 1) * LANES] = dq_refs[3 * u + head][...]
                lanes = slice((3 + head) * LANES, (4 + head) * LANES)
                value = total(head, slice(u * 8, (u + 1) * 8))
                out[:, lanes] = value.reshape(rows, LANES).astype(BF16)
            for which in range(2):
                at = at_ref[which] - 8 * u

                @pl.when((at >= 0) & (at < 8))
                def _():
                    block = jnp.clip(at, 0, 7)
                    row = pl.ds(pl.multiple_of(block * BLOCK, BLOCK), BLOCK)
                    for head in range(3):
                        lanes = slice(head * LANES, (head + 1) * LANES)
                        value = total(head, 8 * u + block)
                        for i in range(2):
                            same = at_ref[i] == at_ref[which]
                            value = value + jnp.where(same, ring_ref[i, :, lanes], 0.0)
                        out[row, (3 + head) * LANES : (4 + head) * LANES] = value.astype(BF16)

            bias = bias + matmul(jnp.ones((8, rows), BF16), out[...])
        bias_ref[...] = bias

    return kernel_call(
        kernel,
        [jax.ShapeDtypeStruct((rows, width), BF16)] * 4 + [jax.ShapeDtypeStruct((8, width), F32)],
        "join_heads",
        in_specs=[smem()] + whole(22),
        out_specs=whole(5),
    )(global_at, *dqs, *owns, *arrived, ring_sum)


def copy_all(sources, target, sems):
    copies = []
    start = 0
    for which, source in enumerate(sources):
        stop = start + source.shape[0]
        copies.append(pltpu.make_async_copy(source, target.at[start:stop], sems.at[which]))
        start = stop
    for copy in copies:
        copy.start()
    return copies


def shard_rows(column=0):
    return [pl.BlockSpec((BLOCK, LANES), lambda i, *_, u=u: (8 * u + i, column)) for u in range(4)]


def attend_forward(slots, query_doc, key_doc, queries, pieces, head, context=None):
    blocks = 32
    joined = 0 if context is None else 4
    columns = LANES if head < 2 else 2 * LANES

    def kernel(slots_ref, *refs):
        doc_refs, key_refs, q_refs = refs[:4], refs[4:8], refs[8:12]
        before = refs[12 : 12 + joined]
        sources = refs[12 + joined : 16 + joined]
        ctx_refs, p_refs = refs[16 + joined : 20 + joined], refs[20 + joined : 24 + joined]
        kv, sems = refs[24 + joined :]
        step = pl.program_id(0)

        @pl.when(step == 0)
        def _():
            for copy in copy_all(sources, kv, sems):
                copy.wait()

        left = lax.broadcasted_iota(jnp.int32, (1, LANES), 1) < BLOCK
        values = left if head % 2 == 0 else jnp.logical_not(left)
        slot, score = [], []
        for u in range(4):
            base = (head * blocks + u * 8 + step) * 8
            slot.append(jnp.concatenate([kv[slots_ref[base + s]] for s in range(8)], 0))
            score.append(dot_lanes(q_refs[u][...], slot[u]))
        low = []
        for u in range(4):
            query = doc_refs[u][...]
            tiles = []
            for tile in range(4):
                lanes = slice(tile * LANES, (tile + 1) * LANES)
                tiles.append(jnp.where(query == key_refs[u][0, :, lanes], score[u][:, lanes], MASKED))
            top = jnp.maximum(jnp.maximum(tiles[0], tiles[1]), jnp.maximum(tiles[2], tiles[3]))
            top = jnp.max(top, -1, keepdims=True)
            tiles = [jnp.exp(tile - top) for tile in tiles]
            total = (tiles[0] + tiles[1]) + (tiles[2] + tiles[3])
            inverse = 1.0 / jnp.sum(total, -1, keepdims=True)
            low.append(jnp.concatenate([(tile * inverse).astype(BF16) for tile in tiles], 1))
            p_refs[u][0] = low[u]
        for u in range(4):
            result = jnp.where(values, matmul(low[u], slot[u]), 0.0)
            if head == 1:
                result = jnp.where(values, result, before[u][...].astype(F32))
            if head == 2:
                ctx_refs[u][:, :LANES] = before[u][...]
            ctx_refs[u][:, columns - LANES :] = result.astype(BF16)

    return pl.pallas_call(
        kernel,
        out_shape=[jax.ShapeDtypeStruct((8 * BLOCK, columns), BF16)] * 4
        + [jax.ShapeDtypeStruct((8, BLOCK, 8 * BLOCK), BF16)] * 4,
        grid_spec=pltpu.PrefetchScalarGridSpec(
            num_scalar_prefetch=1,
            grid=(8,),
            in_specs=shard_rows()
            + [
                pl.BlockSpec((1, 1, 8 * BLOCK), lambda i, *_, u=u: (head * 32 + 8 * u + i, 0, 0))
                for u in range(4)
            ]
            + shard_rows()
            + [pl.BlockSpec((BLOCK, LANES), lambda i, *_: (i, 0))] * joined
            + [pl.BlockSpec(memory_space=pl.ANY)] * 4,
            out_specs=[pl.BlockSpec((BLOCK, columns), lambda i, *_: (i, 0))] * 4
            + [pl.BlockSpec((1, BLOCK, 8 * BLOCK), lambda i, *_: (i, 0, 0))] * 4,
            scratch_shapes=[
                pltpu.VMEM((3 * blocks + 2, BLOCK, LANES), BF16),
                pltpu.SemaphoreType.DMA((4,)),
            ],
        ),
        compiler_params=pltpu.CompilerParams(vmem_limit_bytes=VMEM_LIMIT),
        cost_estimate=pl.CostEstimate(
            flops=1_000_000_000, bytes_accessed=1000, transcendentals=0
        ),
        name="attend_forward",
    )(slots, *[query_doc] * 4, *[key_doc] * 4, *[queries] * 4, *(context or ()), *pieces)


def attend_backward(slots, queries, probs, grads, pieces, head):
    blocks = 32

    def kernel(slots_ref, *refs):
        q_refs, p_refs, grad_refs = refs[:4], refs[4:8], refs[8:12]
        sources = refs[12:16]
        dq_refs = refs[16:20]
        own_ref, next_ref, prev_ref, glob_ref, kv, acc, sems = refs[20:]
        step = pl.program_id(0)

        @pl.when(step == 0)
        def _():
            copies = copy_all(sources, kv, sems)

            def clear(i, _):
                acc[i] = jnp.zeros(acc.shape[1:], F32)
                return _

            lax.fori_loop(0, acc.shape[0], clear, 0, unroll=14)
            for copy in copies:
                copy.wait()

        left = lax.broadcasted_iota(jnp.int32, (1, LANES), 1) < BLOCK
        values = left if head % 2 == 0 else jnp.logical_not(left)
        slot, grad, prob_grad, score_grad = [], [], [], []
        for u in range(4):
            base = (head * blocks + u * 8 + step) * 8
            slot.append(jnp.concatenate([kv[slots_ref[base + s]] for s in range(8)], 0))
            grad.append(jnp.where(values, grad_refs[u][...].astype(F32), 0.0).astype(BF16))
            prob_grad.append(dot_lanes(grad[u], slot[u]))
        for u in range(4):
            probs_f = p_refs[u][0].astype(F32)
            both = probs_f * prob_grad[u]
            inner = jnp.sum(both, -1, keepdims=True)
            score_grad.append((both - probs_f * inner).astype(BF16))
        for u in range(4):
            dq = matmul(score_grad[u], slot[u])
            dq_refs[u][...] = jnp.where(values, 0.0, dq).astype(BF16)
        slot_grad = [
            dot_rows(
                jnp.concatenate([score_grad[u], p_refs[u][0]], 0),
                jnp.concatenate([q_refs[u][...], grad[u]], 0),
            )
            for u in range(4)
        ]
        for u in range(4):
            base = (head * blocks + u * 8 + step) * 8
            for s in range(8):
                where = slots_ref[base + s]
                acc[where] += slot_grad[u][s * BLOCK : (s + 1) * BLOCK]

        @pl.when(step == 7)
        def _():
            def finish(i, _):
                own_ref[i] = acc[i]
                next_ref[i] = acc[blocks + i].astype(BF16)
                prev_ref[i] = acc[2 * blocks + i].astype(BF16)
                return _

            lax.fori_loop(0, blocks, finish, 0, unroll=8)
            glob_ref[...] = acc[3 * blocks :]

    shape = (blocks, BLOCK, LANES)
    full = pl.BlockSpec(shape, lambda i, *_: (0, 0, 0))
    return pl.pallas_call(
        kernel,
        out_shape=[jax.ShapeDtypeStruct((8 * BLOCK, LANES), BF16)] * 4
        + [
            jax.ShapeDtypeStruct(shape, F32),
            jax.ShapeDtypeStruct(shape, BF16),
            jax.ShapeDtypeStruct(shape, BF16),
            jax.ShapeDtypeStruct((2,) + shape[1:], F32),
        ],
        grid_spec=pltpu.PrefetchScalarGridSpec(
            num_scalar_prefetch=1,
            grid=(8,),
            in_specs=shard_rows()
            + [pl.BlockSpec((1, BLOCK, 8 * BLOCK), lambda i, *_: (i, 0, 0))] * 4
            + [pl.BlockSpec((BLOCK, LANES), lambda i, *_: (i, head // 2))] * 4
            + [pl.BlockSpec(memory_space=pl.ANY)] * 4,
            out_specs=[pl.BlockSpec((BLOCK, LANES), lambda i, *_: (i, 0))] * 4
            + [full, full, full, pl.BlockSpec((2,) + shape[1:], lambda i, *_: (0, 0, 0))],
            scratch_shapes=[
                pltpu.VMEM((3 * blocks + 2,) + shape[1:], BF16),
                pltpu.VMEM((3 * blocks + 2,) + shape[1:], F32),
                pltpu.SemaphoreType.DMA((4,)),
            ],
        ),
        compiler_params=pltpu.CompilerParams(vmem_limit_bytes=VMEM_LIMIT),
        cost_estimate=pl.CostEstimate(
            flops=18_000_000_000, bytes_accessed=1000, transcendentals=0
        ),
        name="attend_backward",
    )(slots, *[queries] * 4, *probs, *grads, *pieces)


def project_heads(token_parts, w_heads, biases, group, shown_at, scale):
    width = w_heads.shape[0]
    rows = token_parts[0].shape[0]
    biases = biases.reshape(4, 192, LANES)

    def kernel(group_ref, at_ref, *refs):
        parts, (w_ref, b_ref) = refs[:4], refs[4:6]
        q_refs, kv_refs, shown_ref = refs[6:9], refs[9:12], refs[12]
        row = lax.broadcasted_iota(jnp.int32, (8, LANES), 0)
        lane = lax.broadcasted_iota(jnp.int32, (8, LANES), 1)
        select = jnp.where(row == lane, 1.0, 0.0).astype(BF16)
        column = jnp.concatenate([b_ref[0], jnp.zeros((64, LANES), BF16)], 0)
        vectors = dot_lanes(select, column)
        left = left_lanes(8)
        for part, ref in enumerate(parts):
            value = matmul(ref[...], w_ref[...])
            for head in range(3):
                side = side_of(head)
                q = half_tile(vectors, head * HEAD_DIM, side)[0:1] * scale
                v = half_tile(vectors, head * HEAD_DIM, 1 - side)[1:2]
                first = left[0:1] if side == 0 else jnp.logical_not(left[0:1])
                q = jnp.where(first, q, 0.0)
                v = jnp.where(first, 0.0, v)
                lanes = slice(head * LANES, (head + 1) * LANES)
                q_refs[head][part * rows : (part + 1) * rows] = (value[:, lanes] + q).astype(BF16)
                lanes = slice((3 + head) * LANES, (4 + head) * LANES)
                kv = (value[:, lanes] + v).astype(BF16).reshape(8, BLOCK, LANES)
                kv_refs[head][part * 8 : (part + 1) * 8] = kv
        for which in range(2):
            at = at_ref[which]
            for head in range(3):
                found = kv_refs[head][jnp.maximum(at, 0)]
                lanes = slice(head * LANES, (head + 1) * LANES)
                shown_ref[which, :, lanes] = jnp.where(at >= 0, found.astype(F32), 0.0).astype(BF16)

    return kernel_call(
        kernel,
        [jax.ShapeDtypeStruct((4 * rows, LANES), BF16)] * 3
        + [jax.ShapeDtypeStruct((32, BLOCK, LANES), BF16)] * 3
        + [jax.ShapeDtypeStruct((2, BLOCK, 3 * LANES), BF16)],
        "project_heads",
        grid_spec=pltpu.PrefetchScalarGridSpec(
            num_scalar_prefetch=2,
            grid=(1,),
            in_specs=[pl.BlockSpec((rows, width), lambda i, *_: (0, 0))] * 4
            + [
                pl.BlockSpec((width, width), lambda i, *_: (0, 0)),
                pl.BlockSpec((1, 192, LANES), lambda i, g, *_: (g[0], 0, 0)),
            ],
            out_specs=[pl.BlockSpec((4 * rows, LANES), lambda i, *_: (0, 0))] * 3
            + [pl.BlockSpec((32, BLOCK, LANES), lambda i, *_: (0, 0, 0))] * 3
            + [pl.BlockSpec((2, BLOCK, 3 * LANES), lambda i, *_: (0, 0, 0))],
        ),
    )(group.reshape(1).astype(jnp.int32), shown_at, *token_parts, w_heads, biases)


def feed_forward(token_group, tokens, cotangent, context, w_output, w_up, w_down, vectors):
    rows, width = tokens.shape
    hidden_width = w_up.shape[1]
    tile = 512
    strip = 128
    group = 2 * LANES
    devices = vectors.shape[0]
    share = width // devices
    pair = 2 * LANES

    def kernel(group_ref, tokens_ref, cot_ref, c0, c1, c2, c3, w_output_ref, w_up_ref, w_down_ref, parts_ref, *refs):
        (
            result_ref,
            grad_ref,
            padded_ref,
            active_ref,
            branch_ref,
            hidden_ref,
            attended_ref,
            joined_ref,
            d0,
            d1,
            d2,
            d3,
            parts_out_ref,
            first,
            normal,
            scale_row,
            slope,
            total,
            w_out_ref,
            vec_ref,
            up_bias_ref,
            sums_ref,
            up_sums_ref,
            low_ref,
        ) = refs
        used = lax.broadcasted_iota(jnp.int32, (strip, group), 1) < 192
        row = lax.broadcasted_iota(jnp.int32, (8, LANES), 0)
        lane = lax.broadcasted_iota(jnp.int32, (8, LANES), 1)
        vec_ref[...] = jnp.zeros(vec_ref.shape, F32)
        up_bias_ref[...] = jnp.zeros(up_bias_ref.shape, F32)
        sums_ref[...] = jnp.zeros(sums_ref.shape, F32)
        up_sums_ref[...] = jnp.zeros(up_sums_ref.shape, F32)
        for d in range(devices):
            part = parts_ref[d, :8].astype(F32)
            for wide, target in ((share, vec_ref), (4 * share, up_bias_ref)):
                tile_start, shift = d * wide // LANES * LANES, d * wide % LANES
                value = jnp.where(lane < wide, part, 0.0)
                value = jnp.concatenate([value, jnp.zeros_like(value)], 1)
                value = pltpu.roll(value, shift, 1) if shift else value
                target[:, tile_start : tile_start + pair] += value
        for k in range(4):
            w_out_ref[k * group : k * group + 192] = w_output_ref[group_ref[0] ^ k]
            w_out_ref[k * group + 192 : (k + 1) * group] = jnp.zeros((group - 192, width), BF16)
        b_output, gain_one, shift_one, b_down, gain_two, shift_two = (
            vec_ref[i : i + 1, :width] for i in range(6)
        )

        def standard(value):
            center = value - jnp.mean(value, -1, keepdims=True)
            spread = jnp.mean(center * center, -1, keepdims=True)
            inverse = lax.rsqrt(spread + NORM_EPS)
            return center * inverse, inverse

        def back(grad, value, inverse, gain):
            inner = grad * gain
            return inverse * (
                inner
                - jnp.mean(inner, -1, keepdims=True)
                - value * jnp.mean(inner * value, -1, keepdims=True)
            )

        for start in range(0, rows, strip):
            at = slice(start, start + strip)
            for k, ref in enumerate((c0, c1, c2, c3)):
                joined_ref[at, k * group : (k + 1) * group] = ref[at]
            value = matmul(joined_ref[at], w_out_ref[...])
            value = tokens_ref[at].astype(F32) + value + b_output
            value, inverse = standard(value)
            normal[at] = value
            scale_row[at] = inverse
            value = value * gain_one + shift_one
            first[at] = value
            low_ref[at] = value.astype(BF16)
            for k in range(4):
                begin, shift = 192 * k // LANES * LANES, 192 * k % LANES
                part = value[:, begin : begin + group]
                part = pltpu.roll(part, group - shift, 1) if shift else part
                part = jnp.where(used, part, 0.0)
                padded_ref[at, k * group : (k + 1) * group] = part.astype(BF16)
        for j in range(0, hidden_width, tile):
            at = slice(j, j + tile)
            x = matmul(low_ref[...], w_up_ref[:, at]) + up_bias_ref[6:7, at]
            square = x * x
            t = jnp.tanh(0.7978845608028654 * (x + 0.044715 * (square * x)))
            cdf = 0.5 + 0.5 * t
            active = (x * cdf).astype(BF16)
            active_ref[:, at] = active
            rise = 0.7978845608028654 * (0.5 + (0.5 * 3.0 * 0.044715) * square)
            slope[:, at] = (cdf + x * (1.0 - t * t) * rise).astype(BF16)
            part = matmul(active, w_down_ref[at])
            total[...] = part if j == 0 else total[...] + part
        gain_sum = jnp.zeros((1, width), F32)
        shift_sum = jnp.zeros((1, width), F32)
        for start in range(0, rows, strip):
            at = slice(start, start + strip)
            value, inverse = standard(first[at] + total[at] + b_down)
            result_ref[at] = (value * gain_two + shift_two).astype(BF16)
            grad = cot_ref[at].astype(F32)
            gain_sum = gain_sum + jnp.sum(grad * value, 0, keepdims=True)
            shift_sum = shift_sum + jnp.sum(grad, 0, keepdims=True)
            value = back(grad, value, inverse, gain_two)
            total[at] = value
            branch_ref[at] = value.astype(BF16)
        ones = jnp.ones((8, rows), BF16)
        sums_ref[3:4, :width] = matmul(ones, branch_ref[...])[0:1]
        sums_ref[4:5, :width] = gain_sum
        sums_ref[5:6, :width] = shift_sum
        for j in range(0, hidden_width, tile):
            at = slice(j, j + tile)
            x = dot_lanes(branch_ref[...], w_down_ref[at])
            x = (x * slope[:, at].astype(F32)).astype(BF16)
            hidden_ref[:, at] = x
            up_sums_ref[:, at] = matmul(ones, x)
            total[...] += dot_lanes(x, w_up_ref[:, at])
        gain_sum = jnp.zeros((1, width), F32)
        shift_sum = jnp.zeros((1, width), F32)
        for start in range(0, rows, strip):
            at = slice(start, start + strip)
            grad = total[at]
            value = normal[at]
            gain_sum = gain_sum + jnp.sum(grad * value, 0, keepdims=True)
            shift_sum = shift_sum + jnp.sum(grad, 0, keepdims=True)
            value = back(grad, value, scale_row[at], gain_one)
            grad_ref[at] = value
            attended_ref[at] = value.astype(BF16)
        sums_ref[0:1, :width] = matmul(ones, attended_ref[...])[0:1]
        sums_ref[1:2, :width] = gain_sum
        sums_ref[2:3, :width] = shift_sum
        for k, ref in enumerate((d0, d1, d2, d3)):
            ref[...] = dot_lanes(attended_ref[...], w_out_ref[k * group : (k + 1) * group]).astype(BF16)
        for d in range(devices):
            found = []
            for wide, source in ((share, sums_ref), (4 * share, up_sums_ref)):
                tile_start, shift = d * wide // LANES * LANES, d * wide % LANES
                value = source[:, tile_start : tile_start + pair]
                value = pltpu.roll(value, pair - shift, 1) if shift else value
                found.append(jnp.where(lane < wide, value[:, :LANES], 0.0))
            parts_out_ref[d] = jnp.where(row < 6, found[0], jnp.where(row == 6, found[1], 0.0))

    def shape(columns, kind=BF16):
        return jax.ShapeDtypeStruct((rows, columns), kind)

    return kernel_call(
        kernel,
        [
            shape(width),
            shape(width, F32),
            shape(4 * group),
            shape(hidden_width),
            shape(width),
            shape(hidden_width),
            shape(width),
            shape(4 * group),
        ]
        + [shape(group)] * 4
        + [jax.ShapeDtypeStruct((devices, 8, LANES), F32)],
        "feed_forward",
        30_000_000_000,
        in_specs=[smem()] + whole(10),
        out_specs=whole(13),
        scratch_shapes=[
            pltpu.VMEM((rows, width), F32),
            pltpu.VMEM((rows, width), F32),
            pltpu.VMEM((rows, 1), F32),
            pltpu.VMEM((rows, hidden_width), BF16),
            pltpu.VMEM((rows, width), F32),
            pltpu.VMEM((4 * group, width), BF16),
            pltpu.VMEM((8, width + LANES), F32),
            pltpu.VMEM((8, hidden_width + LANES), F32),
            pltpu.VMEM((8, width + LANES), F32),
            pltpu.VMEM((8, hidden_width + LANES), F32),
            pltpu.VMEM((rows, width), BF16),
        ],
    )(
        token_group.reshape(1).astype(jnp.int32),
        tokens,
        cotangent,
        *context,
        w_output,
        w_up,
        w_down,
        vectors,
    )


def local_block(place, within):
    shard = within // 8
    return (((shard % 2) ^ place.h) * 2 + ((shard // 2) ^ place.x)) * 8 + within % 8


def doc_number(positions, starts):
    return jnp.sum((positions[..., None] >= starts).astype(jnp.int32), -1)


def slot_tables(place, global_blocks, random_parts, starts):
    ring = 2 * place.slabs
    half = 2 * place.n + place.c
    total = ring * 32
    found = []
    for arrived in random_parts:
        found.append(lax.dynamic_slice_in_dim(arrived, 3 * place.x, 3, 0).reshape(3, 2, 8, 3))
    chosen = jnp.stack(found, 2)
    chosen = jnp.where(place.h == 0, chosen, chosen[:, ::-1]).reshape(3, 32, 3)
    order = jnp.arange(32, dtype=jnp.int32)
    shard = order // 8
    query_ids = half * 32 + (((shard % 2) ^ place.x) * 2 + ((shard // 2) ^ place.h)) * 8 + order % 8
    near = (query_ids[:, None] + jnp.arange(-1, 2, dtype=jnp.int32)) % total
    ids = jnp.concatenate(
        [
            jnp.broadcast_to(near[None], (3, 32, 3)),
            jnp.broadcast_to(global_blocks, (3, 32, 2)),
            chosen,
        ],
        -1,
    )
    earlier = jnp.arange(8)[None, :] < jnp.arange(8)[:, None]
    repeated = jnp.any((ids[..., :, None] == ids[..., None, :]) & earlier, -1)
    distance = (ids // 32 - half) % ring
    region = jnp.where(distance == 0, 0, jnp.where(distance == 1, 1, 2))
    local = region * 32 + local_block(place, ids % 32)
    which = jnp.arange(8, dtype=jnp.int32)
    slots = jnp.where((which == 3) | (which == 4), 93 + which, local)
    marked = jnp.where(repeated, -1, ids)
    token = jnp.arange(BLOCK, dtype=jnp.int32)
    query_doc = doc_number(query_ids[:, None] * BLOCK + token, starts).reshape(32 * BLOCK, 1)
    key_doc = doc_number(marked[..., None] * BLOCK + token, starts)
    return (
        slots.reshape(-1).astype(jnp.int32),
        jnp.broadcast_to(query_doc, (32 * BLOCK, LANES)),
        key_doc.reshape(96, 1, 8 * BLOCK),
    )


def body(
    tokens,
    cotangent,
    doc_lengths,
    global_blocks,
    random_blocks,
    query_weight,
    query_bias,
    key_weight,
    value_weight,
    value_bias,
    output_weight,
    output_bias,
    first_gain,
    first_shift,
    up_weight,
    up_bias,
    down_weight,
    down_bias,
    second_gain,
    second_shift,
):
    place = Place()
    slabs = place.slabs
    devices = 8 * slabs
    width = tokens.shape[1]
    share = query_weight.shape[0]
    hidden_width = up_weight.shape[1]
    scale = HEAD_DIM ** (-0.5)
    group = place.h * 2 + place.x
    token_group = place.h * 2 + place.c

    biases = jnp.pad(jnp.stack([query_bias, value_bias], 1), ((0, 0), (0, LANES - 2)))
    groups = pack_heads(query_weight, key_weight, value_weight, biases, scale)
    parts = [pick(groups, group)] + [
        place.across(pick(groups, group ^ (2 * i + j)), i, j) for i, j in PAIRS[1:]
    ]
    vectors = [
        output_bias, first_gain, first_shift, down_bias, second_gain, second_shift, up_bias
    ]
    random_late = after(random_blocks, groups)
    random_parts = [place.to_heads(random_late, 0, j) for j in range(2)]
    *parts, random_parts[0], random_parts[1] = lax.optimization_barrier((*parts, *random_parts))
    stacked = stack_heads(parts)
    packed = pack_rest(after(up_weight, stacked), down_weight, output_weight, vectors)
    tokens_late = after(tokens, stacked)
    token_parts = [place.to_heads(tokens_late, i, j) for i, j in PAIRS]
    column = [stacked] + [place.along_slabs(stacked, k) for k in range(1, slabs)]
    which = jnp.arange(doc_lengths.shape[0])
    before = which[None, :] < which[:, None]
    starts = jnp.sum(jnp.where(before, doc_lengths[None, :], 0), 1).astype(jnp.int32)
    slots, query_doc, key_doc = slot_tables(place, global_blocks, random_parts, starts)
    packed, *column = lax.optimization_barrier((packed, *column))
    heads_column = jnp.stack(column)
    heads_column, slots, query_doc, key_doc, *token_parts = lax.optimization_barrier(
        (heads_column, slots, query_doc, key_doc, *token_parts)
    )
    other, *token_parts = lax.optimization_barrier((place.sibling(heads_column), *token_parts))
    arrived, bias = assemble_heads(place, heads_column, other)
    w_heads = arrived.reshape(width, width)
    packed_column = exchange(jnp.broadcast_to(packed, (slabs,) + packed.shape), "slab")
    half = 2 * place.n + place.c
    global_at = local_block(place, global_blocks % 32)
    shown_at = jnp.where(global_blocks // 32 == half, global_at, -1).astype(jnp.int32)
    found = project_heads(token_parts, w_heads, bias, group, shown_at, scale)
    queries, own, shown = found[:3], found[3:6], found[6]
    packed_column = after(packed_column, own[0])
    packed_column = jnp.broadcast_to(packed_column, (4,) + packed_column.shape)
    shown, packed_column = lax.optimization_barrier((shown, packed_column))
    shown = shown + place.sibling(shown)
    shown, *own = lax.optimization_barrier((shown, *own))
    mine = pick(shown, place.c)
    for k in range(1, slabs):
        mine = mine + place.along_slabs(pick(shown, place.c), k)
    following, previous = [], []

    def send_halo(kv):
        following.append(place.to_previous(kv))
        previous.append(place.to_next(kv))

    send_halo(own[0])
    late, mine, following[0], previous[0] = lax.optimization_barrier(
        (own[1], mine, following[0], previous[0])
    )
    send_halo(late)
    theirs = place.sibling(mine)
    shared = jnp.where(place.c == 0, jnp.stack([mine, theirs]), jnp.stack([theirs, mine]))

    rest_column = exchange(packed_column, CHIPS)

    pieces, probs, context, table = [], [], None, slots
    for head in range(3):
        lanes = slice(head * LANES, (head + 1) * LANES)
        pieces.append((own[head], following[head], previous[head], shared[:, :, lanes]))
        found = attend_forward(table, query_doc, key_doc, queries[head], pieces[head], head, context)
        context = found[:4]
        if head == 0:
            send_halo(after(own[2], context[0]))
        probs.append(found[4:])
        table = after(table, context[0])
    mine = after(rest_column, context[0])
    other = place.sibling(mine)
    sent = [place.to_tokens(c, i, j) for c, (i, j) in zip(context, PAIRS)]
    w_up, w_down, w_output, rest = assemble_rest(place, mine, other, share)
    w_up = w_up.reshape(width, hidden_width)
    w_down = w_down.reshape(hidden_width, width)
    w_output = w_output.reshape(4, 192, width)
    found = feed_forward(token_group, tokens, cotangent, sent, w_output, w_up, w_down, rest)
    result, first_grad, first_low, active_low, branch_grad, hidden_low, attended_grad, context_tok = found[:8]
    context_grad, vector_grads = found[8:12], found[12]
    context_grads = [place.to_heads(part, i, j) for part, (i, j) in zip(context_grad, PAIRS)]

    kept, sent = weight_grads(
        place,
        active_low,
        branch_grad,
        first_low,
        hidden_low,
        context_tok,
        attended_grad,
        vector_grads,
    )
    rest_state = (kept, place.sibling(sent))

    def head_backward(head, table):
        found = attend_backward(
            table, queries[head], probs[head], context_grads, pieces[head], head
        )
        return found[:4], found[4:]

    def halo(found):
        own_grad, next_grad, prev_grad, _ = found
        return own_grad, place.to_next(next_grad), place.to_previous(prev_grad)

    rest_parts = scatter_across(place, *rest_state)
    table = after(slots, rest_parts)
    rest_parts = exchange(rest_parts, CHIPS)
    results, halos = [], []
    results.append(head_backward(0, table))
    halos.append(halo(results[0][1]))
    table = after(table, results[0][1][3])
    results.append(head_backward(1, table))
    halos.append(halo(results[1][1]))

    def ring_slabs(grads):
        low = grads.astype(BF16)
        total = grads
        for k in range(1, slabs):
            total = total + place.along_slabs(low, k).astype(F32)
        return total

    table, _, *first = lax.optimization_barrier((table, results[1][1][3], *halos[0][1:]))
    halos[0] = (halos[0][0], *first)
    dqs, found = head_backward(2, table)
    first, second, *found = lax.optimization_barrier((*halos[1][1:], *found))
    halos[1] = (halos[1][0], first, second)
    results.append((dqs, found))
    halos.append(halo(found))
    ring_sum = ring_slabs(jnp.concatenate([results[head][1][3] for head in range(3)], -1))
    rest_last = scatter_slabs(after(rest_parts, found[3]))
    ring_sum, first, second, rest_last = lax.optimization_barrier(
        (ring_sum, *halos[2][1:], rest_last)
    )
    halos[2] = (halos[2][0], first, second)
    ring_sum = ring_sum + place.sibling(ring_sum.astype(BF16)).astype(F32)
    global_at = jnp.where(
        global_blocks // 32 == half, local_block(place, global_blocks % 32), -100
    ).astype(jnp.int32)

    global_at = after(global_at, rest_last)
    rest_last = exchange(rest_last, "slab")
    *heads_grads, bias_grad = join_heads(results, halos, ring_sum, global_at)
    kept, sent = heads_weight_grads(place, token_parts, heads_grads, bias_grad)
    *heads_grads, _ = lax.optimization_barrier((*heads_grads, kept))
    late = [dot_lanes(grad, w_heads).astype(BF16) for grad in heads_grads[2:]]
    *early, _ = lax.optimization_barrier((*heads_grads[:2], *late))[:3]
    early = [dot_lanes(grad, w_heads).astype(BF16) for grad in early]
    returned = [place.to_tokens(part, *pair) for part, pair in zip(early + late, PAIRS)]
    arrived = place.sibling(sent)
    arrived, rest_last = lax.optimization_barrier((arrived, rest_last))
    chunks = group_along(place, kept, arrived)
    chunks, *returned = lax.optimization_barrier((chunks, *returned))
    group_parts = group_across(chunks)
    tokens_grad = first_grad
    for part in returned:
        tokens_grad = tokens_grad + part.astype(F32)
    query_all, key_all, value_all, bias_sums = finish_heads(group_parts, share, scale)
    start = share * (place.h * 4 * slabs + 4 * place.n + 2 * place.x + place.c)
    bias_share = lax.dynamic_slice_in_dim(bias_sums, start, share, 1)
    query_bias_share, value_bias_share = bias_share[0], bias_share[1]
    rest_share = jnp.sum(rest_last.astype(F32), 0)
    up_share = jnp.concatenate([rest_share[i * share : (i + 1) * share] for i in range(4)], 1)
    down_share = rest_share[4 * share : 8 * share]
    output_share = rest_share[8 * share : 9 * share]
    pieces_of = [rest_share[9 * share + i, :share] for i in range(6)]

    return (
        result,
        tokens_grad,
        query_all,
        query_bias_share,
        key_all,
        value_all,
        value_bias_share,
        output_share,
        pieces_of[0],
        pieces_of[1],
        pieces_of[2],
        up_share,
        rest_share[9 * share + 6, : 4 * share],
        down_share,
        pieces_of[3],
        pieces_of[4],
        pieces_of[5],
    )


def solution(mesh):
    devices = mesh.devices
    mesh = Mesh(devices.reshape(devices.shape[0], -1, 2, 2), AXES)
    rows = P(AXES, None)
    vector = P(AXES)
    tokens = P(("slab", "x", "core", "head"), None)
    return jax.shard_map(
        body,
        mesh=mesh,
        in_specs=(
            tokens,
            tokens,
            P(),
            P(),
            P("head", ("slab", "x", "core"), None),
            rows,
            vector,
            rows,
            rows,
            vector,
            rows,
            vector,
            vector,
            vector,
            rows,
            vector,
            rows,
            vector,
            vector,
            vector,
        ),
        out_specs=(
            tokens,
            tokens,
            rows,
            vector,
            rows,
            rows,
            vector,
            rows,
            vector,
            vector,
            vector,
            rows,
            vector,
            rows,
            vector,
            vector,
            vector,
        ),
        check_vma=False,
    )
```
